128 devices in a mesh: slab: 16 (over x, y_hi, core), cross: 8 (over y_lo, z).
Axes of the slice: x: 4, y: 4 (y_hi: 2, y_lo: 2; y = y_hi * 2 + y_lo), z: 4, core: 2. Of those that a mesh axis runs over, the one named last changes fastest.
Arguments:
- right_side: float32 [6, 6, 6, 16, 64, 128], P(None, None, None, 'slab', 'cross'), may hold values from -6 to 6
- coefficient: float32 [16, 64, 128], P('slab', 'cross'), may hold values from 0.3 to 3
- bottom_top: int32 [2, 16, 64], P(None, 'slab', 'cross'), may hold values 0 or 1
- stiff_five: float32 [216, 216], replicated, may hold values from -1 to 2
- stiff_three: float32 [64, 64], replicated, may hold values from -1 to 2
- stiff_one: float32 [8, 8], replicated, may hold values from -1 to 2
Outputs:
- solution: float32 [6, 6, 6, 16, 64, 128], P(None, None, None, 'slab', 'cross')
- residual: float32 [6, 6, 6, 16, 64, 128], P(None, None, None, 'slab', 'cross')
The draws below stay inside these ranges and needn't reach their ends.
Inputs may be any that keep to these rules, and one draw needn't show every extreme that they name: `bottom_top`: 1 marks a face held at zero, 0 a face with no flux.
All inputs are finite; a program needn't handle non-finite values. No bound on the sum of `bottom_top` on one device may be relied on, other than what follows from the above.
Results may differ from the reference program's by a relative error of at most 0.00017.
Values sent between devices are 32-bit elements; how exact they have to be, the bound alone decides.
A program may use at most 128 MiB of HBM per device.

```python
import math
import jax
import jax.numpy as jnp
import numpy as np
from jax import lax

Q5 = 6
Q3 = 4
Q1 = 2
DEGREE = 3
COARSE_ITERS = 8
NXE = 16
NYE = 64
NZE = 128


def stiffness_matrix(key, order, spread):
    upper_key, middle_key = jax.random.split(key)
    random_part = jax.random.uniform(upper_key, (order, order), jnp.float32, -1.0, 1.0)
    coupling = 0.5 * (random_part + random_part.T) / (order - 1)
    diagonal = 1.0 + spread * jax.random.uniform(middle_key, (order,), jnp.float32)
    identity = jnp.eye(order, dtype=jnp.float32)
    return coupling * (1.0 - identity) + identity * diagonal[:, None]


def draw_stiff_five(key, part):
    key = jax.random.fold_in(key, 11)
    spread = 0.5
    return stiffness_matrix(key, Q5 * Q5 * Q5, spread)


def draw_stiff_three(key, part):
    key = jax.random.fold_in(key, 13)
    spread = 0.5
    return stiffness_matrix(key, Q3 * Q3 * Q3, spread)


def draw_stiff_one(key, part):
    key = jax.random.fold_in(key, 17)
    spread = 0.5
    return stiffness_matrix(key, Q1 * Q1 * Q1, spread)


def plant(entries, own_key, least, largest):
    longest = entries.shape.index(max(entries.shape))
    spots = []
    for shift in (0, 1):
        where = [jax.random.randint(jax.random.fold_in(own_key, axis), (), 0, length) for axis, length in enumerate(entries.shape)]
        where[longest] = (where[longest] + shift) % entries.shape[longest]
        spots.append(tuple(where))
    return entries.at[spots[0]].set(least).at[spots[1]].set(largest)


def level_of(own_key, extent, cuts, low, high):
    def one(axis_at, shards_of):
        steps = jax.random.uniform(jax.random.fold_in(jax.random.fold_in(own_key, 6), axis_at), (shards_of,), jnp.float32, low / len(cuts), high / len(cuts))
        return jnp.repeat(jnp.exp(steps), extent[axis_at] // shards_of).reshape((-1,) + (1,) * (len(extent) - axis_at - 1))

    gain = one(*cuts[0])
    for cut in cuts[1:]:
        gain = gain * one(*cut)
    return gain


def normal_values(stream_key, extent, scale, limit, pieces=(), held_as=jnp.bfloat16):
    entries = scale * jax.random.normal(stream_key, extent, jnp.float32)
    if pieces:
        entries = entries * level_of(stream_key, extent, pieces, -0.22, 0.18)
    return jnp.clip(entries, -limit, limit).astype(held_as)


def setup_inputs(seed: int = 0) -> dict:
    key_of = jax.random.split(jax.random.key(seed), 7)
    right_side = normal_values(key_of[0], (Q5, Q5, Q5, NXE, NYE, NZE), 1.0, 6.0, ((3, 16), (4, 8)), jnp.float32)
    coefficient = jnp.clip(jnp.exp(math.log(3.0) - 2.3025851 * jax.random.uniform(key_of[1], (NXE, NYE, NZE), jnp.float32) ** level_of(key_of[1], (NXE, NYE, NZE), ((0, 16), (1, 8)), -0.2, 0.2)), 0.3, 3.0)
    bottom_top = plant((jax.random.randint(key_of[2], (2, NXE, NYE), 0, 2) < 1).astype(jnp.int32), jax.random.fold_in(key_of[2], 1), 0, 1)
    stiff_five = draw_stiff_five(jax.random.fold_in(key_of[6], 71), 0)
    stiff_three = draw_stiff_three(jax.random.fold_in(key_of[6], 71), 0)
    stiff_one = draw_stiff_one(jax.random.fold_in(key_of[6], 71), 0)
    return {"right_side": right_side, "coefficient": coefficient, "bottom_top": bottom_top, "stiff_five": stiff_five, "stiff_three": stiff_three, "stiff_one": stiff_one}


PRECISE = lax.Precision.HIGHEST
LAMBDA_TOP = 2.2


def cube_side(total_count):
    edge_count = 1
    while edge_count * edge_count * edge_count < total_count:
        edge_count = edge_count + 1
    return edge_count


def lagrange_table(fine_count, coarse_count):
    fine_points = np.linspace(-1.0, 1.0, fine_count)
    coarse_points = np.linspace(-1.0, 1.0, coarse_count)
    interp_table = np.ones((fine_count, coarse_count))
    for column in range(coarse_count):
        for other_node in range(coarse_count):
            if other_node != column:
                interp_table[:, column] = interp_table[:, column] * (fine_points - coarse_points[other_node]) / (coarse_points[column] - coarse_points[other_node])
    return jnp.asarray(interp_table, dtype=jnp.float32)


def prolong(nodal_field, interp_table):
    nodal_field = jnp.einsum("ai,ijkxyz->ajkxyz", interp_table, nodal_field, precision=PRECISE)
    nodal_field = jnp.einsum("bj,ajkxyz->abkxyz", interp_table, nodal_field, precision=PRECISE)
    return jnp.einsum("ck,abkxyz->abcxyz", interp_table, nodal_field, precision=PRECISE)


def restrict(nodal_field, interp_table):
    return prolong(nodal_field, interp_table.T)


def face_index(face_axis, node_index):
    return (slice(None),) * face_axis + (node_index,)


def face_weights(padded, end_flags):
    middle = padded[1:-1, 1:-1]
    weight_x = (0.5 * (middle + padded[:-2, 1:-1]), 0.5 * (middle + padded[2:, 1:-1]))
    weight_y = (0.5 * (middle + padded[1:-1, :-2]), 0.5 * (middle + padded[1:-1, 2:]))
    face_marks = end_flags.astype(jnp.float32)
    below_weight = jnp.concatenate([face_marks[0][..., None] * middle[..., :1], 0.5 * (middle[..., 1:] + middle[..., :-1])], 2)
    above_weight = jnp.concatenate([0.5 * (middle[..., :-1] + middle[..., 1:]), face_marks[1][..., None] * middle[..., -1:]], 2)
    return middle, (weight_x, weight_y, (below_weight, above_weight))


def build_sides(nodal_field, outer_rims):
    q = nodal_field.shape[0]
    neighbours = []
    for face_axis in range(3):
        lower_face = nodal_field[face_index(face_axis, 0)]
        upper_face = nodal_field[face_index(face_axis, q - 1)]
        elem_axis = 2 + face_axis
        elem_count = upper_face.shape[elem_axis]
        if outer_rims is None or face_axis == 2:
            before_rim = jnp.zeros_like(lax.slice_in_dim(upper_face, 0, 1, axis=elem_axis))
            after_rim = before_rim
        else:
            before_rim, after_rim = outer_rims[face_axis]
        side_low = jnp.concatenate([before_rim, lax.slice_in_dim(upper_face, 0, elem_count - 1, axis=elem_axis)], elem_axis)
        side_high = jnp.concatenate([lax.slice_in_dim(lower_face, 1, elem_count, axis=elem_axis), after_rim], elem_axis)
        neighbours.append((side_low, side_high))
    return neighbours


def assemble(nodal_field, middle, stiffness, penalty, neighbours, weights):
    q = nodal_field.shape[0]
    product = jnp.dot(stiffness, nodal_field.reshape(q * q * q, -1), precision=PRECISE)
    result = product.reshape(nodal_field.shape) * middle
    for face_axis in range(3):
        lower_face = nodal_field[face_index(face_axis, 0)]
        upper_face = nodal_field[face_index(face_axis, q - 1)]
        side_low, side_high = neighbours[face_axis]
        weight_low, weight_high = weights[face_axis]
        result = result.at[face_index(face_axis, 0)].add(penalty * weight_low * (lower_face - side_low))
        result = result.at[face_index(face_axis, q - 1)].add(penalty * weight_high * (upper_face - side_high))
    return result


def inverse_diagonal(middle, weights, stiffness, penalty):
    edge_count = cube_side(stiffness.shape[0])
    nodal_diag = jnp.diagonal(stiffness).reshape(edge_count, edge_count, edge_count)
    total = nodal_diag[:, :, :, None, None, None] * middle[None, None, None]
    for face_axis in range(3):
        low_marks = np.zeros(edge_count)
        low_marks[0] = 1.0
        high_marks = np.zeros(edge_count)
        high_marks[edge_count - 1] = 1.0
        shape_list = [1, 1, 1, 1, 1, 1]
        shape_list[face_axis] = edge_count
        low_array = jnp.asarray(low_marks.reshape(shape_list), dtype=jnp.float32)
        high_array = jnp.asarray(high_marks.reshape(shape_list), dtype=jnp.float32)
        weight_low, weight_high = weights[face_axis]
        total = total + penalty * (low_array * weight_low[None, None, None] + high_array * weight_high[None, None, None])
    return 1.0 / total


def chebyshev(solution, residual, inverse, apply_fn, steps, lowest):
    center = 0.5 * (LAMBDA_TOP + lowest)
    radius = 0.5 * (LAMBDA_TOP - lowest)
    sigma_ratio = center / radius
    factor = 1.0 / sigma_ratio
    update = inverse * residual / center
    for k in range(steps):
        solution = solution + update
        residual = residual - apply_fn(update)
        if k + 1 < steps:
            next_factor = 1.0 / (2.0 * sigma_ratio - factor)
            update = next_factor * factor * update + (2.0 * next_factor / radius) * inverse * residual
            factor = next_factor
    return solution, residual


def reference(right_side, coefficient, bottom_top, stiff_five, stiff_three, stiff_one):
    padded = jnp.pad(coefficient, ((1, 1), (1, 1), (0, 0)))
    middle, weights = face_weights(padded, bottom_top)

    def apply_five(nodal_field):
        return assemble(nodal_field, middle, stiff_five, 3.0, build_sides(nodal_field, None), weights)

    def apply_three(nodal_field):
        return assemble(nodal_field, middle, stiff_three, 2.0, build_sides(nodal_field, None), weights)

    def apply_one(nodal_field):
        return assemble(nodal_field, middle, stiff_one, 1.0, build_sides(nodal_field, None), weights)

    inverse_five = inverse_diagonal(middle, weights, stiff_five, 3.0)
    inverse_three = inverse_diagonal(middle, weights, stiff_three, 2.0)
    inverse_one = inverse_diagonal(middle, weights, stiff_one, 1.0)
    table_high = lagrange_table(Q5, Q3)
    table_low = lagrange_table(Q3, Q1)
    solution, residual = chebyshev(jnp.zeros_like(right_side), right_side, inverse_five, apply_five, DEGREE, LAMBDA_TOP / 8.0)
    residual_three = restrict(residual, table_high)
    error_three, rest_three = chebyshev(jnp.zeros_like(residual_three), residual_three, inverse_three, apply_three, DEGREE, LAMBDA_TOP / 8.0)
    residual_one = restrict(rest_three, table_low)
    error_one, unused = chebyshev(jnp.zeros_like(residual_one), residual_one, inverse_one, apply_one, COARSE_ITERS, LAMBDA_TOP / 40.0)
    lifted = prolong(error_one, table_low)
    error_three, rest_three = chebyshev(error_three + lifted, rest_three - apply_three(lifted), inverse_three, apply_three, DEGREE, LAMBDA_TOP / 8.0)
    lifted_five = prolong(error_three, table_high)
    solution, residual = chebyshev(solution + lifted_five, residual - apply_five(lifted_five), inverse_five, apply_five, DEGREE, LAMBDA_TOP / 8.0)
    return solution, residual
```

```python
import functools

import jax
import jax.numpy as jnp
import numpy as np
from jax import lax
from jax.experimental import pallas as pl
from jax.experimental.pallas import tpu as pltpu
from jax.sharding import PartitionSpec as P

MESH = pl.DeviceIdType.MESH
F32 = jnp.float32
BF16 = jnp.bfloat16
Q5, Q3, Q1 = 6, 4, 2
DEGREE = 3
COARSE_ITERS = 8
LAMBDA_TOP = 2.2
NY, NZ = 8, 128
PENALTY = {Q5: 3.0, Q3: 2.0, Q1: 1.0}


def lagrange(fine_count, coarse_count):
    fine = np.linspace(-1.0, 1.0, fine_count)
    coarse = np.linspace(-1.0, 1.0, coarse_count)
    table = np.ones((fine_count, coarse_count))
    for c in range(coarse_count):
        for o in range(coarse_count):
            if o != c:
                table[:, c] = table[:, c] * (fine - coarse[o]) / (coarse[c] - coarse[o])
    return table.astype(np.float32)


def chebyshev_factors(steps, lowest):
    center = 0.5 * (LAMBDA_TOP + lowest)
    radius = 0.5 * (LAMBDA_TOP - lowest)
    sigma = center / radius
    rho = 1.0 / sigma
    pairs = []
    for _ in range(steps - 1):
        rho_next = 1.0 / (2.0 * sigma - rho)
        pairs.append((rho_next * rho, 2.0 * rho_next / radius))
        rho = rho_next
    return 1.0 / center, pairs


def weighted(table_row, terms):
    total = None
    for value, term in zip(table_row, terms):
        if value == 0.0:
            continue
        part = term if value == 1.0 else float(value) * term
        total = part if total is None else total + part
    return total


def tiles(value, *lead):
    return value.reshape(*lead, NY, NZ)


def kernel(
    coef, ends, rhs, s5, s3, s1, sol, res,
    d5, t5, inv5, x3, r3, d3, t3, inv3, x1, r1, d1, t1, inv1,
    sh5, sl5, sh3, sl3, work, weights, hx, hy, ytile, pack, hc,
    ssem, rsem, csem, crsem,
):
    slab, cross = lax.axis_index("slab"), lax.axis_index("cross")
    ns, nc = lax.axis_size("slab"), lax.axis_size("cross")
    sides = (
        ("slab", slab - 1, slab > 0),
        ("slab", slab + 1, slab < ns - 1),
        ("cross", cross - 1, cross > 0),
        ("cross", cross + 1, cross < nc - 1),
    )
    hc[...] = jnp.zeros_like(hc)
    hx[...] = jnp.zeros_like(hx)
    hy[...] = jnp.zeros_like(hy)
    ytile[...] = jnp.zeros_like(ytile)
    barrier = pltpu.get_barrier_semaphore()
    for axis, index, there in sides:

        @pl.when(there)
        def _(axis=axis, index=index):
            pl.semaphore_signal(barrier, inc=1, device_id={axis: index}, device_id_type=MESH)

    pl.semaphore_wait(barrier, sum(there.astype(jnp.int32) for _, _, there in sides))

    def coef_copy(k):
        return pltpu.make_async_remote_copy(
            src_ref=coef, dst_ref=hc.at[k ^ 1], send_sem=csem.at[k], recv_sem=crsem.at[k ^ 1],
            device_id={sides[k][0]: sides[k][1]}, device_id_type=MESH,
        )

    def coef_arrival(k):
        return pltpu.make_async_remote_copy(
            src_ref=coef, dst_ref=hc.at[k], send_sem=csem.at[k], recv_sem=crsem.at[k],
            device_id={sides[k][0]: sides[k][1]}, device_id_type=MESH,
        )

    for k in range(4):

        @pl.when(sides[k][2])
        def _(k=k):
            coef_copy(k).start()

    def split(table, high, low, count, padded):
        value = table[...]
        high[...] = jnp.zeros_like(high)
        low[...] = jnp.zeros_like(low)
        top = value.astype(BF16)
        high[pl.ds(0, count), pl.ds(0, count)] = top
        low[pl.ds(0, count), pl.ds(0, count)] = (value - top.astype(F32)).astype(BF16)

    split(s5, sh5, sl5, Q5**3, sh5.shape[0])
    split(s3, sh3, sl3, Q3**3, sh3.shape[0])

    def spread_diagonal(table, inv, count):
        value = table[...]
        same = lax.broadcasted_iota(jnp.int32, value.shape, 0) == lax.broadcasted_iota(jnp.int32, value.shape, 1)
        column = jnp.sum(jnp.where(same, value, 0.0), axis=1, keepdims=True)
        wide = jnp.broadcast_to(column, (count, NZ))
        for y in range(NY):
            inv[pl.ds(y, count, stride=NY), :] = wide

    spread_diagonal(s5, inv5, Q5**3)
    spread_diagonal(s3, inv3, Q3**3)
    for n in range(Q1**3):
        inv1[pl.ds(n * NY, NY), :] = jnp.full((NY, NZ), s1[n, n])

    for k in range(4):

        @pl.when(sides[k][2])
        def _(k=k):
            coef_arrival(k).wait_recv()
            coef_copy(k).wait_send()

    row = lax.broadcasted_iota(jnp.int32, (NY, NZ), 0)
    lane = lax.broadcasted_iota(jnp.int32, (NY, NZ), 1)
    c = coef[...]
    bottom = jnp.zeros((NY, NZ), F32)
    top = jnp.zeros((NY, NZ), F32)
    for y in range(NY):
        bottom = jnp.where(row == y, ends[0, y].astype(F32), bottom)
        top = jnp.where(row == y, ends[1, y].astype(F32), top)
    y_before = jnp.where(row == 0, pltpu.roll(hc[2], 1, 0), pltpu.roll(c, 1, 0))
    y_after = jnp.where(row == NY - 1, pltpu.roll(hc[3], NY - 1, 0), pltpu.roll(c, NY - 1, 0))
    weights[0] = 0.5 * (c + hc[0])
    weights[1] = 0.5 * (c + hc[1])
    weights[2] = 0.5 * (c + y_before)
    weights[3] = 0.5 * (c + y_after)
    weights[4] = jnp.where(lane == 0, bottom * c, 0.5 * (c + pltpu.roll(c, 1, 1)))
    weights[5] = jnp.where(lane == NZ - 1, top * c, 0.5 * (c + pltpu.roll(c, NZ - 1, 1)))

    def invert(q, inv):
        p = PENALTY[q]
        xl, xh, yl, yh, zl, zh = (p * weights[k] for k in range(6))

        def body(i, carry):
            at = pl.ds(pl.multiple_of(i * q * q * NY, NY), q * q * NY)
            wx = jnp.where(i == 0, xl, 0.0) + jnp.where(i == q - 1, xh, 0.0)
            base = tiles(inv[at, :], q, q) * c + wx
            base = ends_added(base, q, (jnp.broadcast_to(yl, (q, NY, NZ)), jnp.broadcast_to(yh, (q, NY, NZ))),
                              (jnp.broadcast_to(zl, (q, NY, NZ)), jnp.broadcast_to(zh, (q, NY, NZ))))
            inv[at, :] = (1.0 / base).reshape(q * q * NY, NZ)
            return carry

        lax.fori_loop(0, q, body, 0)

    def ends_added(base, q, y_pair, z_pair):
        first = base[0:1] + y_pair[0][None]
        last = base[q - 1 : q] + y_pair[1][None]
        base = jnp.concatenate([first, base[1 : q - 1], last] if q > 2 else [first, last], 0)
        first = base[:, 0:1] + z_pair[0][:, None]
        last = base[:, q - 1 : q] + z_pair[1][:, None]
        return jnp.concatenate([first, base[:, 1 : q - 1], last] if q > 2 else [first, last], 1)

    invert(Q5, inv5)
    invert(Q3, inv3)
    invert(Q1, inv1)

    def face_copy(k, q, d, slot, arriving):
        face = q * q * NY
        if k < 2:
            src = d.at[pl.ds(0 if k == 0 else (q**3) * NY - face, face), :]
            dst = hx.at[slot, k if arriving else k ^ 1, pl.ds(0, face), :]
        else:
            src = pack.at[k - 2, pl.ds(0, q * NY), :]
            dst = hy.at[slot, (k if arriving else k ^ 1) - 2, pl.ds(0, q * NY), :]
        return pltpu.make_async_remote_copy(
            src_ref=src, dst_ref=dst,
            send_sem=ssem.at[k, slot], recv_sem=rsem.at[k if arriving else k ^ 1, slot],
            device_id={sides[k][0]: sides[k][1]}, device_id_type=MESH,
        )

    def send_faces(q, d, slot):
        for k in range(2):

            @pl.when(sides[k][2])
            def _(k=k):
                face_copy(k, q, d, slot, False).start()

        for i in range(q):
            pack[0, pl.ds(i * NY, q), :] = d[pl.ds(i * q * q * NY, q, stride=NY), :]
            pack[1, pl.ds(i * NY, q), :] = d[pl.ds((i * q * q + q * (q - 1)) * NY + NY - 1, q, stride=NY), :]
        for k in range(2, 4):

            @pl.when(sides[k][2])
            def _(k=k):
                face_copy(k, q, d, slot, False).start()

    def take_faces(q, d, slot):
        for k in range(4):

            @pl.when(sides[k][2])
            def _(k=k):
                face_copy(k, q, d, slot, True).wait_recv()

        for k in range(4):

            @pl.when(sides[k][2])
            def _(k=k):
                face_copy(k, q, d, slot, False).wait_send()

        for i in range(q):
            ytile[0, pl.ds(i * q * NY, q, stride=NY), :] = hy[slot, 0, pl.ds(i * NY, q), :]
            ytile[1, pl.ds(i * q * NY + NY - 1, q, stride=NY), :] = hy[slot, 1, pl.ds(i * NY, q), :]

    def product_wide(q, d, t, high, low):
        count = q**3
        padded = high.shape[0]
        s_high, s_low = high[...], low[...]
        for y in range(0, NY, 2):
            pair = [d[pl.ds(y + h, count, stride=NY), :] for h in range(2)]
            v = jnp.concatenate(pair, 1)
            if padded > count:
                v = jnp.concatenate([v, jnp.zeros((padded - count, 2 * NZ), F32)], 0)
            v_high = v.astype(BF16)
            v_low = (v - v_high.astype(F32)).astype(BF16)
            out = jnp.dot(s_high, v_high, preferred_element_type=F32)
            out += jnp.dot(s_high, v_low, preferred_element_type=F32)
            out += jnp.dot(s_low, v_high, preferred_element_type=F32)
            for h in range(2):
                t[pl.ds(y + h, count, stride=NY), :] = out[:count, h * NZ : (h + 1) * NZ]

    def product_small(d, t):
        count = Q1**3
        parts = [d[pl.ds(n * NY, NY), :] for n in range(count)]
        for m in range(count):
            total = s1[m, 0] * parts[0]
            for n in range(1, count):
                total += s1[m, n] * parts[n]
            t[pl.ds(m * NY, NY), :] = total

    def apply(level, slot):
        q, d, t, r = level["q"], level["d"], level["t"], level["r"]
        p = PENALTY[q]
        send_faces(q, d, slot)
        level["product"]()

        def local(i, carry):
            yl, yh, zl, zh = (p * weights[k] for k in range(2, 6))
            at = pl.ds(pl.multiple_of(i * q * q * NY, NY), q * q * NY)
            dv = tiles(d[at, :], q, q)
            lo, hi = dv[0], dv[q - 1]
            y_pair = (
                yl * (lo - jnp.where(row == 0, 0.0, pltpu.roll(hi, 1, 1))),
                yh * (hi - jnp.where(row == NY - 1, 0.0, pltpu.roll(lo, NY - 1, 1))),
            )
            lo, hi = dv[:, 0], dv[:, q - 1]
            z_pair = (
                zl * (lo - jnp.where(lane == 0, 0.0, pltpu.roll(hi, 1, 2))),
                zh * (hi - jnp.where(lane == NZ - 1, 0.0, pltpu.roll(lo, NZ - 1, 2))),
            )
            total = ends_added(tiles(t[at, :], q, q) * c, q, y_pair, z_pair)
            r[at, :] = r[at, :] - total.reshape(q * q * NY, NZ)
            return carry

        lax.fori_loop(0, q, local, 0)
        take_faces(q, d, slot)
        face = q * q * NY
        for k in range(2):
            at = pl.ds(0 if k == 0 else (q**3) * NY - face, face)
            step = p * weights[k] * tiles(d[at, :] - hx[slot, k, pl.ds(0, face), :], q * q)
            r[at, :] = r[at, :] - step.reshape(face, NZ)

        def rim(i, carry):
            for k in range(2):
                at = pl.ds(pl.multiple_of((i * q * q + k * q * (q - 1)) * NY, NY), q * NY)
                step = p * weights[2 + k] * tiles(ytile[k, pl.ds(pl.multiple_of(i * q * NY, NY), q * NY), :], q)
                r[at, :] = r[at, :] + step.reshape(q * NY, NZ)
            return carry

        lax.fori_loop(0, q, rim, 0)

    def first_update(level, factor, fresh):
        q, d, x, r, inv = level["q"], level["d"], level["x"], level["r"], level["inv"]

        def body(i, carry):
            at = pl.ds(pl.multiple_of(i * q * q * NY, NY), q * q * NY)
            step = inv[at, :] * r[at, :] * factor
            d[at, :] = step
            x[at, :] = step if fresh else x[at, :] + step
            return carry

        lax.fori_loop(0, q, body, 0)

    def next_update(level, a, b):
        q, d, x, r, inv = level["q"], level["d"], level["x"], level["r"], level["inv"]

        def body(i, carry):
            at = pl.ds(pl.multiple_of(i * q * q * NY, NY), q * q * NY)
            step = a * d[at, :] + b * inv[at, :] * r[at, :]
            d[at, :] = step
            x[at, :] = x[at, :] + step
            return carry

        lax.fori_loop(0, q, body, 0)

    def pick(k, values):
        out = jnp.float32(values[0])
        for n in range(1, len(values)):
            out = jnp.where(k == n, jnp.float32(values[n]), out)
        return out

    def smooth(level, steps, lowest, fresh, exchange, last):
        factor, pairs = chebyshev_factors(steps, lowest)
        first_update(level, factor, fresh)

        def body(k, carry):
            apply(level, lax.rem(exchange + k, 2))
            next_update(level, pick(k, [a for a, _ in pairs]), pick(k, [b for _, b in pairs]))
            return carry

        lax.fori_loop(0, steps - 1, body, 0)
        if last:
            apply(level, (exchange + steps - 1) % 2)

    def restrict(fine, coarse, qf, qc):
        table = lagrange(qf, qc)

        def body(j, carry):
            rows = [tiles(fine[pl.ds(pl.multiple_of((i * qf * qf + j * qf) * NY, NY), qf * NY), :], qf) for i in range(qf)]
            for a in range(qc):
                along = weighted(table[:, a], rows)
                out = [weighted(table[:, e], [along[k] for k in range(qf)]) for e in range(qc)]
                for e in range(qc):
                    work[pl.ds(pl.multiple_of((j * qc * qc + a * qc + e) * NY, NY), NY), :] = out[e]
            return carry

        lax.fori_loop(0, qf, body, 0)

        def gather(a, carry):
            rows = [work[pl.ds(pl.multiple_of((j * qc * qc + a * qc) * NY, NY), qc * NY), :] for j in range(qf)]
            for b in range(qc):
                coarse[pl.ds(pl.multiple_of((a * qc * qc + b * qc) * NY, NY), qc * NY), :] = weighted(table[:, b], rows)
            return carry

        lax.fori_loop(0, qc, gather, 0)

    def prolong(coarse, fine, sum_into, qf, qc):
        table = lagrange(qf, qc)

        def spread(a, carry):
            rows = [coarse[pl.ds(pl.multiple_of((a * qc * qc + b * qc) * NY, NY), qc * NY), :] for b in range(qc)]
            for j in range(qf):
                work[pl.ds(pl.multiple_of((j * qc * qc + a * qc) * NY, NY), qc * NY), :] = weighted(table[j], rows)
            return carry

        lax.fori_loop(0, qc, spread, 0)

        def body(j, carry):
            along = []
            for a in range(qc):
                part = tiles(work[pl.ds(pl.multiple_of((j * qc * qc + a * qc) * NY, NY), qc * NY), :], qc)
                along.append([weighted(table[k], [part[e] for e in range(qc)]) for k in range(qf)])
            for i in range(qf):
                for k in range(qf):
                    value = weighted(table[i], [along[a][k] for a in range(qc)])
                    at = pl.ds(pl.multiple_of((i * qf * qf + j * qf + k) * NY, NY), NY)
                    fine[at, :] = value
                    sum_into[at, :] = sum_into[at, :] + value
            return carry

        lax.fori_loop(0, qf, body, 0)

    five = dict(q=Q5, d=d5, t=t5, r=res, x=sol, inv=inv5, product=lambda: product_wide(Q5, d5, t5, sh5, sl5))
    three = dict(q=Q3, d=d3, t=t3, r=r3, x=x3, inv=inv3, product=lambda: product_wide(Q3, d3, t3, sh3, sl3))
    one = dict(q=Q1, d=d1, t=t1, r=r1, x=x1, inv=inv1, product=lambda: product_small(d1, t1))

    res[...] = rhs[...]
    smooth(five, DEGREE, LAMBDA_TOP / 8.0, True, 0, True)
    restrict(res, r3, Q5, Q3)
    smooth(three, DEGREE, LAMBDA_TOP / 8.0, True, 3, True)
    restrict(r3, r1, Q3, Q1)
    smooth(one, COARSE_ITERS, LAMBDA_TOP / 40.0, True, 6, False)
    prolong(x1, d3, x3, Q3, Q1)
    apply(three, 13 % 2)
    smooth(three, DEGREE, LAMBDA_TOP / 8.0, False, 14, False)
    prolong(x3, d5, sol, Q5, Q3)
    apply(five, 16 % 2)
    smooth(five, DEGREE, LAMBDA_TOP / 8.0, False, 17, True)


def per_device(right_side, coefficient, bottom_top, stiff_five, stiff_three, stiff_one):
    shape = right_side.shape
    n5, n3, n1 = Q5**3 * NY, Q3**3 * NY, Q1**3 * NY
    vmem = pl.BlockSpec(memory_space=pltpu.VMEM)
    smem = pl.BlockSpec(memory_space=pltpu.SMEM)
    field = lambda n: pltpu.VMEM((n, NZ), F32)
    dma = pltpu.SemaphoreType.DMA
    sol, res = pl.pallas_call(
        kernel,
        out_shape=[jax.ShapeDtypeStruct((n5, NZ), F32)] * 2,
        in_specs=[vmem, smem, vmem, vmem, vmem, smem],
        out_specs=[vmem, vmem],
        scratch_shapes=[
            field(n5), field(n5), field(n5),
            field(n3), field(n3), field(n3), field(n3), field(n3),
            field(n1), field(n1), field(n1), field(n1), field(n1),
            pltpu.VMEM((224, 224), BF16), pltpu.VMEM((224, 224), BF16),
            pltpu.VMEM((64, 64), BF16), pltpu.VMEM((64, 64), BF16),
            field(6 * 16 * NY), pltpu.VMEM((6, NY, NZ), F32),
            pltpu.VMEM((2, 2, Q5 * Q5 * NY, NZ), F32), pltpu.VMEM((2, 2, Q5 * NY, NZ), F32),
            pltpu.VMEM((2, Q5 * Q5 * NY, NZ), F32), pltpu.VMEM((2, Q5 * NY, NZ), F32), pltpu.VMEM((4, NY, NZ), F32),
            dma((4, 2)), dma((4, 2)), dma((4,)), dma((4,)),
        ],
        compiler_params=pltpu.CompilerParams(
            collective_id=0, has_side_effects=True, vmem_limit_bytes=48 * 2**20
        ),
    )(
        coefficient.reshape(NY, NZ), bottom_top.reshape(2, NY), right_side.reshape(n5, NZ),
        stiff_five, stiff_three, stiff_one,
    )
    return sol.reshape(shape), res.reshape(shape)


def solution(mesh):
    field = P(None, None, None, "slab", "cross", None)
    return jax.shard_map(
        per_device,
        mesh=mesh,
        in_specs=(field, P("slab", "cross", None), P(None, "slab", "cross"), P(), P(), P()),
        out_specs=(field, field),
        check_vma=False,
    )
```

```python
import functools

import jax
import jax.numpy as jnp
import numpy as np
from jax import lax
from jax.experimental import pallas as pl
from jax.experimental.pallas import tpu as pltpu
from jax.sharding import PartitionSpec as P

MESH = pl.DeviceIdType.MESH
F32 = jnp.float32
BF16 = jnp.bfloat16
Q5, Q3, Q1 = 6, 4, 2
DEGREE = 3
COARSE_ITERS = 8
LAMBDA_TOP = 2.2
NY, NZ = 8, 128
PENALTY = {Q5: 3.0, Q3: 2.0, Q1: 1.0}


def lagrange(fine_count, coarse_count):
    fine = np.linspace(-1.0, 1.0, fine_count)
    coarse = np.linspace(-1.0, 1.0, coarse_count)
    table = np.ones((fine_count, coarse_count))
    for c in range(coarse_count):
        for o in range(coarse_count):
            if o != c:
                table[:, c] = table[:, c] * (fine - coarse[o]) / (coarse[c] - coarse[o])
    return table.astype(np.float32)


def chebyshev_factors(steps, lowest):
    center = 0.5 * (LAMBDA_TOP + lowest)
    radius = 0.5 * (LAMBDA_TOP - lowest)
    sigma = center / radius
    rho = 1.0 / sigma
    pairs = []
    for _ in range(steps - 1):
        rho_next = 1.0 / (2.0 * sigma - rho)
        pairs.append((rho_next * rho, 2.0 * rho_next / radius))
        rho = rho_next
    return 1.0 / center, pairs


def weighted(table_row, terms):
    total = None
    for value, term in zip(table_row, terms):
        if value == 0.0:
            continue
        part = term if value == 1.0 else float(value) * term
        total = part if total is None else total + part
    return total


def tiles(value, *lead):
    return value.reshape(*lead, NY, NZ)


def kernel(
    coef_in, ends_in, rhs_in, s5_in, s3_in, s1_in, sol, res,
    coef, ends, s5, s3, s1,
    d5, t5, inv5, x3, r3, d3, t3, inv3, x1, r1, d1, t1, inv1,
    sh5, sl5, sh3, sl3, work, weights, hx, hy, ytile, pack, hc,
    xs, xr, ys, yr, csem, crsem, load,
):
    slab, cross = lax.axis_index("slab"), lax.axis_index("cross")
    ns, nc = lax.axis_size("slab"), lax.axis_size("cross")
    sides = (
        ("slab", slab - 1, slab > 0),
        ("slab", slab + 1, slab < ns - 1),
        ("cross", cross - 1, cross > 0),
        ("cross", cross + 1, cross < nc - 1),
    )
    hc[...] = jnp.zeros_like(hc)
    hx[...] = jnp.zeros_like(hx)
    hy[...] = jnp.zeros_like(hy)
    ytile[...] = jnp.zeros_like(ytile)
    barrier = pltpu.get_barrier_semaphore()
    for axis, index, there in sides:

        @pl.when(there)
        def _(axis=axis, index=index):
            pl.semaphore_signal(barrier, inc=1, device_id={axis: index}, device_id_type=MESH)

    pairs = ((coef_in, coef), (s5_in, s5), (s3_in, s3), (rhs_in, res), (ends_in, ends), (s1_in, s1))
    loads = [pltpu.make_async_copy(src, dst, load.at[n]) for n, (src, dst) in enumerate(pairs)]
    for copy in loads:
        copy.start()
    loads[0].wait()
    pl.semaphore_wait(barrier, sum(there.astype(jnp.int32) for _, _, there in sides))

    def coef_copy(k, arriving):
        here = k if arriving else k ^ 1
        return pltpu.make_async_remote_copy(
            src_ref=coef, dst_ref=hc.at[here], send_sem=csem.at[k], recv_sem=crsem.at[here],
            device_id={sides[k][0]: sides[k][1]}, device_id_type=MESH,
        )

    for k in range(4):

        @pl.when(sides[k][2])
        def _(k=k):
            coef_copy(k, False).start()

    for copy in loads[1:]:
        copy.wait()

    def split(table, high, low, count):
        value = table[...]
        high[...] = jnp.zeros_like(high)
        low[...] = jnp.zeros_like(low)
        top = value.astype(BF16)
        high[pl.ds(0, count), pl.ds(0, count)] = top
        low[pl.ds(0, count), pl.ds(0, count)] = (value - top.astype(F32)).astype(BF16)

    split(s5, sh5, sl5, Q5**3)
    split(s3, sh3, sl3, Q3**3)

    def spread_diagonal(table, inv, count):
        value = table[...]
        same = lax.broadcasted_iota(jnp.int32, value.shape, 0) == lax.broadcasted_iota(jnp.int32, value.shape, 1)
        column = jnp.sum(jnp.where(same, value, 0.0), axis=1, keepdims=True)
        wide = jnp.broadcast_to(column, (count, NZ))
        for y in range(NY):
            inv[pl.ds(y, count, stride=NY), :] = wide

    spread_diagonal(s5, inv5, Q5**3)
    spread_diagonal(s3, inv3, Q3**3)
    for n in range(Q1**3):
        inv1[pl.ds(n * NY, NY), :] = jnp.full((NY, NZ), s1[n, n])

    for k in range(4):

        @pl.when(sides[k][2])
        def _(k=k):
            coef_copy(k, True).wait_recv()
            coef_copy(k, False).wait_send()

    row = lax.broadcasted_iota(jnp.int32, (NY, NZ), 0)
    lane = lax.broadcasted_iota(jnp.int32, (NY, NZ), 1)
    c = coef[...]
    bottom = jnp.zeros((NY, NZ), F32)
    top = jnp.zeros((NY, NZ), F32)
    for y in range(NY):
        bottom = jnp.where(row == y, ends[0, y].astype(F32), bottom)
        top = jnp.where(row == y, ends[1, y].astype(F32), top)
    y_before = jnp.where(row == 0, pltpu.roll(hc[2], 1, 0), pltpu.roll(c, 1, 0))
    y_after = jnp.where(row == NY - 1, pltpu.roll(hc[3], NY - 1, 0), pltpu.roll(c, NY - 1, 0))
    weights[0] = 0.5 * (c + hc[0])
    weights[1] = 0.5 * (c + hc[1])
    weights[2] = 0.5 * (c + y_before)
    weights[3] = 0.5 * (c + y_after)
    weights[4] = jnp.where(lane == 0, bottom * c, 0.5 * (c + pltpu.roll(c, 1, 1)))
    weights[5] = jnp.where(lane == NZ - 1, top * c, 0.5 * (c + pltpu.roll(c, NZ - 1, 1)))

    def ends_added(base, q, y_pair, z_pair):
        first = base[0:1] + y_pair[0][None]
        last = base[q - 1 : q] + y_pair[1][None]
        base = jnp.concatenate([first, base[1 : q - 1], last] if q > 2 else [first, last], 0)
        first = base[:, 0:1] + z_pair[0][:, None]
        last = base[:, q - 1 : q] + z_pair[1][:, None]
        return jnp.concatenate([first, base[:, 1 : q - 1], last] if q > 2 else [first, last], 1)

    def slab_weight(i, q):
        return jnp.where(i == 0, PENALTY[q] * weights[0], 0.0) + jnp.where(i == q - 1, PENALTY[q] * weights[1], 0.0)

    def plane_at(i, q):
        return pl.ds(pl.multiple_of(i * (q * q * NY), NY), q * q * NY)

    def invert(q, inv):
        yl, yh, zl, zh = (jnp.broadcast_to(PENALTY[q] * weights[k], (q, NY, NZ)) for k in range(2, 6))

        def body(i, carry):
            at = plane_at(i, q)
            base = tiles(inv[at, :], q, q) * c + slab_weight(i, q)
            base = ends_added(base, q, (yl, yh), (zl, zh))
            inv[at, :] = (1.0 / base).reshape(q * q * NY, NZ)
            return carry

        lax.fori_loop(0, q, body, 0)

    invert(Q5, inv5)
    invert(Q3, inv3)
    invert(Q1, inv1)

    def lines(q):
        return [(0, 1), (q - 1, 1)] + [(j, min(2, q - 1 - j)) for j in range(1, q - 1, 2)]

    def slab_copy(k, q, d, slot, piece, arriving):
        first, count = lines(q)[piece]
        size = count * q * NY
        base = 0 if k == 0 else (q**3 - q * q) * NY
        here = k if arriving else k ^ 1
        return pltpu.make_async_remote_copy(
            src_ref=d.at[slot, pl.ds(base + first * q * NY, size), :],
            dst_ref=hx.at[slot, here, pl.ds(first * q * NY, size), :],
            send_sem=xs.at[k, piece, slot], recv_sem=xr.at[here, piece, slot],
            device_id={"slab": sides[k][1]}, device_id_type=MESH,
        )

    def cross_copy(k, q, slot, arriving):
        here = k if arriving else k ^ 1
        return pltpu.make_async_remote_copy(
            src_ref=pack.at[slot, k, pl.ds(0, q * NY), :], dst_ref=hy.at[slot, here, pl.ds(0, q * NY), :],
            send_sem=ys.at[k, slot], recv_sem=yr.at[here, slot],
            device_id={"cross": sides[2 + k][1]}, device_id_type=MESH,
        )

    def slab_do(k, method, *args):
        @pl.when(sides[k][2])
        def _():
            getattr(slab_copy(k, *args), method)()

    def cross_do(k, method, *args):
        @pl.when(sides[2 + k][2])
        def _():
            getattr(cross_copy(k, *args), method)()

    def send_slab(q, d, slot, pieces):
        for piece in pieces:
            for k in range(2):
                slab_do(k, "start", q, d, slot, piece, False)

    def send_cross(q, d, slot):
        for i in range(q):
            pack[slot, 0, pl.ds(i * NY, q), :] = d[slot, pl.ds(i * q * q * NY, q, stride=NY), :]
            pack[slot, 1, pl.ds(i * NY, q), :] = d[slot, pl.ds((i * q * q + q * (q - 1)) * NY + NY - 1, q, stride=NY), :]
        for k in range(2):
            cross_do(k, "start", q, slot, False)

    def send_all(q, d, slot):
        send_cross(q, d, slot)
        send_slab(q, d, slot, range(len(lines(q))))

    def product_wide(q, d, slot, t, high, low):
        count = q**3
        padded = high.shape[0]
        s_high, s_low = high[...], low[...]
        for y in range(0, NY, 2):
            pair = [d[slot, pl.ds(y + h, count, stride=NY), :] for h in range(2)]
            v = jnp.concatenate(pair, 1)
            if padded > count:
                v = jnp.concatenate([v, jnp.zeros((padded - count, 2 * NZ), F32)], 0)
            v_high = v.astype(BF16)
            v_low = (v - v_high.astype(F32)).astype(BF16)
            out = jnp.dot(s_high, v_high, preferred_element_type=F32)
            out += jnp.dot(s_high, v_low, preferred_element_type=F32)
            out += jnp.dot(s_low, v_high, preferred_element_type=F32)
            for h in range(2):
                t[pl.ds(y + h, count, stride=NY), :] = out[:count, h * NZ : (h + 1) * NZ]

    def product_small(d, slot, t):
        count = Q1**3
        parts = [d[slot, pl.ds(n * NY, NY), :] for n in range(count)]
        for m in range(count):
            total = s1[m, 0] * parts[0]
            for n in range(1, count):
                total += s1[m, n] * parts[n]
            t[pl.ds(m * NY, NY), :] = total

    def step(level, slot, a, b, update, send):
        q, d, t, r, x, inv = (level[name] for name in ("q", "d", "t", "r", "x", "inv"))
        p = PENALTY[q]
        other = 1 - slot
        level["product"](slot)

        def local(i, carry):
            yl, yh, zl, zh = (p * weights[k] for k in range(2, 6))
            at = plane_at(i, q)
            dv = tiles(d[slot, at, :], q, q)
            lo, hi = dv[0], dv[q - 1]
            y_pair = (
                yl * (lo - jnp.where(row == 0, 0.0, pltpu.roll(hi, 1, 1))),
                yh * (hi - jnp.where(row == NY - 1, 0.0, pltpu.roll(lo, NY - 1, 1))),
            )
            lo, hi = dv[:, 0], dv[:, q - 1]
            z_pair = (
                zl * (lo - jnp.where(lane == 0, 0.0, pltpu.roll(hi, 1, 2))),
                zh * (hi - jnp.where(lane == NZ - 1, 0.0, pltpu.roll(lo, NZ - 1, 2))),
            )
            total = ends_added(tiles(t[at, :], q, q) * c, q, y_pair, z_pair)
            r[at, :] = r[at, :] - total.reshape(q * q * NY, NZ)
            return carry

        lax.fori_loop(0, q, local, 0)
        face = q * q * NY
        for k in range(2):
            at = pl.ds(0 if k == 0 else (q**3) * NY - face, face)
            r[at, :] = r[at, :] - (p * weights[k] * tiles(d[slot, at, :], q * q)).reshape(face, NZ)

        for k in range(2):
            cross_do(k, "wait_recv", q, slot, True)
        for i in range(q):
            ytile[0, pl.ds(i * q * NY, q, stride=NY), :] = hy[slot, 0, pl.ds(i * NY, q), :]
            ytile[1, pl.ds(i * q * NY + NY - 1, q, stride=NY), :] = hy[slot, 1, pl.ds(i * NY, q), :]

        def rim(i, carry):
            for k in range(2):
                at = pl.ds(pl.multiple_of(i * (q * q * NY) + k * q * (q - 1) * NY, NY), q * NY)
                part = p * weights[2 + k] * tiles(ytile[k, pl.ds(pl.multiple_of(i * (q * NY), NY), q * NY), :], q)
                r[at, :] = r[at, :] + part.reshape(q * NY, NZ)
            return carry

        lax.fori_loop(0, q, rim, 0)

        def advance(at):
            value = a * d[slot, at, :] + b * inv[at, :] * r[at, :]
            d[other, at, :] = value
            x[at, :] = x[at, :] + value

        if update and q > 2:

            def inside(i, carry):
                advance(plane_at(i, q))
                return carry

            lax.fori_loop(1, q - 1, inside, 0)

        pieces = lines(q)
        groups = [[0, 1]] + [[n] for n in range(2, len(pieces))]
        for number, group in enumerate(groups):
            for piece in group:
                first, count = pieces[piece]
                size = count * q * NY
                for k in range(2):
                    slab_do(k, "wait_recv", q, d, slot, piece, True)
                    at = pl.ds((0 if k == 0 else (q**3 - q * q) * NY) + first * q * NY, size)
                    part = p * weights[k] * tiles(hx[slot, k, pl.ds(first * q * NY, size), :], count * q)
                    r[at, :] = r[at, :] + part.reshape(size, NZ)
                    if update:
                        advance(at)
            if send:
                if number == 0:
                    send_cross(q, d, other)
                send_slab(q, d, other, group)
        for k in range(2):
            cross_do(k, "wait_send", q, slot, False)
            for piece in range(len(pieces)):
                slab_do(k, "wait_send", q, d, slot, piece, False)

    def first_update(level, slot, factor):
        q, d, x, r, inv = (level[name] for name in ("q", "d", "x", "r", "inv"))

        def body(i, carry):
            at = plane_at(i, q)
            value = inv[at, :] * r[at, :] * factor
            d[slot, at, :] = value
            x[at, :] = value
            return carry

        lax.fori_loop(0, q, body, 0)
        send_all(q, d, slot)

    def pick(k, values):
        out = jnp.float32(values[0])
        for n in range(1, len(values)):
            out = jnp.where(k == n, jnp.float32(values[n]), out)
        return out

    def run(level, exchange, factors, last):
        loop = len(factors) if last else len(factors) - 1

        def body(k, carry):
            a, b = pick(k, [f[0] for f in factors]), pick(k, [f[1] for f in factors])
            step(level, lax.rem(exchange + k, 2), a, b, True, True)
            return carry

        lax.fori_loop(0, loop, body, 0)
        slot = (exchange + loop) % 2
        if last:
            step(level, slot, 0.0, 0.0, False, False)
        else:
            step(level, slot, *factors[-1], True, False)

    def restrict(fine, coarse, qf, qc):
        table = lagrange(qf, qc)

        def body(j, carry):
            rows = [tiles(fine[pl.ds(pl.multiple_of(j * (qf * NY) + i * qf * qf * NY, NY), qf * NY), :], qf) for i in range(qf)]
            for a in range(qc):
                along = weighted(table[:, a], rows)
                for e in range(qc):
                    out = weighted(table[:, e], [along[k] for k in range(qf)])
                    work[pl.ds(pl.multiple_of(j * (qc * qc * NY) + (a * qc + e) * NY, NY), NY), :] = out
            return carry

        lax.fori_loop(0, qf, body, 0)

        def gather(a, carry):
            rows = [work[pl.ds(pl.multiple_of(a * (qc * NY) + j * qc * qc * NY, NY), qc * NY), :] for j in range(qf)]
            for b in range(qc):
                at = pl.ds(pl.multiple_of(a * (qc * qc * NY) + b * qc * NY, NY), qc * NY)
                coarse[at, :] = weighted(table[:, b], rows)
            return carry

        lax.fori_loop(0, qc, gather, 0)

    def prolong(coarse, fine, slot, sum_into, qf, qc):
        table = lagrange(qf, qc)

        def spread(a, carry):
            rows = [coarse[pl.ds(pl.multiple_of(a * (qc * qc * NY) + b * qc * NY, NY), qc * NY), :] for b in range(qc)]
            for j in range(qf):
                at = pl.ds(pl.multiple_of(a * (qc * NY) + j * qc * qc * NY, NY), qc * NY)
                work[at, :] = weighted(table[j], rows)
            return carry

        lax.fori_loop(0, qc, spread, 0)

        def body(j, carry):
            along = []
            for a in range(qc):
                at = pl.ds(pl.multiple_of(j * (qc * qc * NY) + a * qc * NY, NY), qc * NY)
                part = tiles(work[at, :], qc)
                along.append([weighted(table[k], [part[e] for e in range(qc)]) for k in range(qf)])
            for i in range(qf):
                for k in range(qf):
                    value = weighted(table[i], [along[a][k] for a in range(qc)])
                    at = pl.ds(pl.multiple_of(j * (qf * NY) + (i * qf * qf + k) * NY, NY), NY)
                    fine[slot, at, :] = value
                    sum_into[at, :] = sum_into[at, :] + value
            return carry

        lax.fori_loop(0, qf, body, 0)
        send_all(qf, fine, slot)

    five = dict(q=Q5, d=d5, t=t5, r=res, x=sol, inv=inv5, product=lambda slot: product_wide(Q5, d5, slot, t5, sh5, sl5))
    three = dict(q=Q3, d=d3, t=t3, r=r3, x=x3, inv=inv3, product=lambda slot: product_wide(Q3, d3, slot, t3, sh3, sl3))
    one = dict(q=Q1, d=d1, t=t1, r=r1, x=x1, inv=inv1, product=lambda slot: product_small(d1, slot, t1))

    first, pairs = chebyshev_factors(DEGREE, LAMBDA_TOP / 8.0)
    coarse_first, coarse_pairs = chebyshev_factors(COARSE_ITERS, LAMBDA_TOP / 40.0)
    first_update(five, 0, first)
    run(five, 0, pairs, True)
    restrict(res, r3, Q5, Q3)
    first_update(three, 1, first)
    run(three, 3, pairs, True)
    restrict(r3, r1, Q3, Q1)
    first_update(one, 0, coarse_first)
    run(one, 6, coarse_pairs, False)
    prolong(x1, d3, 1, x3, Q3, Q1)
    run(three, 13, [(0.0, first)] + pairs, False)
    prolong(x3, d5, 0, sol, Q5, Q3)
    run(five, 16, [(0.0, first)] + pairs, True)


def per_device(right_side, coefficient, bottom_top, stiff_five, stiff_three, stiff_one):
    shape = right_side.shape
    n5, n3, n1 = Q5**3 * NY, Q3**3 * NY, Q1**3 * NY
    vmem = pl.BlockSpec(memory_space=pltpu.VMEM)
    hbm = pl.BlockSpec(memory_space=pltpu.HBM)
    field = lambda n: pltpu.VMEM((n, NZ), F32)
    pair = lambda n: pltpu.VMEM((2, n, NZ), F32)
    dma = pltpu.SemaphoreType.DMA
    sol, res = pl.pallas_call(
        kernel,
        out_shape=[jax.ShapeDtypeStruct((n5, NZ), F32)] * 2,
        in_specs=[hbm] * 6,
        out_specs=[vmem, vmem],
        scratch_shapes=[
            field(NY), pltpu.SMEM((2, NY), jnp.int32), pltpu.VMEM((Q5**3, Q5**3), F32), pltpu.VMEM((Q3**3, Q3**3), F32),
            pltpu.SMEM((Q1**3, Q1**3), F32),
            pair(n5), field(n5), field(n5),
            field(n3), field(n3), pair(n3), field(n3), field(n3),
            field(n1), field(n1), pair(n1), field(n1), field(n1),
            pltpu.VMEM((224, 224), BF16), pltpu.VMEM((224, 224), BF16),
            pltpu.VMEM((64, 64), BF16), pltpu.VMEM((64, 64), BF16),
            field(6 * 16 * NY), pltpu.VMEM((6, NY, NZ), F32),
            pltpu.VMEM((2, 2, Q5 * Q5 * NY, NZ), F32), pltpu.VMEM((2, 2, Q5 * NY, NZ), F32),
            pltpu.VMEM((2, Q5 * Q5 * NY, NZ), F32), pltpu.VMEM((2, 2, Q5 * NY, NZ), F32), pltpu.VMEM((4, NY, NZ), F32),
            dma((2, 4, 2)), dma((2, 4, 2)), dma((2, 2)), dma((2, 2)), dma((4,)), dma((4,)), dma((6,)),
        ],
        compiler_params=pltpu.CompilerParams(
            collective_id=0, has_side_effects=True, vmem_limit_bytes=48 * 2**20
        ),
    )(
        coefficient.reshape(NY, NZ), bottom_top.reshape(2, NY), right_side.reshape(n5, NZ),
        stiff_five, stiff_three, stiff_one,
    )
    return sol.reshape(shape), res.reshape(shape)


def solution(mesh):
    field = P(None, None, None, "slab", "cross", None)
    return jax.shard_map(
        per_device,
        mesh=mesh,
        in_specs=(field, P("slab", "cross", None), P(None, "slab", "cross"), P(), P(), P()),
        out_specs=(field, field),
        check_vma=False,
    )
```

```python
import functools

import jax
import jax.numpy as jnp
import numpy as np
from jax import lax
from jax.experimental import pallas as pl
from jax.experimental.pallas import tpu as pltpu
from jax.sharding import PartitionSpec as P

MESH = pl.DeviceIdType.MESH
F32 = jnp.float32
BF16 = jnp.bfloat16
Q5, Q3, Q1 = 6, 4, 2
DEGREE = 3
COARSE_ITERS = 8
LAMBDA_TOP = 2.2
NY, NZ = 8, 128
SLOTS = 4
PENALTY = {Q5: 3.0, Q3: 2.0, Q1: 1.0}


def lagrange(fine_count, coarse_count):
    fine = np.linspace(-1.0, 1.0, fine_count)
    coarse = np.linspace(-1.0, 1.0, coarse_count)
    table = np.ones((fine_count, coarse_count))
    for c in range(coarse_count):
        for o in range(coarse_count):
            if o != c:
                table[:, c] = table[:, c] * (fine - coarse[o]) / (coarse[c] - coarse[o])
    return table.astype(np.float32)


def chebyshev_factors(steps, lowest):
    center = 0.5 * (LAMBDA_TOP + lowest)
    radius = 0.5 * (LAMBDA_TOP - lowest)
    sigma = center / radius
    rho = 1.0 / sigma
    pairs = []
    for _ in range(steps - 1):
        rho_next = 1.0 / (2.0 * sigma - rho)
        pairs.append((rho_next * rho, 2.0 * rho_next / radius))
        rho = rho_next
    return 1.0 / center, pairs


def weighted(table_row, terms):
    total = None
    for value, term in zip(table_row, terms):
        if value == 0.0:
            continue
        part = term if value == 1.0 else float(value) * term
        total = part if total is None else total + part
    return total


def tiles(value, *lead):
    return value.reshape(*lead, NY, NZ)


def kernel(
    coef_in, ends_in, rhs_in, s5_in, s3_in, s1_in, sol, res,
    coef, ends, s5, s3, s1,
    d5, t5, inv5, x3, r3, d3, t3, inv3, x1, r1, d1, t1, inv1,
    sh5, sl5, sh3, sl3, work, weights, hx, hy, ytile, pack, hc,
    hd, dpack, dtile, gx3, gx1, gy3, gy1, gp3, gp1, gw,
    xs, xr, ys, yr, cs, cr, gs, gr, csem, crsem, load,
):
    slab, cross = lax.axis_index("slab"), lax.axis_index("cross")
    ns, nc = lax.axis_size("slab"), lax.axis_size("cross")
    sides = (
        ("slab", slab - 1, slab > 0),
        ("slab", slab + 1, slab < ns - 1),
        ("cross", cross - 1, cross > 0),
        ("cross", cross + 1, cross < nc - 1),
    )
    corners = [
        ({"slab": slab + 2 * k - 1, "cross": cross + 2 * m - 1}, sides[k][2] & sides[2 + m][2])
        for k in range(2) for m in range(2)
    ]

    for k in range(2):

        @pl.when(jnp.logical_not(sides[k][2]))
        def _(k=k):
            hc[k] = jnp.zeros_like(hc[k])
            gw[k] = jnp.zeros_like(gw[k])
            gx3[k] = jnp.zeros_like(gx3[k])
            gx1[k] = jnp.zeros_like(gx1[k])
            for slot in range(SLOTS):
                hx[slot, k] = jnp.zeros_like(hx[slot, k])

        @pl.when(jnp.logical_not(sides[2 + k][2]))
        def _(k=k):
            hc[2 + k] = jnp.zeros_like(hc[2 + k])
            gw[2 + k] = jnp.zeros_like(gw[2 + k])
            gy3[k] = jnp.zeros_like(gy3[k])
            gy1[k] = jnp.zeros_like(gy1[k])
            for slot in range(SLOTS):
                hy[slot, k] = jnp.zeros_like(hy[slot, k])

    for g in range(4):

        @pl.when(jnp.logical_not(corners[g][1]))
        def _(g=g):
            for slot in range(SLOTS):
                hd[slot, g] = jnp.zeros_like(hd[slot, g])

    barrier = pltpu.get_barrier_semaphore()
    peers = [({axis: index}, there) for axis, index, there in sides] + corners
    for device, there in peers:

        @pl.when(there)
        def _(device=device):
            pl.semaphore_signal(barrier, inc=1, device_id=device, device_id_type=MESH)

    pairs = ((coef_in, coef), (s5_in, s5), (s3_in, s3), (rhs_in, res), (ends_in, ends), (s1_in, s1))
    loads = [pltpu.make_async_copy(src, dst, load.at[n]) for n, (src, dst) in enumerate(pairs)]
    for copy in loads:
        copy.start()
    ytile[...] = jnp.zeros_like(ytile)
    dtile[...] = jnp.zeros_like(dtile)
    loads[0].wait()
    pl.semaphore_wait(barrier, sum(there.astype(jnp.int32) for _, there in peers))

    def coef_copy(k, arriving):
        here = k if arriving else k ^ 1
        return pltpu.make_async_remote_copy(
            src_ref=coef, dst_ref=hc.at[here], send_sem=csem.at[k], recv_sem=crsem.at[here],
            device_id={sides[k][0]: sides[k][1]}, device_id_type=MESH,
        )

    for k in range(4):

        @pl.when(sides[k][2])
        def _(k=k):
            coef_copy(k, False).start()

    for copy in loads[1:]:
        copy.wait()

    def split(table, high, low, count):
        value = table[...]
        high[...] = jnp.zeros_like(high)
        low[...] = jnp.zeros_like(low)
        top = value.astype(BF16)
        high[pl.ds(0, count), pl.ds(0, count)] = top
        low[pl.ds(0, count), pl.ds(0, count)] = (value - top.astype(F32)).astype(BF16)

    split(s5, sh5, sl5, Q5**3)
    split(s3, sh3, sl3, Q3**3)

    def spread_diagonal(table, inv, count):
        value = table[...]
        same = lax.broadcasted_iota(jnp.int32, value.shape, 0) == lax.broadcasted_iota(jnp.int32, value.shape, 1)
        column = jnp.sum(jnp.where(same, value, 0.0), axis=1, keepdims=True)
        wide = jnp.broadcast_to(column, (count, NZ))
        for y in range(NY):
            inv[pl.ds(y, count, stride=NY), :] = wide

    spread_diagonal(s5, inv5, Q5**3)
    spread_diagonal(s3, inv3, Q3**3)
    for n in range(Q1**3):
        inv1[pl.ds(n * NY, NY), :] = jnp.full((NY, NZ), s1[n, n])

    for k in range(4):

        @pl.when(sides[k][2])
        def _(k=k):
            coef_copy(k, True).wait_recv()
            coef_copy(k, False).wait_send()

    row = lax.broadcasted_iota(jnp.int32, (NY, NZ), 0)
    lane = lax.broadcasted_iota(jnp.int32, (NY, NZ), 1)
    c = coef[...]
    bottom = jnp.zeros((NY, NZ), F32)
    top = jnp.zeros((NY, NZ), F32)
    for y in range(NY):
        bottom = jnp.where(row == y, ends[0, y].astype(F32), bottom)
        top = jnp.where(row == y, ends[1, y].astype(F32), top)
    y_before = jnp.where(row == 0, pltpu.roll(hc[2], 1, 0), pltpu.roll(c, 1, 0))
    y_after = jnp.where(row == NY - 1, pltpu.roll(hc[3], NY - 1, 0), pltpu.roll(c, NY - 1, 0))
    weights[0] = 0.5 * (c + hc[0])
    weights[1] = 0.5 * (c + hc[1])
    weights[2] = 0.5 * (c + y_before)
    weights[3] = 0.5 * (c + y_after)
    weights[4] = jnp.where(lane == 0, bottom * c, 0.5 * (c + pltpu.roll(c, 1, 1)))
    weights[5] = jnp.where(lane == NZ - 1, top * c, 0.5 * (c + pltpu.roll(c, NZ - 1, 1)))

    def ends_added(base, q, y_pair, z_pair):
        first = base[0:1] + y_pair[0][None]
        last = base[q - 1 : q] + y_pair[1][None]
        base = jnp.concatenate([first, base[1 : q - 1], last] if q > 2 else [first, last], 0)
        first = base[:, 0:1] + z_pair[0][:, None]
        last = base[:, q - 1 : q] + z_pair[1][:, None]
        return jnp.concatenate([first, base[:, 1 : q - 1], last] if q > 2 else [first, last], 1)

    def slab_weight(i, q):
        return jnp.where(i == 0, PENALTY[q] * weights[0], 0.0) + jnp.where(i == q - 1, PENALTY[q] * weights[1], 0.0)

    def plane_at(i, q):
        return pl.ds(pl.multiple_of(i * (q * q * NY), NY), q * q * NY)

    def invert(q, inv):
        yl, yh, zl, zh = (jnp.broadcast_to(PENALTY[q] * weights[k], (q, NY, NZ)) for k in range(2, 6))

        def body(i, carry):
            at = plane_at(i, q)
            base = tiles(inv[at, :], q, q) * c + slab_weight(i, q)
            base = ends_added(base, q, (yl, yh), (zl, zh))
            inv[at, :] = (1.0 / base).reshape(q * q * NY, NZ)
            return carry

        lax.fori_loop(0, q, body, 0)

    invert(Q3, inv3)
    invert(Q1, inv1)

    def pack_rows(q, source, target):
        for i in range(q):
            target[0, pl.ds(i * NY, q), :] = source[pl.ds(i * q * q * NY, q, stride=NY), :]
            target[1, pl.ds(i * NY, q), :] = source[pl.ds((i * q * q + q * (q - 1)) * NY + NY - 1, q, stride=NY), :]

    pack_rows(Q3, inv3, gp3)
    pack_rows(Q1, inv1, gp1)

    def greet_copy(k, n, arriving):
        here = k if arriving else k ^ 1
        if n == 0:
            src, dst = weights.at[pl.ds(2 if k < 2 else 0, 2)], gw.at[here]
        elif k < 2:
            q, inv, target = ((Q3, inv3, gx3), (Q1, inv1, gx1))[n - 1]
            src, dst = inv.at[pl.ds(k * (q**3 - q * q) * NY, q * q * NY), :], target.at[here]
        else:
            source, target = ((gp3, gy3), (gp1, gy1))[n - 1]
            src, dst = source.at[k - 2], target.at[here - 2]
        return pltpu.make_async_remote_copy(
            src_ref=src, dst_ref=dst, send_sem=gs.at[k, n], recv_sem=gr.at[here, n],
            device_id={sides[k][0]: sides[k][1]}, device_id_type=MESH,
        )

    for k in (2, 3, 0, 1):

        @pl.when(sides[k][2])
        def _(k=k):
            for n in range(3):
                greet_copy(k, n, False).start()

    invert(Q5, inv5)

    def greeted():
        for k in range(4):

            @pl.when(sides[k][2])
            def _(k=k):
                for n in range(3):
                    greet_copy(k, n, True).wait_recv()
                    greet_copy(k, n, False).wait_send()

    far = lax.rem(slab, 2)
    near = 1 - far

    def lines(q):
        if q < Q5:
            return [(0, q)]
        return [(0, 1), (q - 1, 1)] + [(j, min(2, q - 1 - j)) for j in range(1, q - 1, 2)]

    def face_at(k, q, first, count):
        return pl.ds(pl.multiple_of(k * ((q**3 - q * q) * NY) + first * q * NY, NY), count * q * NY)

    def slab_copy(k, q, d, slot, piece, arriving):
        first, count = (0, q) if piece is None else lines(q)[piece]
        number = 0 if piece is None else piece
        here = k if arriving else 1 - k
        return pltpu.make_async_remote_copy(
            src_ref=d.at[slot, face_at(k, q, first, count), :],
            dst_ref=hx.at[slot, here, pl.ds(first * q * NY, count * q * NY), :],
            send_sem=xs.at[k, number, slot], recv_sem=xr.at[here, number, slot],
            device_id={"slab": slab + 2 * k - 1}, device_id_type=MESH,
        )

    def cross_copy(k, q, slot, arriving):
        here = k if arriving else k ^ 1
        return pltpu.make_async_remote_copy(
            src_ref=pack.at[slot, k, pl.ds(0, q * NY), :], dst_ref=hy.at[slot, here, pl.ds(0, q * NY), :],
            send_sem=ys.at[k, slot], recv_sem=yr.at[here, slot],
            device_id={"cross": sides[2 + k][1]}, device_id_type=MESH,
        )

    def slab_do(k, method, *args):
        index = slab + 2 * k - 1

        @pl.when((index >= 0) & (index < ns))
        def _():
            getattr(slab_copy(k, *args), method)()

    def cross_do(k, method, *args):
        @pl.when(sides[2 + k][2])
        def _():
            getattr(cross_copy(k, *args), method)()

    def send_near(q, d, slot):
        slab_do(near, "start", q, d, slot, None, False)

    def send_far(q, d, slot, pieces):
        for piece in pieces:
            slab_do(far, "start", q, d, slot, piece, False)

    def send_cross(q, d, slot):
        for i in range(q):
            pack[slot, 0, pl.ds(i * NY, q), :] = d[slot, pl.ds(i * q * q * NY, q, stride=NY), :]
            pack[slot, 1, pl.ds(i * NY, q), :] = d[slot, pl.ds((i * q * q + q * (q - 1)) * NY + NY - 1, q, stride=NY), :]
        for k in range(2):
            cross_do(k, "start", q, slot, False)

    def corner_copy(g, slot, arriving):
        here = g if arriving else 3 - g
        return pltpu.make_async_remote_copy(
            src_ref=dpack.at[slot, g], dst_ref=hd.at[slot, here],
            send_sem=cs.at[g, slot], recv_sem=cr.at[here, slot],
            device_id=corners[g][0], device_id_type=MESH,
        )

    def corner_do(g, method, *args):
        @pl.when(corners[g][1])
        def _():
            getattr(corner_copy(g, *args), method)()

    def send_corners(q, d, slot):
        for g in range(4):
            k, m = g // 2, g % 2
            node = k * (q**3 - q * q) + m * (q * q - q)
            dpack[slot, g, pl.ds(0, q), :] = d[slot, pl.ds(node * NY + m * (NY - 1), q, stride=NY), :]
        for g in range(4):
            corner_do(g, "start", slot, False)

    def send_all(q, d, slot, with_corners):
        if with_corners:
            send_corners(q, d, slot)
        send_cross(q, d, slot)
        send_far(q, d, slot, range(len(lines(q))))
        send_near(q, d, slot)

    def arrived(q, d, slot, with_corners):
        for k in range(2):
            cross_do(k, "wait_recv", q, slot, True)
        slab_do(near, "wait_recv", q, d, slot, None, True)
        for piece in range(len(lines(q))):
            slab_do(far, "wait_recv", q, d, slot, piece, True)
        if with_corners:
            for g in range(4):
                corner_do(g, "wait_recv", slot, True)

    def sent(q, d, slot, with_corners):
        slab_do(near, "wait_send", q, d, slot, None, False)
        for piece in range(len(lines(q))):
            slab_do(far, "wait_send", q, d, slot, piece, False)
        for k in range(2):
            cross_do(k, "wait_send", q, slot, False)
        if with_corners:
            for g in range(4):
                corner_do(g, "wait_send", slot, False)

    def product_wide(q, d, slot, t, high, low):
        count = q**3
        padded = high.shape[0]
        s_high, s_low = high[...], low[...]
        for y in range(0, NY, 2):
            pair = [d[slot, pl.ds(y + h, count, stride=NY), :] for h in range(2)]
            v = jnp.concatenate(pair, 1)
            if padded > count:
                v = jnp.concatenate([v, jnp.zeros((padded - count, 2 * NZ), F32)], 0)
            v_high = v.astype(BF16)
            v_low = (v - v_high.astype(F32)).astype(BF16)
            out = jnp.dot(s_high, v_high, preferred_element_type=F32)
            out += jnp.dot(s_high, v_low, preferred_element_type=F32)
            out += jnp.dot(s_low, v_high, preferred_element_type=F32)
            for h in range(2):
                t[pl.ds(y + h, count, stride=NY), :] = out[:count, h * NZ : (h + 1) * NZ]

    def product_small(d, slot, t):
        count = Q1**3
        parts = [d[slot, pl.ds(n * NY, NY), :] for n in range(count)]
        for m in range(count):
            total = s1[m, 0] * parts[0]
            for n in range(1, count):
                total += s1[m, n] * parts[n]
            t[pl.ds(m * NY, NY), :] = total

    def local_part(level, slot):
        q, d, t, r = (level[name] for name in ("q", "d", "t", "r"))
        p = PENALTY[q]
        level["product"](slot)

        def local(i, carry):
            yl, yh, zl, zh = (p * weights[k] for k in range(2, 6))
            at = plane_at(i, q)
            dv = tiles(d[slot, at, :], q, q)
            lo, hi = dv[0], dv[q - 1]
            y_pair = (
                yl * (lo - jnp.where(row == 0, 0.0, pltpu.roll(hi, 1, 1))),
                yh * (hi - jnp.where(row == NY - 1, 0.0, pltpu.roll(lo, NY - 1, 1))),
            )
            lo, hi = dv[:, 0], dv[:, q - 1]
            z_pair = (
                zl * (lo - jnp.where(lane == 0, 0.0, pltpu.roll(hi, 1, 2))),
                zh * (hi - jnp.where(lane == NZ - 1, 0.0, pltpu.roll(lo, NZ - 1, 2))),
            )
            total = ends_added(tiles(t[at, :], q, q) * c, q, y_pair, z_pair)
            r[at, :] = r[at, :] - total.reshape(q * q * NY, NZ)
            return carry

        lax.fori_loop(0, q, local, 0)
        face = q * q * NY
        for k in range(2):
            at = pl.ds(0 if k == 0 else (q**3) * NY - face, face)
            r[at, :] = r[at, :] - (p * weights[k] * tiles(d[slot, at, :], q * q)).reshape(face, NZ)

    def rims(level, slot, put):
        q = level["q"]
        for i in range(q):
            ytile[0, pl.ds(i * q * NY, q, stride=NY), :] = hy[slot, 0, pl.ds(i * NY, q), :]
            ytile[1, pl.ds(i * q * NY + NY - 1, q, stride=NY), :] = hy[slot, 1, pl.ds(i * NY, q), :]

        def rim(i, carry):
            for k in range(2):
                at = pl.ds(pl.multiple_of(i * (q * q * NY) + k * q * (q - 1) * NY, NY), q * NY)
                part = PENALTY[q] * weights[2 + k] * tiles(ytile[k, pl.ds(pl.multiple_of(i * (q * NY), NY), q * NY), :], q)
                put(at, part.reshape(q * NY, NZ))
            return carry

        lax.fori_loop(0, q, rim, 0)

    def slab_term(level, slot, k, first, count):
        q = level["q"]
        part = PENALTY[q] * weights[k] * tiles(hx[slot, k, pl.ds(first * q * NY, count * q * NY), :], count * q)
        return part.reshape(count * q * NY, NZ)

    def step(level, slot, a, b, update, send):
        q, d, r, x, inv = (level[name] for name in ("q", "d", "r", "x", "inv"))
        other = lax.rem(slot + 1, SLOTS)

        def put(at, part):
            r[at, :] = r[at, :] + part

        local_part(level, slot)
        for k in range(2):
            cross_do(k, "wait_recv", q, slot, True)
        rims(level, slot, put)

        def advance(at):
            value = a * d[slot, at, :] + b * inv[at, :] * r[at, :]
            d[other, at, :] = value
            x[at, :] = x[at, :] + value

        if update and q > 2:

            def inside(i, carry):
                advance(plane_at(i, q))
                return carry

            lax.fori_loop(1, q - 1, inside, 0)

        def slab_face(k, first, count):
            at = face_at(k, q, first, count)
            put(at, slab_term(level, slot, k, first, count))
            if update:
                advance(at)

        slab_do(near, "wait_recv", q, d, slot, None, True)
        slab_face(near, 0, q)
        if send:
            send_near(q, d, other)
        pieces = lines(q)
        groups = [[0, 1]] + [[n] for n in range(2, len(pieces))] if len(pieces) > 1 else [[0]]
        for number, group in enumerate(groups):
            for piece in group:
                slab_do(far, "wait_recv", q, d, slot, piece, True)
                slab_face(far, *pieces[piece])
            if send:
                if number == 0:
                    send_cross(q, d, other)
                send_far(q, d, other, group)
        sent(q, d, slot, False)

    def correct(level, slot, other, b):
        q, d, gx, gy = (level[name] for name in ("q", "d", "gx", "gy"))
        p = PENALTY[q]
        face = q * q * NY
        for k in range(2):
            for m in range(2):
                dtile[m, pl.ds(m * (NY - 1), q, stride=NY), :] = hd[slot, 2 * k + m, pl.ds(0, q), :]
            term = p * weights[k] * tiles(d[slot, pl.ds(k * (q**3 - q * q) * NY, face), :], q, q)
            low, high = (p * gw[k, m] * tiles(dtile[m, pl.ds(0, q * NY), :], q) for m in range(2))
            first, last = term[0:1] + low[None], term[q - 1 : q] + high[None]
            term = jnp.concatenate([first, term[1 : q - 1], last] if q > 2 else [first, last], 0)
            at = pl.ds(0, face)
            hx[other, k, at, :] = hx[other, k, at, :] + b * gx[k, at, :] * term.reshape(face, NZ)
        for m in range(2):
            mine, theirs = pl.ds(m * (NY - 1), 1), pl.ds((1 - m) * (NY - 1), 1)
            for i in range(q):
                at = pl.ds(i * NY, q)
                term = p * weights[2 + m, mine, :] * pack[slot, m, at, :]
                for k in range(2):
                    if i == k * (q - 1):
                        term = term + p * gw[2 + m, k, theirs, :] * hd[slot, 2 * k + m, pl.ds(0, q), :]
                hy[other, m, at, :] = hy[other, m, at, :] + b * gy[m, at, :] * term

    def double_step(level, slot, first, second, with_corners):
        q, d, r, x, inv = (level[name] for name in ("q", "d", "r", "x", "inv"))
        other, third = lax.rem(slot + 1, SLOTS), lax.rem(slot + 2, SLOTS)

        def planes(body):
            def one_plane(i, carry):
                body(plane_at(i, q))
                return carry

            lax.fori_loop(0, q, one_plane, 0)

        def partial_next(at):
            d[other, at, :] = first[0] * d[slot, at, :] + first[1] * inv[at, :] * r[at, :]

        def put_both(at, part):
            r[at, :] = r[at, :] + part
            d[other, at, :] = d[other, at, :] + first[1] * inv[at, :] * part

        def put(at, part):
            r[at, :] = r[at, :] + part

        def add(at):
            x[at, :] = x[at, :] + d[other, at, :]

        def advance(at):
            value = second[0] * d[other, at, :] + second[1] * inv[at, :] * r[at, :]
            d[third, at, :] = value
            x[at, :] = x[at, :] + value

        local_part(level, slot)
        planes(partial_next)
        send_all(q, d, other, False)
        arrived(q, d, slot, True)
        sent(q, d, other, False)
        rims(level, slot, put_both)
        for k in range(2):
            put_both(face_at(k, q, 0, q), slab_term(level, slot, k, 0, q))
        planes(add)
        local_part(level, other)
        arrived(q, d, other, False)
        correct(level, slot, other, first[1])
        rims(level, other, put)
        for k in range(2):
            put(face_at(k, q, 0, q), slab_term(level, other, k, 0, q))
        planes(advance)
        send_all(q, d, third, with_corners)
        sent(q, d, slot, True)

    def first_update(level, slot, factor, with_corners):
        q, d, x, r, inv = (level[name] for name in ("q", "d", "x", "r", "inv"))

        def body(i, carry):
            at = plane_at(i, q)
            value = inv[at, :] * r[at, :] * factor
            d[slot, at, :] = value
            x[at, :] = value
            return carry

        lax.fori_loop(0, q, body, 0)
        send_all(q, d, slot, with_corners)

    def pick(k, values):
        out = jnp.float32(values[0])
        for n in range(1, len(values)):
            out = jnp.where(k == n, jnp.float32(values[n]), out)
        return out

    def run(level, exchange, factors, last):
        loop = len(factors) if last else len(factors) - 1

        def body(k, carry):
            a, b = pick(k, [f[0] for f in factors]), pick(k, [f[1] for f in factors])
            step(level, lax.rem(exchange + k, SLOTS), a, b, True, True)
            return carry

        lax.fori_loop(0, loop, body, 0)
        slot = (exchange + loop) % SLOTS
        if last:
            step(level, slot, 0.0, 0.0, False, False)
        else:
            step(level, slot, *factors[-1], True, False)

    def run_doubled(level, exchange, factors, last):
        loop = (len(factors) - (0 if last else 1)) // 2

        def body(k, carry):
            first = [pick(k, [f[n] for f in factors[: 2 * loop : 2]]) for n in range(2)]
            second = [pick(k, [f[n] for f in factors[1 : 2 * loop : 2]]) for n in range(2)]
            double_step(level, lax.rem(exchange + 2 * k, SLOTS), first, second, True)
            return carry

        if loop > 1:
            lax.fori_loop(0, loop - 1, body, 0)
        double_step(level, (exchange + 2 * loop - 2) % SLOTS, *factors[2 * loop - 2 : 2 * loop], False)
        slot = (exchange + 2 * loop) % SLOTS
        if last:
            step(level, slot, 0.0, 0.0, False, False)
        else:
            step(level, slot, *factors[-1], True, False)

    def restrict(fine, coarse, qf, qc):
        table = lagrange(qf, qc)

        def body(j, carry):
            rows = [tiles(fine[pl.ds(pl.multiple_of(j * (qf * NY) + i * qf * qf * NY, NY), qf * NY), :], qf) for i in range(qf)]
            for a in range(qc):
                along = weighted(table[:, a], rows)
                for e in range(qc):
                    out = weighted(table[:, e], [along[k] for k in range(qf)])
                    work[pl.ds(pl.multiple_of(j * (qc * qc * NY) + (a * qc + e) * NY, NY), NY), :] = out
            return carry

        lax.fori_loop(0, qf, body, 0)

        def gather(a, carry):
            rows = [work[pl.ds(pl.multiple_of(a * (qc * NY) + j * qc * qc * NY, NY), qc * NY), :] for j in range(qf)]
            for b in range(qc):
                at = pl.ds(pl.multiple_of(a * (qc * qc * NY) + b * qc * NY, NY), qc * NY)
                coarse[at, :] = weighted(table[:, b], rows)
            return carry

        lax.fori_loop(0, qc, gather, 0)

    def prolong(coarse, fine, slot, sum_into, qf, qc, with_corners):
        table = lagrange(qf, qc)

        def spread(a, carry):
            rows = [coarse[pl.ds(pl.multiple_of(a * (qc * qc * NY) + b * qc * NY, NY), qc * NY), :] for b in range(qc)]
            for j in range(qf):
                at = pl.ds(pl.multiple_of(a * (qc * NY) + j * qc * qc * NY, NY), qc * NY)
                work[at, :] = weighted(table[j], rows)
            return carry

        lax.fori_loop(0, qc, spread, 0)

        def body(j, carry):
            along = []
            for a in range(qc):
                at = pl.ds(pl.multiple_of(j * (qc * qc * NY) + a * qc * NY, NY), qc * NY)
                part = tiles(work[at, :], qc)
                along.append([weighted(table[k], [part[e] for e in range(qc)]) for k in range(qf)])
            for i in range(qf):
                for k in range(qf):
                    value = weighted(table[i], [along[a][k] for a in range(qc)])
                    at = pl.ds(pl.multiple_of(j * (qf * NY) + (i * qf * qf + k) * NY, NY), NY)
                    fine[slot, at, :] = value
                    sum_into[at, :] = sum_into[at, :] + value
            return carry

        lax.fori_loop(0, qf, body, 0)
        send_all(qf, fine, slot, with_corners)

    five = dict(q=Q5, d=d5, t=t5, r=res, x=sol, inv=inv5, product=lambda slot: product_wide(Q5, d5, slot, t5, sh5, sl5))
    three = dict(q=Q3, d=d3, t=t3, r=r3, x=x3, inv=inv3, gx=gx3, gy=gy3, product=lambda slot: product_wide(Q3, d3, slot, t3, sh3, sl3))
    one = dict(q=Q1, d=d1, t=t1, r=r1, x=x1, inv=inv1, gx=gx1, gy=gy1, product=lambda slot: product_small(d1, slot, t1))

    first, pairs = chebyshev_factors(DEGREE, LAMBDA_TOP / 8.0)
    coarse_first, coarse_pairs = chebyshev_factors(COARSE_ITERS, LAMBDA_TOP / 40.0)
    first_update(five, 0, first, False)
    run(five, 0, pairs, True)
    restrict(res, r3, Q5, Q3)
    first_update(three, 3, first, True)
    greeted()
    run_doubled(three, 3, pairs, True)
    restrict(r3, r1, Q3, Q1)
    first_update(one, 6 % SLOTS, coarse_first, True)
    run_doubled(one, 6, coarse_pairs, False)
    prolong(x1, d3, 13 % SLOTS, x3, Q3, Q1, True)
    run_doubled(three, 13, [(0.0, first)] + pairs, False)
    prolong(x3, d5, 16 % SLOTS, sol, Q5, Q3, False)
    run(five, 16, [(0.0, first)] + pairs, True)


def per_device(right_side, coefficient, bottom_top, stiff_five, stiff_three, stiff_one):
    shape = right_side.shape
    n5, n3, n1 = Q5**3 * NY, Q3**3 * NY, Q1**3 * NY
    vmem = pl.BlockSpec(memory_space=pltpu.VMEM)
    hbm = pl.BlockSpec(memory_space=pltpu.HBM)
    field = lambda n: pltpu.VMEM((n, NZ), F32)
    slots = lambda *n: pltpu.VMEM((SLOTS, *n, NZ), F32)
    two = lambda n: pltpu.VMEM((2, n, NZ), F32)
    dma = pltpu.SemaphoreType.DMA
    sol, res = pl.pallas_call(
        kernel,
        out_shape=[jax.ShapeDtypeStruct((n5, NZ), F32)] * 2,
        in_specs=[hbm] * 6,
        out_specs=[vmem, vmem],
        scratch_shapes=[
            field(NY), pltpu.SMEM((2, NY), jnp.int32), pltpu.VMEM((Q5**3, Q5**3), F32), pltpu.VMEM((Q3**3, Q3**3), F32),
            pltpu.SMEM((Q1**3, Q1**3), F32),
            slots(n5), field(n5), field(n5),
            field(n3), field(n3), slots(n3), field(n3), field(n3),
            field(n1), field(n1), slots(n1), field(n1), field(n1),
            pltpu.VMEM((224, 224), BF16), pltpu.VMEM((224, 224), BF16),
            pltpu.VMEM((64, 64), BF16), pltpu.VMEM((64, 64), BF16),
            field(6 * 16 * NY), pltpu.VMEM((6, NY, NZ), F32),
            slots(2, Q5 * Q5 * NY), slots(2, Q5 * NY), two(Q5 * Q5 * NY), slots(2, Q5 * NY), pltpu.VMEM((4, NY, NZ), F32),
            slots(4, NY), slots(4, NY), two(Q3 * NY),
            two(Q3 * Q3 * NY), two(Q1 * Q1 * NY), two(Q3 * NY), two(Q1 * NY), two(Q3 * NY), two(Q1 * NY),
            pltpu.VMEM((4, 2, NY, NZ), F32),
            dma((2, 4, SLOTS)), dma((2, 4, SLOTS)), dma((2, SLOTS)), dma((2, SLOTS)), dma((4, SLOTS)), dma((4, SLOTS)),
            dma((4, 3)), dma((4, 3)), dma((4,)), dma((4,)), dma((6,)),
        ],
        compiler_params=pltpu.CompilerParams(
            collective_id=0, has_side_effects=True, vmem_limit_bytes=48 * 2**20
        ),
    )(
        *(
            pltpu.with_memory_space_constraint(value, pltpu.HBM)
            for value in (
                coefficient.reshape(NY, NZ), bottom_top.reshape(2, NY), right_side.reshape(n5, NZ),
                stiff_five, stiff_three, stiff_one,
            )
        )
    )
    return sol.reshape(shape), res.reshape(shape)


def solution(mesh):
    field = P(None, None, None, "slab", "cross", None)
    return jax.shard_map(
        per_device,
        mesh=mesh,
        in_specs=(field, P("slab", "cross", None), P(None, "slab", "cross"), P(), P(), P()),
        out_specs=(field, field),
        check_vma=False,
    )
```

```python
import functools

import jax
import jax.numpy as jnp
import numpy as np
from jax import lax
from jax.experimental import pallas as pl
from jax.experimental.pallas import tpu as pltpu
from jax.sharding import PartitionSpec as P

MESH = pl.DeviceIdType.MESH
F32 = jnp.float32
BF16 = jnp.bfloat16
Q5, Q3, Q1 = 6, 4, 2
DEGREE = 3
COARSE_ITERS = 8
LAMBDA_TOP = 2.2
NY, NZ = 8, 128
SLOTS = 4
PENALTY = {Q5: 3.0, Q3: 2.0, Q1: 1.0}


def lagrange(fine_count, coarse_count):
    fine = np.linspace(-1.0, 1.0, fine_count)
    coarse = np.linspace(-1.0, 1.0, coarse_count)
    table = np.ones((fine_count, coarse_count))
    for c in range(coarse_count):
        for o in range(coarse_count):
            if o != c:
                table[:, c] = table[:, c] * (fine - coarse[o]) / (coarse[c] - coarse[o])
    return table.astype(np.float32)


def chebyshev_factors(steps, lowest):
    center = 0.5 * (LAMBDA_TOP + lowest)
    radius = 0.5 * (LAMBDA_TOP - lowest)
    sigma = center / radius
    rho = 1.0 / sigma
    pairs = []
    for _ in range(steps - 1):
        rho_next = 1.0 / (2.0 * sigma - rho)
        pairs.append((rho_next * rho, 2.0 * rho_next / radius))
        rho = rho_next
    return 1.0 / center, pairs


def weighted(table_row, terms):
    total = None
    for value, term in zip(table_row, terms):
        if value == 0.0:
            continue
        part = term if value == 1.0 else float(value) * term
        total = part if total is None else total + part
    return total


def tiles(value, *lead):
    return value.reshape(*lead, NY, NZ)


def kernel(
    coef_in, ends_in, rhs_in, s5_in, s3_in, s1_in, sol, res,
    coef, ends, s5, s3, s1,
    d5, t5, inv5, x3, r3, d3, t3, inv3, x1, r1, d1, t1, inv1,
    sh5, sl5, sh3, sl3, work, weights, hx, hy, ytile, pack, hc,
    hd, dpack, dtile, gx3, gx1, gy3, gy1, gp3, gp1, gw, hxl, hyl,
    xs, xr, ys, yr, cs, cr, gs, gr, csem, crsem, load,
):
    slab, cross = lax.axis_index("slab"), lax.axis_index("cross")
    ns, nc = lax.axis_size("slab"), lax.axis_size("cross")
    sides = (
        ("slab", slab - 1, slab > 0),
        ("slab", slab + 1, slab < ns - 1),
        ("cross", cross - 1, cross > 0),
        ("cross", cross + 1, cross < nc - 1),
    )
    corners = [
        ({"slab": slab + 2 * k - 1, "cross": cross + 2 * m - 1}, sides[k][2] & sides[2 + m][2])
        for k in range(2) for m in range(2)
    ]

    for k in range(2):

        @pl.when(jnp.logical_not(sides[k][2]))
        def _(k=k):
            hc[k] = jnp.zeros_like(hc[k])
            gw[k] = jnp.zeros_like(gw[k])
            gx3[k] = jnp.zeros_like(gx3[k])
            gx1[k] = jnp.zeros_like(gx1[k])
            for slot in range(SLOTS):
                hx[slot, k] = jnp.zeros_like(hx[slot, k])

        @pl.when(jnp.logical_not(sides[2 + k][2]))
        def _(k=k):
            hc[2 + k] = jnp.zeros_like(hc[2 + k])
            gw[2 + k] = jnp.zeros_like(gw[2 + k])
            gy3[k] = jnp.zeros_like(gy3[k])
            gy1[k] = jnp.zeros_like(gy1[k])
            for slot in range(SLOTS):
                hy[slot, k] = jnp.zeros_like(hy[slot, k])

    for g in range(4):

        @pl.when(jnp.logical_not(corners[g][1]))
        def _(g=g):
            for slot in range(SLOTS):
                hd[slot, g] = jnp.zeros_like(hd[slot, g])

    barrier = pltpu.get_barrier_semaphore()
    peers = [({axis: index}, there) for axis, index, there in sides] + corners
    for device, there in peers:

        @pl.when(there)
        def _(device=device):
            pl.semaphore_signal(barrier, inc=1, device_id=device, device_id_type=MESH)

    pairs = ((coef_in, coef), (s5_in, s5), (s3_in, s3), (rhs_in, res), (ends_in, ends), (s1_in, s1))
    loads = [pltpu.make_async_copy(src, dst, load.at[n]) for n, (src, dst) in enumerate(pairs)]
    for copy in loads:
        copy.start()
    ytile[...] = jnp.zeros_like(ytile)
    dtile[...] = jnp.zeros_like(dtile)
    loads[0].wait()
    pl.semaphore_wait(barrier, sum(there.astype(jnp.int32) for _, there in peers))

    def coef_copy(k, arriving):
        here = k if arriving else k ^ 1
        return pltpu.make_async_remote_copy(
            src_ref=coef, dst_ref=hc.at[here], send_sem=csem.at[k], recv_sem=crsem.at[here],
            device_id={sides[k][0]: sides[k][1]}, device_id_type=MESH,
        )

    for k in range(4):

        @pl.when(sides[k][2])
        def _(k=k):
            coef_copy(k, False).start()

    for copy in loads[1:]:
        copy.wait()

    def split(table, high, low, count):
        value = table[...]
        high[...] = jnp.zeros_like(high)
        low[...] = jnp.zeros_like(low)
        top = value.astype(BF16)
        high[pl.ds(0, count), pl.ds(0, count)] = top
        low[pl.ds(0, count), pl.ds(0, count)] = (value - top.astype(F32)).astype(BF16)

    split(s5, sh5, sl5, Q5**3)
    split(s3, sh3, sl3, Q3**3)

    def spread_diagonal(table, inv, count):
        value = table[...]
        same = lax.broadcasted_iota(jnp.int32, value.shape, 0) == lax.broadcasted_iota(jnp.int32, value.shape, 1)
        column = jnp.sum(jnp.where(same, value, 0.0), axis=1, keepdims=True)
        wide = jnp.broadcast_to(column, (count, NZ))
        for y in range(NY):
            inv[pl.ds(y, count, stride=NY), :] = wide

    spread_diagonal(s5, inv5, Q5**3)
    spread_diagonal(s3, inv3, Q3**3)
    for n in range(Q1**3):
        inv1[pl.ds(n * NY, NY), :] = jnp.full((NY, NZ), s1[n, n])

    for k in range(4):

        @pl.when(sides[k][2])
        def _(k=k):
            coef_copy(k, True).wait_recv()
            coef_copy(k, False).wait_send()

    row = lax.broadcasted_iota(jnp.int32, (NY, NZ), 0)
    lane = lax.broadcasted_iota(jnp.int32, (NY, NZ), 1)
    c = coef[...]
    bottom = jnp.zeros((NY, NZ), F32)
    top = jnp.zeros((NY, NZ), F32)
    for y in range(NY):
        bottom = jnp.where(row == y, ends[0, y].astype(F32), bottom)
        top = jnp.where(row == y, ends[1, y].astype(F32), top)
    y_before = jnp.where(row == 0, pltpu.roll(hc[2], 1, 0), pltpu.roll(c, 1, 0))
    y_after = jnp.where(row == NY - 1, pltpu.roll(hc[3], NY - 1, 0), pltpu.roll(c, NY - 1, 0))
    weights[0] = 0.5 * (c + hc[0])
    weights[1] = 0.5 * (c + hc[1])
    weights[2] = 0.5 * (c + y_before)
    weights[3] = 0.5 * (c + y_after)
    weights[4] = jnp.where(lane == 0, bottom * c, 0.5 * (c + pltpu.roll(c, 1, 1)))
    weights[5] = jnp.where(lane == NZ - 1, top * c, 0.5 * (c + pltpu.roll(c, NZ - 1, 1)))

    def ends_added(base, q, y_pair, z_pair):
        first = base[0:1] + y_pair[0][None]
        last = base[q - 1 : q] + y_pair[1][None]
        base = jnp.concatenate([first, base[1 : q - 1], last] if q > 2 else [first, last], 0)
        first = base[:, 0:1] + z_pair[0][:, None]
        last = base[:, q - 1 : q] + z_pair[1][:, None]
        return jnp.concatenate([first, base[:, 1 : q - 1], last] if q > 2 else [first, last], 1)

    def slab_weight(i, q):
        return jnp.where(i == 0, PENALTY[q] * weights[0], 0.0) + jnp.where(i == q - 1, PENALTY[q] * weights[1], 0.0)

    def plane_at(i, q):
        return pl.ds(pl.multiple_of(i * (q * q * NY), NY), q * q * NY)

    def invert(q, inv):
        yl, yh, zl, zh = (jnp.broadcast_to(PENALTY[q] * weights[k], (q, NY, NZ)) for k in range(2, 6))

        def body(i, carry):
            at = plane_at(i, q)
            base = tiles(inv[at, :], q, q) * c + slab_weight(i, q)
            base = ends_added(base, q, (yl, yh), (zl, zh))
            inv[at, :] = (1.0 / base).reshape(q * q * NY, NZ)
            return carry

        lax.fori_loop(0, q, body, 0)

    invert(Q3, inv3)
    invert(Q1, inv1)

    def pack_rows(q, source, target):
        for i in range(q):
            target[0, pl.ds(i * NY, q), :] = source[pl.ds(i * q * q * NY, q, stride=NY), :]
            target[1, pl.ds(i * NY, q), :] = source[pl.ds((i * q * q + q * (q - 1)) * NY + NY - 1, q, stride=NY), :]

    pack_rows(Q3, inv3, gp3)
    pack_rows(Q1, inv1, gp1)

    def greet_copy(k, n, arriving):
        here = k if arriving else k ^ 1
        if n == 0:
            src, dst = weights.at[pl.ds(2 if k < 2 else 0, 2)], gw.at[here]
        elif k < 2:
            q, inv, target = ((Q3, inv3, gx3), (Q1, inv1, gx1))[n - 1]
            src, dst = inv.at[pl.ds(k * (q**3 - q * q) * NY, q * q * NY), :], target.at[here]
        else:
            source, target = ((gp3, gy3), (gp1, gy1))[n - 1]
            src, dst = source.at[k - 2], target.at[here - 2]
        return pltpu.make_async_remote_copy(
            src_ref=src, dst_ref=dst, send_sem=gs.at[k, n], recv_sem=gr.at[here, n],
            device_id={sides[k][0]: sides[k][1]}, device_id_type=MESH,
        )

    for k in (2, 3, 0, 1):

        @pl.when(sides[k][2])
        def _(k=k):
            for n in range(3):
                greet_copy(k, n, False).start()

    invert(Q5, inv5)

    def greeted():
        for k in range(4):

            @pl.when(sides[k][2])
            def _(k=k):
                for n in range(3):
                    greet_copy(k, n, True).wait_recv()
                    greet_copy(k, n, False).wait_send()

    far = lax.rem(slab, 2)
    near = 1 - far

    def lines(q):
        if q < Q5:
            return [(0, q)]
        return [(0, 1), (q - 1, 1)] + [(j, min(2, q - 1 - j)) for j in range(1, q - 1, 2)]

    def face_at(k, q, first, count):
        return pl.ds(pl.multiple_of(k * ((q**3 - q * q) * NY) + first * q * NY, NY), count * q * NY)

    def slab_copy(k, q, d, slot, piece, arriving):
        first, count = (0, q) if piece is None else lines(q)[piece]
        number = 0 if piece is None else piece
        here = k if arriving else 1 - k
        return pltpu.make_async_remote_copy(
            src_ref=d.at[slot, face_at(k, q, first, count), :],
            dst_ref=hx.at[slot, here, pl.ds(first * q * NY, count * q * NY), :],
            send_sem=xs.at[k, number, slot], recv_sem=xr.at[here, number, slot],
            device_id={"slab": slab + 2 * k - 1}, device_id_type=MESH,
        )

    def cross_copy(k, q, slot, arriving):
        here = k if arriving else k ^ 1
        return pltpu.make_async_remote_copy(
            src_ref=pack.at[slot, k, pl.ds(0, q * NY), :], dst_ref=hy.at[slot, here, pl.ds(0, q * NY), :],
            send_sem=ys.at[k, slot], recv_sem=yr.at[here, slot],
            device_id={"cross": sides[2 + k][1]}, device_id_type=MESH,
        )

    def slab_do(k, method, *args):
        index = slab + 2 * k - 1

        @pl.when((index >= 0) & (index < ns))
        def _():
            getattr(slab_copy(k, *args), method)()

    def cross_do(k, method, *args):
        @pl.when(sides[2 + k][2])
        def _():
            getattr(cross_copy(k, *args), method)()

    def send_near(q, d, slot):
        slab_do(near, "start", q, d, slot, None, False)

    def send_far(q, d, slot, pieces):
        for piece in pieces:
            slab_do(far, "start", q, d, slot, piece, False)

    def send_cross(q, d, slot):
        for i in range(q):
            pack[slot, 0, pl.ds(i * NY, q), :] = d[slot, pl.ds(i * q * q * NY, q, stride=NY), :]
            pack[slot, 1, pl.ds(i * NY, q), :] = d[slot, pl.ds((i * q * q + q * (q - 1)) * NY + NY - 1, q, stride=NY), :]
        for k in range(2):
            cross_do(k, "start", q, slot, False)

    def corner_copy(g, slot, arriving):
        here = g if arriving else 3 - g
        return pltpu.make_async_remote_copy(
            src_ref=dpack.at[slot, g], dst_ref=hd.at[slot, here],
            send_sem=cs.at[g, slot], recv_sem=cr.at[here, slot],
            device_id=corners[g][0], device_id_type=MESH,
        )

    def corner_do(g, method, *args):
        @pl.when(corners[g][1])
        def _():
            getattr(corner_copy(g, *args), method)()

    def send_corners(q, d, slot):
        for g in range(4):
            k, m = g // 2, g % 2
            node = k * (q**3 - q * q) + m * (q * q - q)
            dpack[slot, g, pl.ds(0, q), :] = d[slot, pl.ds(node * NY + m * (NY - 1), q, stride=NY), :]
        for g in range(4):
            corner_do(g, "start", slot, False)

    def send_all(q, d, slot, with_corners):
        if with_corners:
            send_corners(q, d, slot)
        send_cross(q, d, slot)
        send_far(q, d, slot, range(len(lines(q))))
        send_near(q, d, slot)

    def arrived(q, d, slot, with_corners):
        for k in range(2):
            cross_do(k, "wait_recv", q, slot, True)
        slab_do(near, "wait_recv", q, d, slot, None, True)
        for piece in range(len(lines(q))):
            slab_do(far, "wait_recv", q, d, slot, piece, True)
        if with_corners:
            for g in range(4):
                corner_do(g, "wait_recv", slot, True)

    def sent(q, d, slot, with_corners):
        slab_do(near, "wait_send", q, d, slot, None, False)
        for piece in range(len(lines(q))):
            slab_do(far, "wait_send", q, d, slot, piece, False)
        for k in range(2):
            cross_do(k, "wait_send", q, slot, False)
        if with_corners:
            for g in range(4):
                corner_do(g, "wait_send", slot, False)

    def product_wide(q, d, slot, t, high, low):
        count = q**3
        padded = high.shape[0]
        s_high, s_low = high[...], low[...]
        for y in range(0, NY, 2):
            pair = [d[slot, pl.ds(y + h, count, stride=NY), :] for h in range(2)]
            v = jnp.concatenate(pair, 1)
            if padded > count:
                v = jnp.concatenate([v, jnp.zeros((padded - count, 2 * NZ), F32)], 0)
            v_high = v.astype(BF16)
            v_low = (v - v_high.astype(F32)).astype(BF16)
            out = jnp.dot(s_high, v_high, preferred_element_type=F32)
            out += jnp.dot(s_high, v_low, preferred_element_type=F32)
            out += jnp.dot(s_low, v_high, preferred_element_type=F32)
            for h in range(2):
                t[pl.ds(y + h, count, stride=NY), :] = out[:count, h * NZ : (h + 1) * NZ]

    def product_small(d, slot, t):
        count = Q1**3
        parts = [d[slot, pl.ds(n * NY, NY), :] for n in range(count)]
        for m in range(count):
            total = s1[m, 0] * parts[0]
            for n in range(1, count):
                total += s1[m, n] * parts[n]
            t[pl.ds(m * NY, NY), :] = total

    def local_part(level, slot):
        q, d, t, r = (level[name] for name in ("q", "d", "t", "r"))
        p = PENALTY[q]
        level["product"](slot)

        def local(i, carry):
            yl, yh, zl, zh = (p * weights[k] for k in range(2, 6))
            at = plane_at(i, q)
            dv = tiles(d[slot, at, :], q, q)
            lo, hi = dv[0], dv[q - 1]
            y_pair = (
                yl * (lo - jnp.where(row == 0, 0.0, pltpu.roll(hi, 1, 1))),
                yh * (hi - jnp.where(row == NY - 1, 0.0, pltpu.roll(lo, NY - 1, 1))),
            )
            lo, hi = dv[:, 0], dv[:, q - 1]
            z_pair = (
                zl * (lo - jnp.where(lane == 0, 0.0, pltpu.roll(hi, 1, 2))),
                zh * (hi - jnp.where(lane == NZ - 1, 0.0, pltpu.roll(lo, NZ - 1, 2))),
            )
            total = ends_added(tiles(t[at, :], q, q) * c, q, y_pair, z_pair)
            r[at, :] = r[at, :] - total.reshape(q * q * NY, NZ)
            return carry

        lax.fori_loop(0, q, local, 0)
        face = q * q * NY
        for k in range(2):
            at = pl.ds(0 if k == 0 else (q**3) * NY - face, face)
            r[at, :] = r[at, :] - (p * weights[k] * tiles(d[slot, at, :], q * q)).reshape(face, NZ)

    def rims(level, source, put):
        q = level["q"]
        for i in range(q):
            ytile[0, pl.ds(i * q * NY, q, stride=NY), :] = source[0, pl.ds(i * NY, q), :]
            ytile[1, pl.ds(i * q * NY + NY - 1, q, stride=NY), :] = source[1, pl.ds(i * NY, q), :]

        def rim(i, carry):
            for k in range(2):
                at = pl.ds(pl.multiple_of(i * (q * q * NY) + k * q * (q - 1) * NY, NY), q * NY)
                part = PENALTY[q] * weights[2 + k] * tiles(ytile[k, pl.ds(pl.multiple_of(i * (q * NY), NY), q * NY), :], q)
                put(at, part.reshape(q * NY, NZ))
            return carry

        lax.fori_loop(0, q, rim, 0)

    def slab_term(level, source, k, first, count):
        q = level["q"]
        part = PENALTY[q] * weights[k] * tiles(source[k, pl.ds(first * q * NY, count * q * NY), :], count * q)
        return part.reshape(count * q * NY, NZ)

    def step(level, slot, a, b, update, send):
        q, d, r, x, inv = (level[name] for name in ("q", "d", "r", "x", "inv"))
        other = lax.rem(slot + 1, SLOTS)

        def put(at, part):
            r[at, :] = r[at, :] + part

        local_part(level, slot)
        for k in range(2):
            cross_do(k, "wait_recv", q, slot, True)
        rims(level, hy.at[slot], put)

        def advance(at):
            value = a * d[slot, at, :] + b * inv[at, :] * r[at, :]
            d[other, at, :] = value
            x[at, :] = x[at, :] + value

        if update and q > 2:

            def inside(i, carry):
                advance(plane_at(i, q))
                return carry

            lax.fori_loop(1, q - 1, inside, 0)

        def slab_face(k, first, count):
            at = face_at(k, q, first, count)
            put(at, slab_term(level, hx.at[slot], k, first, count))
            if update:
                advance(at)

        slab_do(near, "wait_recv", q, d, slot, None, True)
        slab_face(near, 0, q)
        if send:
            send_near(q, d, other)
        pieces = lines(q)
        groups = [[0, 1]] + [[n] for n in range(2, len(pieces))] if len(pieces) > 1 else [[0]]
        for number, group in enumerate(groups):
            for piece in group:
                slab_do(far, "wait_recv", q, d, slot, piece, True)
                slab_face(far, *pieces[piece])
            if send:
                if number == 0:
                    send_cross(q, d, other)
                send_far(q, d, other, group)
        sent(q, d, slot, False)

    def correct(level, slot, other, b):
        q, d, gx, gy = (level[name] for name in ("q", "d", "gx", "gy"))
        p = PENALTY[q]
        face = q * q * NY
        for k in range(2):
            for m in range(2):
                dtile[m, pl.ds(m * (NY - 1), q, stride=NY), :] = hd[slot, 2 * k + m, pl.ds(0, q), :]
            term = p * weights[k] * tiles(d[slot, pl.ds(k * (q**3 - q * q) * NY, face), :], q, q)
            low, high = (p * gw[k, m] * tiles(dtile[m, pl.ds(0, q * NY), :], q) for m in range(2))
            first, last = term[0:1] + low[None], term[q - 1 : q] + high[None]
            term = jnp.concatenate([first, term[1 : q - 1], last] if q > 2 else [first, last], 0)
            at = pl.ds(0, face)
            hx[other, k, at, :] = hx[other, k, at, :] + b * gx[k, at, :] * term.reshape(face, NZ)
        for m in range(2):
            mine, theirs = pl.ds(m * (NY - 1), 1), pl.ds((1 - m) * (NY - 1), 1)
            for i in range(q):
                at = pl.ds(i * NY, q)
                term = p * weights[2 + m, mine, :] * pack[slot, m, at, :]
                for k in range(2):
                    if i == k * (q - 1):
                        term = term + p * gw[2 + m, k, theirs, :] * hd[slot, 2 * k + m, pl.ds(0, q), :]
                hy[other, m, at, :] = hy[other, m, at, :] + b * gy[m, at, :] * term

    def planes(q, body):
        def one_plane(i, carry):
            body(plane_at(i, q))
            return carry

        lax.fori_loop(0, q, one_plane, 0)

    def half_round(level, slot, a, b, total):
        q, d, r, x, inv = (level[name] for name in ("q", "d", "r", "x", "inv"))
        other = lax.rem(slot + 1, SLOTS)

        def partial_next(at):
            value = a * d[slot, at, :] + b * inv[at, :] * r[at, :]
            d[other, at, :] = x[at, :] + value if total else value

        def put_both(at, part):
            r[at, :] = r[at, :] + part
            d[other, at, :] = d[other, at, :] + b * inv[at, :] * part

        local_part(level, slot)
        planes(q, partial_next)
        send_all(q, d, other, False)
        arrived(q, d, slot, True)
        sent(q, d, other, False)
        rims(level, hy.at[slot], put_both)
        for k in range(2):
            put_both(face_at(k, q, 0, q), slab_term(level, hx.at[slot], k, 0, q))

    def double_step(level, slot, first, second, with_corners, total):
        q, d, r, x, inv = (level[name] for name in ("q", "d", "r", "x", "inv"))
        other, third = lax.rem(slot + 1, SLOTS), lax.rem(slot + 2, SLOTS)

        def put(at, part):
            r[at, :] = r[at, :] + part

        def add(at):
            x[at, :] = x[at, :] + d[other, at, :]

        def advance(at):
            value = second[0] * d[other, at, :] + second[1] * inv[at, :] * r[at, :]
            if total:
                d[third, at, :] = x[at, :] + value
            else:
                d[third, at, :] = value
                x[at, :] = x[at, :] + value

        half_round(level, slot, *first, False)
        planes(q, add)
        local_part(level, other)
        arrived(q, d, other, False)
        correct(level, slot, other, first[1])
        rims(level, hy.at[other], put)
        for k in range(2):
            put(face_at(k, q, 0, q), slab_term(level, hx.at[other], k, 0, q))
        planes(q, advance)
        send_all(q, d, third, with_corners)
        sent(q, d, slot, True)

    def finish_round(level, slot, a, b):
        q, d = level["q"], level["d"]
        other = lax.rem(slot + 1, SLOTS)
        half_round(level, slot, a, b, True)
        arrived(q, d, other, False)
        correct(level, slot, other, b)
        sent(q, d, slot, True)

    def lift_faces(qc, qf, slot):
        table = lagrange(qf, qc)
        spread = []
        for e in range(qc):
            column = jnp.zeros((NY, NZ), F32)
            for n in range(qf):
                if table[n, e] != 0.0:
                    column = jnp.where(row == n, float(table[n, e]), column)
            spread.append(column)
        for k in range(2):
            lines_in = tiles(hx[slot, k, pl.ds(0, qc * qc * NY), :], qc, qc)
            for j in range(qf):
                line = weighted(table[j], [lines_in[n] for n in range(qc)])
                for n in range(qf):
                    hxl[k, pl.ds((j * qf + n) * NY, NY), :] = weighted(table[n], [line[e] for e in range(qc)])
            for i in range(qf):
                line = weighted(table[i], [hy[slot, k, pl.ds(a * NY, qc), :] for a in range(qc)])
                value = spread[0] * line[0:1]
                for e in range(1, qc):
                    value = value + spread[e] * line[e : e + 1]
                hyl[k, pl.ds(i * NY, NY), :] = value

    def lifted_step(coarse, slot, level, here, factor, awaited, with_corners):
        q, d, r, x, inv = (level[name] for name in ("q", "d", "r", "x", "inv"))
        following = (here + 1) % SLOTS
        prolong(coarse["d"].at[slot], d, here, x, q, coarse["q"])
        local_part(level, here)
        if awaited:
            arrived(coarse["q"], coarse["d"], slot, False)
        lift_faces(coarse["q"], q, slot)

        def put(at, part):
            r[at, :] = r[at, :] + part

        def advance(at):
            value = factor * inv[at, :] * r[at, :]
            d[following, at, :] = value
            x[at, :] = x[at, :] + value

        rims(level, hyl, put)
        for k in range(2):
            put(face_at(k, q, 0, q), slab_term(level, hxl, k, 0, q))
        planes(q, advance)
        send_all(q, d, following, with_corners)
        if awaited:
            sent(coarse["q"], coarse["d"], slot, False)

    def first_update(level, slot, factor, with_corners):
        q, d, x, r, inv = (level[name] for name in ("q", "d", "x", "r", "inv"))

        def body(i, carry):
            at = plane_at(i, q)
            value = inv[at, :] * r[at, :] * factor
            d[slot, at, :] = value
            x[at, :] = value
            return carry

        lax.fori_loop(0, q, body, 0)
        send_all(q, d, slot, with_corners)

    def pick(k, values):
        out = jnp.float32(values[0])
        for n in range(1, len(values)):
            out = jnp.where(k == n, jnp.float32(values[n]), out)
        return out

    def run(level, exchange, factors, last):
        loop = len(factors) if last else len(factors) - 1

        def body(k, carry):
            a, b = pick(k, [f[0] for f in factors]), pick(k, [f[1] for f in factors])
            step(level, lax.rem(exchange + k, SLOTS), a, b, True, True)
            return carry

        lax.fori_loop(0, loop, body, 0)
        slot = (exchange + loop) % SLOTS
        if last:
            step(level, slot, 0.0, 0.0, False, False)
        else:
            step(level, slot, *factors[-1], True, False)

    def restrict(fine, coarse, qf, qc):
        table = lagrange(qf, qc)

        def body(j, carry):
            rows = [tiles(fine[pl.ds(pl.multiple_of(j * (qf * NY) + i * qf * qf * NY, NY), qf * NY), :], qf) for i in range(qf)]
            for a in range(qc):
                along = weighted(table[:, a], rows)
                for e in range(qc):
                    out = weighted(table[:, e], [along[k] for k in range(qf)])
                    work[pl.ds(pl.multiple_of(j * (qc * qc * NY) + (a * qc + e) * NY, NY), NY), :] = out
            return carry

        lax.fori_loop(0, qf, body, 0)

        def gather(a, carry):
            rows = [work[pl.ds(pl.multiple_of(a * (qc * NY) + j * qc * qc * NY, NY), qc * NY), :] for j in range(qf)]
            for b in range(qc):
                at = pl.ds(pl.multiple_of(a * (qc * qc * NY) + b * qc * NY, NY), qc * NY)
                coarse[at, :] = weighted(table[:, b], rows)
            return carry

        lax.fori_loop(0, qc, gather, 0)

    def prolong(coarse, fine, slot, sum_into, qf, qc):
        table = lagrange(qf, qc)

        def spread(a, carry):
            rows = [coarse[pl.ds(pl.multiple_of(a * (qc * qc * NY) + b * qc * NY, NY), qc * NY), :] for b in range(qc)]
            for j in range(qf):
                at = pl.ds(pl.multiple_of(a * (qc * NY) + j * qc * qc * NY, NY), qc * NY)
                work[at, :] = weighted(table[j], rows)
            return carry

        lax.fori_loop(0, qc, spread, 0)

        def body(j, carry):
            along = []
            for a in range(qc):
                at = pl.ds(pl.multiple_of(j * (qc * qc * NY) + a * qc * NY, NY), qc * NY)
                part = tiles(work[at, :], qc)
                along.append([weighted(table[k], [part[e] for e in range(qc)]) for k in range(qf)])
            for i in range(qf):
                for k in range(qf):
                    value = weighted(table[i], [along[a][k] for a in range(qc)])
                    at = pl.ds(pl.multiple_of(j * (qf * NY) + (i * qf * qf + k) * NY, NY), NY)
                    fine[slot, at, :] = value
                    sum_into[at, :] = sum_into[at, :] + value
            return carry

        lax.fori_loop(0, qf, body, 0)

    five = dict(q=Q5, d=d5, t=t5, r=res, x=sol, inv=inv5, product=lambda slot: product_wide(Q5, d5, slot, t5, sh5, sl5))
    three = dict(q=Q3, d=d3, t=t3, r=r3, x=x3, inv=inv3, gx=gx3, gy=gy3, product=lambda slot: product_wide(Q3, d3, slot, t3, sh3, sl3))
    one = dict(q=Q1, d=d1, t=t1, r=r1, x=x1, inv=inv1, gx=gx1, gy=gy1, product=lambda slot: product_small(d1, slot, t1))

    first, pairs = chebyshev_factors(DEGREE, LAMBDA_TOP / 8.0)
    coarse_first, coarse_pairs = chebyshev_factors(COARSE_ITERS, LAMBDA_TOP / 40.0)
    first_update(five, 0, first, False)
    run(five, 0, pairs, True)
    restrict(res, r3, Q5, Q3)
    first_update(three, 3, first, True)
    greeted()
    double_step(three, 3, *pairs, False, False)
    step(three, 5 % SLOTS, 0.0, 0.0, False, False)
    restrict(r3, r1, Q3, Q1)
    first_update(one, 6 % SLOTS, coarse_first, True)

    def coarse_rounds(n, carry):
        factors = [[pick(n, [f[part] for f in coarse_pairs[half:6:2]]) for part in range(2)] for half in range(2)]
        double_step(one, lax.rem(6 + 2 * n, SLOTS), *factors, True, False)
        return carry

    lax.fori_loop(0, 3, coarse_rounds, 0)
    finish_round(one, 12 % SLOTS, *coarse_pairs[6])
    lifted_step(one, 13 % SLOTS, three, 13 % SLOTS, first, False, True)
    double_step(three, 14 % SLOTS, *pairs, False, True)
    lifted_step(three, 16 % SLOTS, five, 16 % SLOTS, first, True, False)
    run(five, 17, pairs, True)


def per_device(right_side, coefficient, bottom_top, stiff_five, stiff_three, stiff_one):
    shape = right_side.shape
    n5, n3, n1 = Q5**3 * NY, Q3**3 * NY, Q1**3 * NY
    vmem = pl.BlockSpec(memory_space=pltpu.VMEM)
    hbm = pl.BlockSpec(memory_space=pltpu.HBM)
    field = lambda n: pltpu.VMEM((n, NZ), F32)
    slots = lambda *n: pltpu.VMEM((SLOTS, *n, NZ), F32)
    two = lambda n: pltpu.VMEM((2, n, NZ), F32)
    dma = pltpu.SemaphoreType.DMA
    sol, res = pl.pallas_call(
        kernel,
        out_shape=[jax.ShapeDtypeStruct((n5, NZ), F32)] * 2,
        in_specs=[hbm] * 6,
        out_specs=[vmem, vmem],
        scratch_shapes=[
            field(NY), pltpu.SMEM((2, NY), jnp.int32), pltpu.VMEM((Q5**3, Q5**3), F32), pltpu.VMEM((Q3**3, Q3**3), F32),
            pltpu.SMEM((Q1**3, Q1**3), F32),
            slots(n5), field(n5), field(n5),
            field(n3), field(n3), slots(n3), field(n3), field(n3),
            field(n1), field(n1), slots(n1), field(n1), field(n1),
            pltpu.VMEM((224, 224), BF16), pltpu.VMEM((224, 224), BF16),
            pltpu.VMEM((64, 64), BF16), pltpu.VMEM((64, 64), BF16),
            field(6 * 16 * NY), pltpu.VMEM((6, NY, NZ), F32),
            slots(2, Q5 * Q5 * NY), slots(2, Q5 * NY), two(Q5 * Q5 * NY), slots(2, Q5 * NY), pltpu.VMEM((4, NY, NZ), F32),
            slots(4, NY), slots(4, NY), two(Q3 * NY),
            two(Q3 * Q3 * NY), two(Q1 * Q1 * NY), two(Q3 * NY), two(Q1 * NY), two(Q3 * NY), two(Q1 * NY),
            pltpu.VMEM((4, 2, NY, NZ), F32), two(Q5 * Q5 * NY), two(Q5 * NY),
            dma((2, 4, SLOTS)), dma((2, 4, SLOTS)), dma((2, SLOTS)), dma((2, SLOTS)), dma((4, SLOTS)), dma((4, SLOTS)),
            dma((4, 3)), dma((4, 3)), dma((4,)), dma((4,)), dma((6,)),
        ],
        compiler_params=pltpu.CompilerParams(
            collective_id=0, has_side_effects=True, vmem_limit_bytes=48 * 2**20
        ),
    )(
        *(
            pltpu.with_memory_space_constraint(value, pltpu.HBM)
            for value in (
                coefficient.reshape(NY, NZ), bottom_top.reshape(2, NY), right_side.reshape(n5, NZ),
                stiff_five, stiff_three, stiff_one,
            )
        )
    )
    return sol.reshape(shape), res.reshape(shape)


def solution(mesh):
    field = P(None, None, None, "slab", "cross", None)
    return jax.shard_map(
        per_device,
        mesh=mesh,
        in_specs=(field, P("slab", "cross", None), P(None, "slab", "cross"), P(), P(), P()),
        out_specs=(field, field),
        check_vma=False,
    )
```

```python
import functools

import jax
import jax.numpy as jnp
import numpy as np
from jax import lax
from jax.experimental import pallas as pl
from jax.experimental.pallas import tpu as pltpu
from jax.sharding import PartitionSpec as P

MESH = pl.DeviceIdType.MESH
F32 = jnp.float32
BF16 = jnp.bfloat16
Q5, Q3, Q1 = 6, 4, 2
DEGREE = 3
COARSE_ITERS = 8
LAMBDA_TOP = 2.2
NY, NZ = 8, 128
SLOTS = 4
PENALTY = {Q5: 3.0, Q3: 2.0, Q1: 1.0}


def lagrange(fine_count, coarse_count):
    fine = np.linspace(-1.0, 1.0, fine_count)
    coarse = np.linspace(-1.0, 1.0, coarse_count)
    table = np.ones((fine_count, coarse_count))
    for c in range(coarse_count):
        for o in range(coarse_count):
            if o != c:
                table[:, c] = table[:, c] * (fine - coarse[o]) / (coarse[c] - coarse[o])
    return table.astype(np.float32)


def chebyshev_factors(steps, lowest):
    center = 0.5 * (LAMBDA_TOP + lowest)
    radius = 0.5 * (LAMBDA_TOP - lowest)
    sigma = center / radius
    rho = 1.0 / sigma
    pairs = []
    for _ in range(steps - 1):
        rho_next = 1.0 / (2.0 * sigma - rho)
        pairs.append((rho_next * rho, 2.0 * rho_next / radius))
        rho = rho_next
    return 1.0 / center, pairs


def weighted(table_row, terms):
    total = None
    for value, term in zip(table_row, terms):
        if value == 0.0:
            continue
        part = term if value == 1.0 else float(value) * term
        total = part if total is None else total + part
    return total


def tiles(value, *lead):
    return value.reshape(*lead, NY, NZ)


class Unslotted:
    def __init__(self, ref):
        self.ref, self.at = ref, self

    def __getitem__(self, index):
        return self.ref.at[index[1:]]


def kernel(
    coef_in, ends_in, rhs_in, s5_in, s3_in, s1_in, sol, res,
    mine, ends, s5, s3, s1,
    d5, t5, inv5, x3, r3, d3, t3, inv3, x1, r1, d1, t1, inv1,
    sh5, sl5, sh3, sl3, work, weights, hx, hy, ytile, pack, hc,
    hd, dpack, dtile, gx3, gx1, gy3, gy1, gp3, gp1, gw, hxl, hyl, hcc, gx5, gy5,
    xs, xr, ys, yr, cs, cr, gs, gr, csem, crsem, load,
):
    slab, cross = lax.axis_index("slab"), lax.axis_index("cross")
    ns, nc = lax.axis_size("slab"), lax.axis_size("cross")
    sides = (
        ("slab", slab - 1, slab > 0),
        ("slab", slab + 1, slab < ns - 1),
        ("cross", cross - 1, cross > 0),
        ("cross", cross + 1, cross < nc - 1),
    )
    corners = [
        ({"slab": slab + 2 * k - 1, "cross": cross + 2 * m - 1}, sides[k][2] & sides[2 + m][2])
        for k in range(2) for m in range(2)
    ]

    for k in range(2):

        @pl.when(jnp.logical_not(sides[k][2]))
        def _(k=k):
            hc[k] = jnp.zeros_like(hc[k])
            gw[k] = jnp.zeros_like(gw[k])
            gx3[k] = jnp.zeros_like(gx3[k])
            gx1[k] = jnp.zeros_like(gx1[k])
            for slot in range(SLOTS):
                hx[slot, k] = jnp.zeros_like(hx[slot, k])

        @pl.when(jnp.logical_not(sides[2 + k][2]))
        def _(k=k):
            hc[2 + k] = jnp.zeros_like(hc[2 + k])
            gw[2 + k] = jnp.zeros_like(gw[2 + k])
            gy3[k] = jnp.zeros_like(gy3[k])
            gy1[k] = jnp.zeros_like(gy1[k])
            for slot in range(SLOTS):
                hy[slot, k] = jnp.zeros_like(hy[slot, k])

    for g in range(4):

        @pl.when(jnp.logical_not(corners[g][1]))
        def _(g=g):
            hcc[g] = jnp.zeros_like(hcc[g])
            for slot in range(SLOTS):
                hd[slot, g] = jnp.zeros_like(hd[slot, g])

    barrier = pltpu.get_barrier_semaphore()
    peers = [({axis: index}, there) for axis, index, there in sides] + corners
    for device, there in peers:

        @pl.when(there)
        def _(device=device):
            pl.semaphore_signal(barrier, inc=1, device_id=device, device_id_type=MESH)

    pairs = ((coef_in, mine.at[0]), (s5_in, s5), (s3_in, s3), (rhs_in, res), (ends_in, ends), (s1_in, s1))
    loads = [pltpu.make_async_copy(src, dst, load.at[n]) for n, (src, dst) in enumerate(pairs)]
    for copy in loads:
        copy.start()
    ytile[...] = jnp.zeros_like(ytile)
    dtile[...] = jnp.zeros_like(dtile)
    for copy in loads:
        copy.wait()

    row = lax.broadcasted_iota(jnp.int32, (NY, NZ), 0)
    lane = lax.broadcasted_iota(jnp.int32, (NY, NZ), 1)
    bottom = jnp.zeros((NY, NZ), F32)
    top = jnp.zeros((NY, NZ), F32)
    for y in range(NY):
        bottom = jnp.where(row == y, ends[0, y].astype(F32), bottom)
        top = jnp.where(row == y, ends[1, y].astype(F32), top)
    mine[1] = jnp.where(lane == 0, bottom, jnp.where(lane == NZ - 1, top, 0.0))

    far = lax.rem(slab, 2)
    near = 1 - far

    def lines(q):
        if q < Q5:
            return [(0, q)]
        return [(0, 1), (q - 1, 1)] + [(j, min(2, q - 1 - j)) for j in range(1, q - 1, 2)]

    def face_at(k, q, first, count):
        return pl.ds(pl.multiple_of(k * ((q**3 - q * q) * NY) + first * q * NY, NY), count * q * NY)

    def slab_copy(k, q, d, slot, piece, arriving):
        first, count = (0, q) if piece is None else lines(q)[piece]
        number = 0 if piece is None else piece
        here = k if arriving else 1 - k
        return pltpu.make_async_remote_copy(
            src_ref=d.at[slot, face_at(k, q, first, count), :],
            dst_ref=hx.at[slot, here, pl.ds(first * q * NY, count * q * NY), :],
            send_sem=xs.at[k, number, slot], recv_sem=xr.at[here, number, slot],
            device_id={"slab": slab + 2 * k - 1}, device_id_type=MESH,
        )

    def cross_copy(k, q, slot, arriving):
        here = k if arriving else k ^ 1
        return pltpu.make_async_remote_copy(
            src_ref=pack.at[slot, k, pl.ds(0, q * NY), :], dst_ref=hy.at[slot, here, pl.ds(0, q * NY), :],
            send_sem=ys.at[k, slot], recv_sem=yr.at[here, slot],
            device_id={"cross": sides[2 + k][1]}, device_id_type=MESH,
        )

    def slab_do(k, method, *args):
        index = slab + 2 * k - 1

        @pl.when((index >= 0) & (index < ns))
        def _():
            getattr(slab_copy(k, *args), method)()

    def cross_do(k, method, *args):
        @pl.when(sides[2 + k][2])
        def _():
            getattr(cross_copy(k, *args), method)()

    def send_near(q, d, slot):
        slab_do(near, "start", q, d, slot, None, False)

    def send_far(q, d, slot, pieces):
        for piece in pieces:
            slab_do(far, "start", q, d, slot, piece, False)

    def send_cross(q, d, slot):
        for i in range(q):
            pack[slot, 0, pl.ds(i * NY, q), :] = d[slot, pl.ds(i * q * q * NY, q, stride=NY), :]
            pack[slot, 1, pl.ds(i * NY, q), :] = d[slot, pl.ds((i * q * q + q * (q - 1)) * NY + NY - 1, q, stride=NY), :]
        for k in range(2):
            cross_do(k, "start", q, slot, False)

    def corner_copy(g, slot, arriving):
        here = g if arriving else 3 - g
        return pltpu.make_async_remote_copy(
            src_ref=dpack.at[slot, g], dst_ref=hd.at[slot, here],
            send_sem=cs.at[g, slot], recv_sem=cr.at[here, slot],
            device_id=corners[g][0], device_id_type=MESH,
        )

    def corner_do(g, method, *args):
        @pl.when(corners[g][1])
        def _():
            getattr(corner_copy(g, *args), method)()

    def send_corners(q, d, slot):
        for g in range(4):
            k, m = g // 2, g % 2
            node = k * (q**3 - q * q) + m * (q * q - q)
            dpack[slot, g, pl.ds(0, q), :] = d[slot, pl.ds(node * NY + m * (NY - 1), q, stride=NY), :]
        for g in range(4):
            corner_do(g, "start", slot, False)

    def send_all(q, d, slot, with_corners):
        if with_corners:
            send_corners(q, d, slot)
        send_cross(q, d, slot)
        send_far(q, d, slot, range(len(lines(q))))
        send_near(q, d, slot)

    def arrived_cross(q, slot):
        for k in range(2):
            cross_do(k, "wait_recv", q, slot, True)

    def arrived_slab(q, d, slot):
        slab_do(near, "wait_recv", q, d, slot, None, True)
        for piece in range(len(lines(q))):
            slab_do(far, "wait_recv", q, d, slot, piece, True)

    def arrived_corners(slot):
        for g in range(4):
            corner_do(g, "wait_recv", slot, True)

    def sent(q, d, slot, with_corners):
        slab_do(near, "wait_send", q, d, slot, None, False)
        for piece in range(len(lines(q))):
            slab_do(far, "wait_send", q, d, slot, piece, False)
        for k in range(2):
            cross_do(k, "wait_send", q, slot, False)
        if with_corners:
            for g in range(4):
                corner_do(g, "wait_send", slot, False)

    def pack_rows(q, source, target):
        for i in range(q):
            target[0, pl.ds(i * NY, q), :] = source[pl.ds(i * q * q * NY, q, stride=NY), :]
            target[1, pl.ds(i * NY, q), :] = source[pl.ds((i * q * q + q * (q - 1)) * NY + NY - 1, q, stride=NY), :]

    pack_rows(Q5, res, pack.at[0])
    pl.semaphore_wait(barrier, sum(there.astype(jnp.int32) for _, there in peers))

    def coef_copy(k, arriving):
        if k < 4:
            here = k if arriving else k ^ 1
            src, dst = mine, hc.at[here]
        else:
            here = k if arriving else 11 - k
            src, dst = mine.at[0], hcc.at[here - 4]
        return pltpu.make_async_remote_copy(
            src_ref=src, dst_ref=dst, send_sem=csem.at[k], recv_sem=crsem.at[here],
            device_id=peers[k][0], device_id_type=MESH,
        )

    for k in (2, 3, 0, 1, 4, 5, 6, 7):

        @pl.when(peers[k][1])
        def _(k=k):
            coef_copy(k, False).start()

    raw = Unslotted(res)
    for k in range(2):
        cross_do(k, "start", Q5, 0, False)
    slab_do(far, "start", Q5, raw, 0, None, False)
    slab_do(near, "start", Q5, raw, 0, None, False)

    def split(table, high, low, count):
        value = table[...]
        high[...] = jnp.zeros_like(high)
        low[...] = jnp.zeros_like(low)
        top = value.astype(BF16)
        high[pl.ds(0, count), pl.ds(0, count)] = top
        low[pl.ds(0, count), pl.ds(0, count)] = (value - top.astype(F32)).astype(BF16)

    split(s5, sh5, sl5, Q5**3)
    split(s3, sh3, sl3, Q3**3)

    def spread_diagonal(table, inv, count):
        value = table[...]
        same = lax.broadcasted_iota(jnp.int32, value.shape, 0) == lax.broadcasted_iota(jnp.int32, value.shape, 1)
        column = jnp.sum(jnp.where(same, value, 0.0), axis=1, keepdims=True)
        wide = jnp.broadcast_to(column, (count, NZ))
        for y in range(NY):
            inv[pl.ds(y, count, stride=NY), :] = wide

    spread_diagonal(s5, inv5, Q5**3)
    spread_diagonal(s3, inv3, Q3**3)
    for n in range(Q1**3):
        inv1[pl.ds(n * NY, NY), :] = jnp.full((NY, NZ), s1[n, n])
    for k in range(2):
        gx5[k] = inv5[face_at(1 - k, Q5, 0, Q5), :]
        for i in range(Q5):
            node = i * Q5 * Q5 + (1 - k) * Q5 * (Q5 - 1)
            gy5[k, pl.ds(i * NY, Q5), :] = inv5[pl.ds(node * NY, Q5, stride=NY), :]

    def coefs_done(ks):
        for k in ks:

            @pl.when(peers[k][1])
            def _(k=k):
                coef_copy(k, True).wait_recv()
                coef_copy(k, False).wait_send()

    coefs_done(range(4))
    c = mine[0]

    def cross_weights(own, below, above):
        before = jnp.where(row == 0, pltpu.roll(below, 1, 0), pltpu.roll(own, 1, 0))
        after = jnp.where(row == NY - 1, pltpu.roll(above, NY - 1, 0), pltpu.roll(own, NY - 1, 0))
        return 0.5 * (own + before), 0.5 * (own + after)

    def end_weights(own, flags):
        low = jnp.where(lane == 0, flags * own, 0.5 * (own + pltpu.roll(own, 1, 1)))
        high = jnp.where(lane == NZ - 1, flags * own, 0.5 * (own + pltpu.roll(own, NZ - 1, 1)))
        return low, high

    weights[0] = 0.5 * (c + hc[0, 0])
    weights[1] = 0.5 * (c + hc[1, 0])
    weights[2], weights[3] = cross_weights(c, hc[2, 0], hc[3, 0])
    weights[4], weights[5] = end_weights(c, mine[1])

    def ends_added(base, q, y_pair, z_pair):
        first = base[0:1] + y_pair[0][None]
        last = base[q - 1 : q] + y_pair[1][None]
        base = jnp.concatenate([first, base[1 : q - 1], last] if q > 2 else [first, last], 0)
        first = base[:, 0:1] + z_pair[0][:, None]
        last = base[:, q - 1 : q] + z_pair[1][:, None]
        return jnp.concatenate([first, base[:, 1 : q - 1], last] if q > 2 else [first, last], 1)

    def slab_weight(i, q):
        return jnp.where(i == 0, PENALTY[q] * weights[0], 0.0) + jnp.where(i == q - 1, PENALTY[q] * weights[1], 0.0)

    def plane_at(i, q):
        return pl.ds(pl.multiple_of(i * (q * q * NY), NY), q * q * NY)

    def invert(q, inv):
        yl, yh, zl, zh = (jnp.broadcast_to(PENALTY[q] * weights[k], (q, NY, NZ)) for k in range(2, 6))

        def body(i, carry):
            at = plane_at(i, q)
            base = tiles(inv[at, :], q, q) * c + slab_weight(i, q)
            base = ends_added(base, q, (yl, yh), (zl, zh))
            inv[at, :] = (1.0 / base).reshape(q * q * NY, NZ)
            return carry

        lax.fori_loop(0, q, body, 0)

    invert(Q3, inv3)
    invert(Q1, inv1)

    pack_rows(Q3, inv3, gp3)
    pack_rows(Q1, inv1, gp1)

    def greet_copy(k, n, arriving):
        here = k if arriving else k ^ 1
        if n == 0:
            src, dst = weights.at[pl.ds(2 if k < 2 else 0, 2)], gw.at[here]
        elif k < 2:
            q, inv, target = ((Q3, inv3, gx3), (Q1, inv1, gx1))[n - 1]
            src, dst = inv.at[pl.ds(k * (q**3 - q * q) * NY, q * q * NY), :], target.at[here]
        else:
            source, target = ((gp3, gy3), (gp1, gy1))[n - 1]
            src, dst = source.at[k - 2], target.at[here - 2]
        return pltpu.make_async_remote_copy(
            src_ref=src, dst_ref=dst, send_sem=gs.at[k, n], recv_sem=gr.at[here, n],
            device_id={sides[k][0]: sides[k][1]}, device_id_type=MESH,
        )

    for k in (2, 3, 0, 1):

        @pl.when(sides[k][2])
        def _(k=k):
            for n in range(3):
                greet_copy(k, n, False).start()

    invert(Q5, inv5)

    def greeted():
        for k in range(4):

            @pl.when(sides[k][2])
            def _(k=k):
                for n in range(3):
                    greet_copy(k, n, True).wait_recv()
                    greet_copy(k, n, False).wait_send()

    def product_wide(q, d, slot, t, high, low):
        count = q**3
        padded = high.shape[0]
        s_high, s_low = high[...], low[...]
        for y in range(0, NY, 2):
            pair = [d[slot, pl.ds(y + h, count, stride=NY), :] for h in range(2)]
            v = jnp.concatenate(pair, 1)
            if padded > count:
                v = jnp.concatenate([v, jnp.zeros((padded - count, 2 * NZ), F32)], 0)
            v_high = v.astype(BF16)
            v_low = (v - v_high.astype(F32)).astype(BF16)
            out = jnp.dot(s_high, v_high, preferred_element_type=F32)
            out += jnp.dot(s_high, v_low, preferred_element_type=F32)
            out += jnp.dot(s_low, v_high, preferred_element_type=F32)
            for h in range(2):
                t[pl.ds(y + h, count, stride=NY), :] = out[:count, h * NZ : (h + 1) * NZ]

    def product_small(d, slot, t):
        count = Q1**3
        parts = [d[slot, pl.ds(n * NY, NY), :] for n in range(count)]
        for m in range(count):
            total = s1[m, 0] * parts[0]
            for n in range(1, count):
                total += s1[m, n] * parts[n]
            t[pl.ds(m * NY, NY), :] = total

    def local_part(level, slot):
        q, d, t, r = (level[name] for name in ("q", "d", "t", "r"))
        p = PENALTY[q]
        level["product"](slot)

        def local(i, carry):
            yl, yh, zl, zh = (p * weights[k] for k in range(2, 6))
            at = plane_at(i, q)
            dv = tiles(d[slot, at, :], q, q)
            lo, hi = dv[0], dv[q - 1]
            y_pair = (
                yl * (lo - jnp.where(row == 0, 0.0, pltpu.roll(hi, 1, 1))),
                yh * (hi - jnp.where(row == NY - 1, 0.0, pltpu.roll(lo, NY - 1, 1))),
            )
            lo, hi = dv[:, 0], dv[:, q - 1]
            z_pair = (
                zl * (lo - jnp.where(lane == 0, 0.0, pltpu.roll(hi, 1, 2))),
                zh * (hi - jnp.where(lane == NZ - 1, 0.0, pltpu.roll(lo, NZ - 1, 2))),
            )
            total = ends_added(tiles(t[at, :], q, q) * c, q, y_pair, z_pair)
            r[at, :] = r[at, :] - total.reshape(q * q * NY, NZ)
            return carry

        lax.fori_loop(0, q, local, 0)
        face = q * q * NY
        for k in range(2):
            at = pl.ds(0 if k == 0 else (q**3) * NY - face, face)
            r[at, :] = r[at, :] - (p * weights[k] * tiles(d[slot, at, :], q * q)).reshape(face, NZ)

    def rims(level, source, put):
        q = level["q"]
        for i in range(q):
            ytile[0, pl.ds(i * q * NY, q, stride=NY), :] = source[0, pl.ds(i * NY, q), :]
            ytile[1, pl.ds(i * q * NY + NY - 1, q, stride=NY), :] = source[1, pl.ds(i * NY, q), :]

        def rim(i, carry):
            for k in range(2):
                at = pl.ds(pl.multiple_of(i * (q * q * NY) + k * q * (q - 1) * NY, NY), q * NY)
                part = PENALTY[q] * weights[2 + k] * tiles(ytile[k, pl.ds(pl.multiple_of(i * (q * NY), NY), q * NY), :], q)
                put(at, part.reshape(q * NY, NZ))
            return carry

        lax.fori_loop(0, q, rim, 0)

    def slab_term(level, source, k, first, count):
        q = level["q"]
        part = PENALTY[q] * weights[k] * tiles(source[k, pl.ds(first * q * NY, count * q * NY), :], count * q)
        return part.reshape(count * q * NY, NZ)

    def step(level, slot, a, b, update, send):
        q, d, r, x, inv = (level[name] for name in ("q", "d", "r", "x", "inv"))
        other = lax.rem(slot + 1, SLOTS)

        def put(at, part):
            r[at, :] = r[at, :] + part

        local_part(level, slot)
        for k in range(2):
            cross_do(k, "wait_recv", q, slot, True)
        rims(level, hy.at[slot], put)

        def advance(at):
            value = a * d[slot, at, :] + b * inv[at, :] * r[at, :]
            d[other, at, :] = value
            x[at, :] = x[at, :] + value

        if update and q > 2:

            def inside(i, carry):
                advance(plane_at(i, q))
                return carry

            lax.fori_loop(1, q - 1, inside, 0)

        def slab_face(k, first, count):
            at = face_at(k, q, first, count)
            put(at, slab_term(level, hx.at[slot], k, first, count))
            if update:
                advance(at)

        slab_do(near, "wait_recv", q, d, slot, None, True)
        slab_face(near, 0, q)
        if send:
            send_near(q, d, other)
        pieces = lines(q)
        groups = [[0, 1]] + [[n] for n in range(2, len(pieces))] if len(pieces) > 1 else [[0]]
        for number, group in enumerate(groups):
            for piece in group:
                slab_do(far, "wait_recv", q, d, slot, piece, True)
                slab_face(far, *pieces[piece])
            if send:
                if number == 0:
                    send_cross(q, d, other)
                send_far(q, d, other, group)
        sent(q, d, slot, False)

    def correct(level, slot, b, slab_put, cross_put):
        q, d, gx, gy = (level[name] for name in ("q", "d", "gx", "gy"))
        p = PENALTY[q]
        face = q * q * NY
        for k in range(2):
            for m in range(2):
                dtile[m, pl.ds(m * (NY - 1), q, stride=NY), :] = hd[slot, 2 * k + m, pl.ds(0, q), :]
            term = p * weights[k] * tiles(d[slot, pl.ds(k * (q**3 - q * q) * NY, face), :], q, q)
            low, high = (p * gw[k, m] * tiles(dtile[m, pl.ds(0, q * NY), :], q) for m in range(2))
            first, last = term[0:1] + low[None], term[q - 1 : q] + high[None]
            term = jnp.concatenate([first, term[1 : q - 1], last] if q > 2 else [first, last], 0)
            at = pl.ds(0, face)
            slab_put(k, at, b * gx[k, at, :] * term.reshape(face, NZ))
        for m in range(2):
            mine, theirs = pl.ds(m * (NY - 1), 1), pl.ds((1 - m) * (NY - 1), 1)
            for i in range(q):
                at = pl.ds(i * NY, q)
                term = p * weights[2 + m, mine, :] * pack[slot, m, at, :]
                for k in range(2):
                    if i == k * (q - 1):
                        term = term + p * gw[2 + m, k, theirs, :] * hd[slot, 2 * k + m, pl.ds(0, q), :]
                cross_put(m, at, b * gy[m, at, :] * term)

    def planes(q, body):
        def one_plane(i, carry):
            body(plane_at(i, q))
            return carry

        lax.fori_loop(0, q, one_plane, 0)

    def half_round(level, slot, a, b, total):
        q, d, r, x, inv = (level[name] for name in ("q", "d", "r", "x", "inv"))
        other = lax.rem(slot + 1, SLOTS)

        def partial_next(at):
            value = a * d[slot, at, :] + b * inv[at, :] * r[at, :]
            d[other, at, :] = x[at, :] + value if total else value

        def put_both(at, part):
            r[at, :] = r[at, :] + part
            d[other, at, :] = d[other, at, :] + b * inv[at, :] * part

        local_part(level, slot)
        planes(q, partial_next)
        send_all(q, d, other, False)
        arrived_cross(q, slot)
        sent(q, d, other, False)
        rims(level, hy.at[slot], put_both)
        arrived_slab(q, d, slot)
        for k in range(2):
            put_both(face_at(k, q, 0, q), slab_term(level, hx.at[slot], k, 0, q))

    def double_step(level, slot, first, second, with_corners, total):
        q, d, r, x, inv = (level[name] for name in ("q", "d", "r", "x", "inv"))
        other, third = lax.rem(slot + 1, SLOTS), lax.rem(slot + 2, SLOTS)

        def put(at, part):
            r[at, :] = r[at, :] + part

        def add(at):
            x[at, :] = x[at, :] + d[other, at, :]

        def advance(at):
            value = second[0] * d[other, at, :] + second[1] * inv[at, :] * r[at, :]
            if total:
                d[third, at, :] = x[at, :] + value
            else:
                d[third, at, :] = value
                x[at, :] = x[at, :] + value

        half_round(level, slot, *first, False)
        planes(q, add)
        local_part(level, other)
        arrived_corners(slot)

        def keep_slab(k, at, part):
            hxl[k, at, :] = part

        def keep_cross(m, at, part):
            hyl[m, at, :] = part

        correct(level, slot, first[1], keep_slab, keep_cross)
        rims(level, hyl, put)
        for k in range(2):
            put(face_at(k, q, 0, q), slab_term(level, hxl, k, 0, q))
        arrived_cross(q, other)
        rims(level, hy.at[other], put)
        arrived_slab(q, d, other)
        for k in range(2):
            put(face_at(k, q, 0, q), slab_term(level, hx.at[other], k, 0, q))
        planes(q, advance)
        send_all(q, d, third, with_corners)
        sent(q, d, slot, True)

    def finish_round(level, slot, a, b):
        q, d = level["q"], level["d"]
        other = lax.rem(slot + 1, SLOTS)
        half_round(level, slot, a, b, True)
        arrived_corners(slot)
        arrived_cross(q, other)
        arrived_slab(q, d, other)

        def add_slab(k, at, part):
            hx[other, k, at, :] = hx[other, k, at, :] + part

        def add_cross(m, at, part):
            hy[other, m, at, :] = hy[other, m, at, :] + part

        correct(level, slot, b, add_slab, add_cross)
        sent(q, d, slot, True)

    def lift_slab(qc, qf, slot):
        table = lagrange(qf, qc)
        for k in range(2):
            lines_in = tiles(hx[slot, k, pl.ds(0, qc * qc * NY), :], qc, qc)
            for j in range(qf):
                line = weighted(table[j], [lines_in[n] for n in range(qc)])
                for n in range(qf):
                    hxl[k, pl.ds((j * qf + n) * NY, NY), :] = weighted(table[n], [line[e] for e in range(qc)])

    def lift_cross(qc, qf, slot):
        table = lagrange(qf, qc)
        spread = []
        for e in range(qc):
            column = jnp.zeros((NY, NZ), F32)
            for n in range(qf):
                if table[n, e] != 0.0:
                    column = jnp.where(row == n, float(table[n, e]), column)
            spread.append(column)
        for k in range(2):
            for i in range(qf):
                line = weighted(table[i], [hy[slot, k, pl.ds(a * NY, qc), :] for a in range(qc)])
                value = spread[0] * line[0:1]
                for e in range(1, qc):
                    value = value + spread[e] * line[e : e + 1]
                hyl[k, pl.ds(i * NY, NY), :] = value

    def lifted_step(coarse, slot, level, here, factor, awaited, with_corners):
        q, d, r, x, inv = (level[name] for name in ("q", "d", "r", "x", "inv"))
        following = (here + 1) % SLOTS
        prolong(coarse["d"].at[slot], d, here, x, q, coarse["q"])
        local_part(level, here)

        def put(at, part):
            r[at, :] = r[at, :] + part

        def advance(at):
            value = factor * inv[at, :] * r[at, :]
            d[following, at, :] = value
            x[at, :] = x[at, :] + value

        if awaited:
            arrived_cross(coarse["q"], slot)
        lift_cross(coarse["q"], q, slot)
        rims(level, hyl, put)

        def inside(i, carry):
            advance(plane_at(i, q))
            return carry

        lax.fori_loop(1, q - 1, inside, 0)
        if awaited:
            arrived_slab(coarse["q"], coarse["d"], slot)
        lift_slab(coarse["q"], q, slot)
        for k in range(2):
            at = face_at(k, q, 0, q)
            put(at, slab_term(level, hxl, k, 0, q))
            advance(at)
        send_all(q, d, following, with_corners)
        if awaited:
            sent(coarse["q"], coarse["d"], slot, False)

    def first_update(level, slot, factor, with_corners):
        q, d, x, r, inv = (level[name] for name in ("q", "d", "x", "r", "inv"))

        def body(i, carry):
            at = plane_at(i, q)
            value = inv[at, :] * r[at, :] * factor
            d[slot, at, :] = value
            x[at, :] = value
            return carry

        lax.fori_loop(0, q, body, 0)
        send_all(q, d, slot, with_corners)

    def opening_step(level, factor, a, b):
        q, d, r, x, inv = (level[name] for name in ("q", "d", "r", "x", "inv"))
        p = PENALTY[q]

        def start(at):
            value = inv[at, :] * r[at, :] * factor
            d[0, at, :] = value
            x[at, :] = value

        def put(at, part):
            r[at, :] = r[at, :] + part

        def advance(at):
            value = a * d[0, at, :] + b * inv[at, :] * r[at, :]
            d[1, at, :] = value
            x[at, :] = x[at, :] + value

        planes(q, start)
        slab_do(far, "wait_send", q, raw, 0, None, False)
        slab_do(near, "wait_send", q, raw, 0, None, False)
        local_part(level, 0)
        coefs_done(range(4, 8))
        for k in range(2):
            own = hc[k, 0]
            y_pair = cross_weights(own, hcc[2 * k], hcc[2 * k + 1])
            z_pair = end_weights(own, hc[k, 1])
            y_pair, z_pair = ([jnp.broadcast_to(p * w, (q, NY, NZ)) for w in pair] for pair in (y_pair, z_pair))
            base = ends_added(tiles(gx5[k], q, q) * own + p * weights[k], q, y_pair, z_pair)
            gx5[k] = (1.0 / base).reshape(q * q * NY, NZ)
        node = lax.broadcasted_iota(jnp.int32, (q, NZ), 0)
        for m in range(2):
            here, theirs = m * (NY - 1), (1 - m) * (NY - 1)
            low, high = (w[theirs : theirs + 1] for w in end_weights(hc[2 + m, 0], hc[2 + m, 1]))
            own = hc[2 + m, 0, pl.ds(theirs, 1), :]
            across = p * weights[2 + m, pl.ds(here, 1), :]
            along = p * (jnp.where(node == 0, low, 0.0) + jnp.where(node == q - 1, high, 0.0))
            for i in range(q):
                at = pl.ds(i * NY, q)
                base = gy5[m, at, :] * own + across + along
                for k in range(2):
                    if i == k * (q - 1):
                        base = base + p * (0.5 * (own + hcc[2 * k + m, pl.ds(theirs, 1), :]))
                gy5[m, at, :] = 1.0 / base
        for k in range(2):
            cross_do(k, "wait_recv", q, 0, True)
        for m in range(2):
            for i in range(q):
                at = pl.ds(i * NY, q)
                hy[0, m, at, :] = gy5[m, at, :] * hy[0, m, at, :] * factor
        rims(level, hy.at[0], put)

        def inside(i, carry):
            advance(plane_at(i, q))
            return carry

        lax.fori_loop(1, q - 1, inside, 0)
        for k in (near, far):
            slab_do(k, "wait_recv", q, raw, 0, None, True)
            hx[0, k] = gx5[k] * hx[0, k] * factor
            at = face_at(k, q, 0, q)
            put(at, slab_term(level, hx.at[0], k, 0, q))
            advance(at)
        send_all(q, d, 1, False)
        for k in range(2):
            cross_do(k, "wait_send", q, 0, False)

    def pick(k, values):
        out = jnp.float32(values[0])
        for n in range(1, len(values)):
            out = jnp.where(k == n, jnp.float32(values[n]), out)
        return out

    def run(level, exchange, factors, last):
        loop = len(factors) if last else len(factors) - 1

        def body(k, carry):
            a, b = pick(k, [f[0] for f in factors]), pick(k, [f[1] for f in factors])
            step(level, lax.rem(exchange + k, SLOTS), a, b, True, True)
            return carry

        lax.fori_loop(0, loop, body, 0)
        slot = (exchange + loop) % SLOTS
        if last:
            step(level, slot, 0.0, 0.0, False, False)
        else:
            step(level, slot, *factors[-1], True, False)

    def restrict(fine, coarse, qf, qc):
        table = lagrange(qf, qc)

        def body(j, carry):
            rows = [tiles(fine[pl.ds(pl.multiple_of(j * (qf * NY) + i * qf * qf * NY, NY), qf * NY), :], qf) for i in range(qf)]
            for a in range(qc):
                along = weighted(table[:, a], rows)
                for e in range(qc):
                    out = weighted(table[:, e], [along[k] for k in range(qf)])
                    work[pl.ds(pl.multiple_of(j * (qc * qc * NY) + (a * qc + e) * NY, NY), NY), :] = out
            return carry

        lax.fori_loop(0, qf, body, 0)

        def gather(a, carry):
            rows = [work[pl.ds(pl.multiple_of(a * (qc * NY) + j * qc * qc * NY, NY), qc * NY), :] for j in range(qf)]
            for b in range(qc):
                at = pl.ds(pl.multiple_of(a * (qc * qc * NY) + b * qc * NY, NY), qc * NY)
                coarse[at, :] = weighted(table[:, b], rows)
            return carry

        lax.fori_loop(0, qc, gather, 0)

    def prolong(coarse, fine, slot, sum_into, qf, qc):
        table = lagrange(qf, qc)

        def spread(a, carry):
            rows = [coarse[pl.ds(pl.multiple_of(a * (qc * qc * NY) + b * qc * NY, NY), qc * NY), :] for b in range(qc)]
            for j in range(qf):
                at = pl.ds(pl.multiple_of(a * (qc * NY) + j * qc * qc * NY, NY), qc * NY)
                work[at, :] = weighted(table[j], rows)
            return carry

        lax.fori_loop(0, qc, spread, 0)

        def body(j, carry):
            along = []
            for a in range(qc):
                at = pl.ds(pl.multiple_of(j * (qc * qc * NY) + a * qc * NY, NY), qc * NY)
                part = tiles(work[at, :], qc)
                along.append([weighted(table[k], [part[e] for e in range(qc)]) for k in range(qf)])
            for i in range(qf):
                for k in range(qf):
                    value = weighted(table[i], [along[a][k] for a in range(qc)])
                    at = pl.ds(pl.multiple_of(j * (qf * NY) + (i * qf * qf + k) * NY, NY), NY)
                    fine[slot, at, :] = value
                    sum_into[at, :] = sum_into[at, :] + value
            return carry

        lax.fori_loop(0, qf, body, 0)

    five = dict(q=Q5, d=d5, t=t5, r=res, x=sol, inv=inv5, product=lambda slot: product_wide(Q5, d5, slot, t5, sh5, sl5))
    three = dict(q=Q3, d=d3, t=t3, r=r3, x=x3, inv=inv3, gx=gx3, gy=gy3, product=lambda slot: product_wide(Q3, d3, slot, t3, sh3, sl3))
    one = dict(q=Q1, d=d1, t=t1, r=r1, x=x1, inv=inv1, gx=gx1, gy=gy1, product=lambda slot: product_small(d1, slot, t1))

    first, pairs = chebyshev_factors(DEGREE, LAMBDA_TOP / 8.0)
    coarse_first, coarse_pairs = chebyshev_factors(COARSE_ITERS, LAMBDA_TOP / 40.0)
    opening_step(five, first, *pairs[0])
    run(five, 1, pairs[1:], True)
    restrict(res, r3, Q5, Q3)
    first_update(three, 3, first, True)
    greeted()
    double_step(three, 3, *pairs, False, False)
    step(three, 5 % SLOTS, 0.0, 0.0, False, False)
    restrict(r3, r1, Q3, Q1)
    first_update(one, 6 % SLOTS, coarse_first, True)

    def coarse_rounds(n, carry):
        factors = [[pick(n, [f[part] for f in coarse_pairs[half:6:2]]) for part in range(2)] for half in range(2)]
        double_step(one, lax.rem(6 + 2 * n, SLOTS), *factors, True, False)
        return carry

    lax.fori_loop(0, 3, coarse_rounds, 0)
    finish_round(one, 12 % SLOTS, *coarse_pairs[6])
    lifted_step(one, 13 % SLOTS, three, 13 % SLOTS, first, False, True)
    double_step(three, 14 % SLOTS, *pairs, False, True)
    lifted_step(three, 16 % SLOTS, five, 16 % SLOTS, first, True, False)
    run(five, 17, pairs, True)


def hand_out(sol, res, sol_out, res_out, done):
    rows = Q5**3 * NY // 4
    copies = [
        pltpu.make_async_copy(src.at[pl.ds(n * rows, rows), :], dst.at[pl.ds(n * rows, rows), :], done.at[k, n])
        for k, (src, dst) in enumerate(((sol, sol_out), (res, res_out))) for n in range(4)
    ]
    for copy in copies:
        copy.start()
    for copy in copies:
        copy.wait()


def per_device(right_side, coefficient, bottom_top, stiff_five, stiff_three, stiff_one):
    shape = right_side.shape
    n5, n3, n1 = Q5**3 * NY, Q3**3 * NY, Q1**3 * NY
    vmem = pl.BlockSpec(memory_space=pltpu.VMEM)
    hbm = pl.BlockSpec(memory_space=pltpu.HBM)
    field = lambda n: pltpu.VMEM((n, NZ), F32)
    slots = lambda *n: pltpu.VMEM((SLOTS, *n, NZ), F32)
    two = lambda n: pltpu.VMEM((2, n, NZ), F32)
    dma = pltpu.SemaphoreType.DMA
    sol, res = pl.pallas_call(
        kernel,
        out_shape=[jax.ShapeDtypeStruct((n5, NZ), F32)] * 2,
        in_specs=[hbm] * 6,
        out_specs=[vmem, vmem],
        scratch_shapes=[
            two(NY), pltpu.SMEM((2, NY), jnp.int32), pltpu.VMEM((Q5**3, Q5**3), F32), pltpu.VMEM((Q3**3, Q3**3), F32),
            pltpu.SMEM((Q1**3, Q1**3), F32),
            slots(n5), field(n5), field(n5),
            field(n3), field(n3), slots(n3), field(n3), field(n3),
            field(n1), field(n1), slots(n1), field(n1), field(n1),
            pltpu.VMEM((224, 224), BF16), pltpu.VMEM((224, 224), BF16),
            pltpu.VMEM((64, 64), BF16), pltpu.VMEM((64, 64), BF16),
            field(6 * 16 * NY), pltpu.VMEM((6, NY, NZ), F32),
            slots(2, Q5 * Q5 * NY), slots(2, Q5 * NY), two(Q5 * Q5 * NY), slots(2, Q5 * NY), pltpu.VMEM((4, 2, NY, NZ), F32),
            slots(4, NY), slots(4, NY), two(Q3 * NY),
            two(Q3 * Q3 * NY), two(Q1 * Q1 * NY), two(Q3 * NY), two(Q1 * NY), two(Q3 * NY), two(Q1 * NY),
            pltpu.VMEM((4, 2, NY, NZ), F32), two(Q5 * Q5 * NY), two(Q5 * NY),
            pltpu.VMEM((4, NY, NZ), F32), two(Q5 * Q5 * NY), two(Q5 * NY),
            dma((2, 4, SLOTS)), dma((2, 4, SLOTS)), dma((2, SLOTS)), dma((2, SLOTS)), dma((4, SLOTS)), dma((4, SLOTS)),
            dma((4, 3)), dma((4, 3)), dma((8,)), dma((8,)), dma((6,)),
        ],
        compiler_params=pltpu.CompilerParams(
            collective_id=0, has_side_effects=True, vmem_limit_bytes=48 * 2**20
        ),
    )(
        *(
            pltpu.with_memory_space_constraint(value, pltpu.HBM)
            for value in (
                coefficient.reshape(NY, NZ), bottom_top.reshape(2, NY), right_side.reshape(n5, NZ),
                stiff_five, stiff_three, stiff_one,
            )
        )
    )
    sol, res = pl.pallas_call(
        hand_out,
        out_shape=[jax.ShapeDtypeStruct((n5, NZ), F32)] * 2,
        in_specs=[vmem] * 2,
        out_specs=[hbm, hbm],
        scratch_shapes=[dma((2, 4))],
    )(*(pltpu.with_memory_space_constraint(value, pltpu.VMEM) for value in (sol, res)))
    return sol.reshape(shape), res.reshape(shape)


def solution(mesh):
    field = P(None, None, None, "slab", "cross", None)
    return jax.shard_map(
        per_device,
        mesh=mesh,
        in_specs=(field, P("slab", "cross", None), P(None, "slab", "cross"), P(), P(), P()),
        out_specs=(field, field),
        check_vma=False,
    )
```

```python
import functools

import jax
import jax.numpy as jnp
import numpy as np
from jax import lax
from jax.experimental import pallas as pl
from jax.experimental.pallas import tpu as pltpu
from jax.sharding import PartitionSpec as P

MESH = pl.DeviceIdType.MESH
F32 = jnp.float32
BF16 = jnp.bfloat16
Q5, Q3, Q1 = 6, 4, 2
DEGREE = 3
COARSE_ITERS = 8
LAMBDA_TOP = 2.2
NY, NZ = 8, 128
SLOTS = 4
PENALTY = {Q5: 3.0, Q3: 2.0, Q1: 1.0}


def lagrange(fine_count, coarse_count):
    fine = np.linspace(-1.0, 1.0, fine_count)
    coarse = np.linspace(-1.0, 1.0, coarse_count)
    table = np.ones((fine_count, coarse_count))
    for c in range(coarse_count):
        for o in range(coarse_count):
            if o != c:
                table[:, c] = table[:, c] * (fine - coarse[o]) / (coarse[c] - coarse[o])
    return table.astype(np.float32)


def chebyshev_factors(steps, lowest):
    center = 0.5 * (LAMBDA_TOP + lowest)
    radius = 0.5 * (LAMBDA_TOP - lowest)
    sigma = center / radius
    rho = 1.0 / sigma
    pairs = []
    for _ in range(steps - 1):
        rho_next = 1.0 / (2.0 * sigma - rho)
        pairs.append((rho_next * rho, 2.0 * rho_next / radius))
        rho = rho_next
    return 1.0 / center, pairs


def weighted(table_row, terms):
    total = None
    for value, term in zip(table_row, terms):
        if value == 0.0:
            continue
        part = term if value == 1.0 else float(value) * term
        total = part if total is None else total + part
    return total


def tiles(value, *lead):
    return value.reshape(*lead, NY, NZ)


class Unslotted:
    def __init__(self, ref):
        self.ref, self.at = ref, self

    def __getitem__(self, index):
        return self.ref.at[index[1:]]


def kernel(
    coef_in, ends_in, rhs_in, s5_in, s3_in, s1_in, sol, res,
    mine, ends, s5, s3, s1,
    d5, t5, inv5, x3, r3, d3, t3, inv3, x1, r1, d1, t1, inv1,
    sh5, sl5, sh3, sl3, work, weights, hx, hy, ytile, pack, hc,
    hd, dpack, dtile, gx3, gx1, gy3, gy1, gp3, gp1, gw, hxl, hyl, hcc, gx5, gy5,
    xs, xr, ys, yr, cs, cr, gs, gr, csem, crsem, load,
):
    slab, cross = lax.axis_index("slab"), lax.axis_index("cross")
    ns, nc = lax.axis_size("slab"), lax.axis_size("cross")
    sides = (
        ("slab", slab - 1, slab > 0),
        ("slab", slab + 1, slab < ns - 1),
        ("cross", cross - 1, cross > 0),
        ("cross", cross + 1, cross < nc - 1),
    )
    corners = [
        ({"slab": slab + 2 * k - 1, "cross": cross + 2 * m - 1}, sides[k][2] & sides[2 + m][2])
        for k in range(2) for m in range(2)
    ]

    for k in range(2):

        @pl.when(jnp.logical_not(sides[k][2]))
        def _(k=k):
            hc[k] = jnp.zeros_like(hc[k])
            gw[k] = jnp.zeros_like(gw[k])
            gx3[k] = jnp.zeros_like(gx3[k])
            gx1[k] = jnp.zeros_like(gx1[k])
            for slot in range(SLOTS):
                hx[slot, k] = jnp.zeros_like(hx[slot, k])

        @pl.when(jnp.logical_not(sides[2 + k][2]))
        def _(k=k):
            hc[2 + k] = jnp.zeros_like(hc[2 + k])
            gw[2 + k] = jnp.zeros_like(gw[2 + k])
            gy3[k] = jnp.zeros_like(gy3[k])
            gy1[k] = jnp.zeros_like(gy1[k])
            for slot in range(SLOTS):
                hy[slot, k] = jnp.zeros_like(hy[slot, k])

    for g in range(4):

        @pl.when(jnp.logical_not(corners[g][1]))
        def _(g=g):
            hcc[g] = jnp.zeros_like(hcc[g])
            for slot in range(SLOTS):
                hd[slot, g] = jnp.zeros_like(hd[slot, g])

    barrier = pltpu.get_barrier_semaphore()
    peers = [({axis: index}, there) for axis, index, there in sides] + corners
    for device, there in peers:

        @pl.when(there)
        def _(device=device):
            pl.semaphore_signal(barrier, inc=1, device_id=device, device_id_type=MESH)

    pairs = ((coef_in, mine.at[0]), (s5_in, s5), (s3_in, s3), (rhs_in, res), (ends_in, ends), (s1_in, s1))
    loads = [pltpu.make_async_copy(src, dst, load.at[n]) for n, (src, dst) in enumerate(pairs)]
    for copy in loads:
        copy.start()
    ytile[...] = jnp.zeros_like(ytile)
    dtile[...] = jnp.zeros_like(dtile)
    for copy in loads:
        copy.wait()

    row = lax.broadcasted_iota(jnp.int32, (NY, NZ), 0)
    lane = lax.broadcasted_iota(jnp.int32, (NY, NZ), 1)
    bottom = jnp.zeros((NY, NZ), F32)
    top = jnp.zeros((NY, NZ), F32)
    for y in range(NY):
        bottom = jnp.where(row == y, ends[0, y].astype(F32), bottom)
        top = jnp.where(row == y, ends[1, y].astype(F32), top)
    mine[1] = jnp.where(lane == 0, bottom, jnp.where(lane == NZ - 1, top, 0.0))

    far = lax.rem(slab, 2)
    near = 1 - far

    def lines(q):
        if q < Q5:
            return [(0, q)]
        return [(0, 1), (q - 1, 1)] + [(j, min(2, q - 1 - j)) for j in range(1, q - 1, 2)]

    def face_at(k, q, first, count):
        return pl.ds(pl.multiple_of(k * ((q**3 - q * q) * NY) + first * q * NY, NY), count * q * NY)

    def slab_copy(k, q, d, slot, piece, arriving):
        first, count = (0, q) if piece is None else lines(q)[piece]
        number = 0 if piece is None else piece
        here = k if arriving else 1 - k
        return pltpu.make_async_remote_copy(
            src_ref=d.at[slot, face_at(k, q, first, count), :],
            dst_ref=hx.at[slot, here, pl.ds(first * q * NY, count * q * NY), :],
            send_sem=xs.at[k, number, slot], recv_sem=xr.at[here, number, slot],
            device_id={"slab": slab + 2 * k - 1}, device_id_type=MESH,
        )

    def cross_copy(k, q, slot, arriving):
        here = k if arriving else k ^ 1
        return pltpu.make_async_remote_copy(
            src_ref=pack.at[slot, k, pl.ds(0, q * NY), :], dst_ref=hy.at[slot, here, pl.ds(0, q * NY), :],
            send_sem=ys.at[k, slot], recv_sem=yr.at[here, slot],
            device_id={"cross": sides[2 + k][1]}, device_id_type=MESH,
        )

    def slab_do(k, method, *args):
        index = slab + 2 * k - 1

        @pl.when((index >= 0) & (index < ns))
        def _():
            getattr(slab_copy(k, *args), method)()

    def cross_do(k, method, *args):
        @pl.when(sides[2 + k][2])
        def _():
            getattr(cross_copy(k, *args), method)()

    def send_near(q, d, slot):
        slab_do(near, "start", q, d, slot, None, False)

    def send_far(q, d, slot, pieces):
        for piece in pieces:
            slab_do(far, "start", q, d, slot, piece, False)

    def send_cross(q, d, slot):
        for i in range(q):
            pack[slot, 0, pl.ds(i * NY, q), :] = d[slot, pl.ds(i * q * q * NY, q, stride=NY), :]
            pack[slot, 1, pl.ds(i * NY, q), :] = d[slot, pl.ds((i * q * q + q * (q - 1)) * NY + NY - 1, q, stride=NY), :]
        for k in range(2):
            cross_do(k, "start", q, slot, False)

    def corner_copy(g, slot, arriving):
        here = g if arriving else 3 - g
        return pltpu.make_async_remote_copy(
            src_ref=dpack.at[slot, g], dst_ref=hd.at[slot, here],
            send_sem=cs.at[g, slot], recv_sem=cr.at[here, slot],
            device_id=corners[g][0], device_id_type=MESH,
        )

    def corner_do(g, method, *args):
        @pl.when(corners[g][1])
        def _():
            getattr(corner_copy(g, *args), method)()

    def send_corners(q, d, slot):
        for g in range(4):
            k, m = g // 2, g % 2
            node = k * (q**3 - q * q) + m * (q * q - q)
            dpack[slot, g, pl.ds(0, q), :] = d[slot, pl.ds(node * NY + m * (NY - 1), q, stride=NY), :]
        for g in range(4):
            corner_do(g, "start", slot, False)

    def send_all(q, d, slot, with_corners):
        if with_corners:
            send_corners(q, d, slot)
        send_cross(q, d, slot)
        send_far(q, d, slot, range(len(lines(q))))
        send_near(q, d, slot)

    def arrived_cross(q, slot):
        for k in range(2):
            cross_do(k, "wait_recv", q, slot, True)

    def arrived_slab(q, d, slot):
        slab_do(near, "wait_recv", q, d, slot, None, True)
        for piece in range(len(lines(q))):
            slab_do(far, "wait_recv", q, d, slot, piece, True)

    def arrived_corners(slot):
        for g in range(4):
            corner_do(g, "wait_recv", slot, True)

    def sent(q, d, slot, with_corners):
        slab_do(near, "wait_send", q, d, slot, None, False)
        for piece in range(len(lines(q))):
            slab_do(far, "wait_send", q, d, slot, piece, False)
        for k in range(2):
            cross_do(k, "wait_send", q, slot, False)
        if with_corners:
            for g in range(4):
                corner_do(g, "wait_send", slot, False)

    def pack_rows(q, source, target):
        for i in range(q):
            target[0, pl.ds(i * NY, q), :] = source[pl.ds(i * q * q * NY, q, stride=NY), :]
            target[1, pl.ds(i * NY, q), :] = source[pl.ds((i * q * q + q * (q - 1)) * NY + NY - 1, q, stride=NY), :]

    pack_rows(Q5, res, pack.at[0])
    pl.semaphore_wait(barrier, sum(there.astype(jnp.int32) for _, there in peers))

    def coef_copy(k, arriving):
        if k < 4:
            here = k if arriving else k ^ 1
            src, dst = mine, hc.at[here]
        else:
            here = k if arriving else 11 - k
            src, dst = mine.at[0], hcc.at[here - 4]
        return pltpu.make_async_remote_copy(
            src_ref=src, dst_ref=dst, send_sem=csem.at[k], recv_sem=crsem.at[here],
            device_id=peers[k][0], device_id_type=MESH,
        )

    for k in (2, 3, 0, 1, 4, 5, 6, 7):

        @pl.when(peers[k][1])
        def _(k=k):
            coef_copy(k, False).start()

    raw = Unslotted(res)
    for k in range(2):
        cross_do(k, "start", Q5, 0, False)
    slab_do(far, "start", Q5, raw, 0, None, False)
    slab_do(near, "start", Q5, raw, 0, None, False)

    def split(table, high, low, count):
        value = table[...]
        high[...] = jnp.zeros_like(high)
        low[...] = jnp.zeros_like(low)
        top = value.astype(BF16)
        high[pl.ds(0, count), pl.ds(0, count)] = top
        low[pl.ds(0, count), pl.ds(0, count)] = (value - top.astype(F32)).astype(BF16)

    split(s5, sh5, sl5, Q5**3)
    split(s3, sh3, sl3, Q3**3)

    def spread_diagonal(table, inv, count):
        value = table[...]
        same = lax.broadcasted_iota(jnp.int32, value.shape, 0) == lax.broadcasted_iota(jnp.int32, value.shape, 1)
        column = jnp.sum(jnp.where(same, value, 0.0), axis=1, keepdims=True)
        wide = jnp.broadcast_to(column, (count, NZ))
        for y in range(NY):
            inv[pl.ds(y, count, stride=NY), :] = wide

    spread_diagonal(s5, inv5, Q5**3)
    spread_diagonal(s3, inv3, Q3**3)
    for n in range(Q1**3):
        inv1[pl.ds(n * NY, NY), :] = jnp.full((NY, NZ), s1[n, n])
    for k in range(2):
        gx5[k] = inv5[face_at(1 - k, Q5, 0, Q5), :]
        for i in range(Q5):
            node = i * Q5 * Q5 + (1 - k) * Q5 * (Q5 - 1)
            gy5[k, pl.ds(i * NY, Q5), :] = inv5[pl.ds(node * NY, Q5, stride=NY), :]

    def coefs_done(ks):
        for k in ks:

            @pl.when(peers[k][1])
            def _(k=k):
                coef_copy(k, True).wait_recv()
                coef_copy(k, False).wait_send()

    coefs_done(range(4))
    c = mine[0]

    def cross_weights(own, below, above):
        before = jnp.where(row == 0, pltpu.roll(below, 1, 0), pltpu.roll(own, 1, 0))
        after = jnp.where(row == NY - 1, pltpu.roll(above, NY - 1, 0), pltpu.roll(own, NY - 1, 0))
        return 0.5 * (own + before), 0.5 * (own + after)

    def end_weights(own, flags):
        low = jnp.where(lane == 0, flags * own, 0.5 * (own + pltpu.roll(own, 1, 1)))
        high = jnp.where(lane == NZ - 1, flags * own, 0.5 * (own + pltpu.roll(own, NZ - 1, 1)))
        return low, high

    weights[0] = 0.5 * (c + hc[0, 0])
    weights[1] = 0.5 * (c + hc[1, 0])
    weights[2], weights[3] = cross_weights(c, hc[2, 0], hc[3, 0])
    weights[4], weights[5] = end_weights(c, mine[1])

    def ends_added(base, q, y_pair, z_pair):
        first = base[0:1] + y_pair[0][None]
        last = base[q - 1 : q] + y_pair[1][None]
        base = jnp.concatenate([first, base[1 : q - 1], last] if q > 2 else [first, last], 0)
        first = base[:, 0:1] + z_pair[0][:, None]
        last = base[:, q - 1 : q] + z_pair[1][:, None]
        return jnp.concatenate([first, base[:, 1 : q - 1], last] if q > 2 else [first, last], 1)

    def slab_weight(i, q):
        return jnp.where(i == 0, PENALTY[q] * weights[0], 0.0) + jnp.where(i == q - 1, PENALTY[q] * weights[1], 0.0)

    def plane_at(i, q):
        return pl.ds(pl.multiple_of(i * (q * q * NY), NY), q * q * NY)

    def invert(q, inv):
        yl, yh, zl, zh = (jnp.broadcast_to(PENALTY[q] * weights[k], (q, NY, NZ)) for k in range(2, 6))

        def body(i, carry):
            at = plane_at(i, q)
            base = tiles(inv[at, :], q, q) * c + slab_weight(i, q)
            base = ends_added(base, q, (yl, yh), (zl, zh))
            inv[at, :] = (1.0 / base).reshape(q * q * NY, NZ)
            return carry

        lax.fori_loop(0, q, body, 0)

    invert(Q3, inv3)
    invert(Q1, inv1)

    pack_rows(Q3, inv3, gp3)
    pack_rows(Q1, inv1, gp1)

    def greet_copy(k, n, arriving):
        here = k if arriving else k ^ 1
        if n == 0:
            src, dst = weights.at[pl.ds(2 if k < 2 else 0, 2)], gw.at[here]
        elif k < 2:
            q, inv, target = ((Q3, inv3, gx3), (Q1, inv1, gx1))[n - 1]
            src, dst = inv.at[pl.ds(k * (q**3 - q * q) * NY, q * q * NY), :], target.at[here]
        else:
            source, target = ((gp3, gy3), (gp1, gy1))[n - 1]
            src, dst = source.at[k - 2], target.at[here - 2]
        return pltpu.make_async_remote_copy(
            src_ref=src, dst_ref=dst, send_sem=gs.at[k, n], recv_sem=gr.at[here, n],
            device_id={sides[k][0]: sides[k][1]}, device_id_type=MESH,
        )

    for k in (2, 3, 0, 1):

        @pl.when(sides[k][2])
        def _(k=k):
            for n in range(3):
                greet_copy(k, n, False).start()

    invert(Q5, inv5)

    def greeted():
        for k in range(4):

            @pl.when(sides[k][2])
            def _(k=k):
                for n in range(3):
                    greet_copy(k, n, True).wait_recv()
                    greet_copy(k, n, False).wait_send()

    def product_wide(q, d, slot, t, high, low):
        count = q**3
        padded = high.shape[0]
        s_high, s_low = high[...], low[...]
        for y in range(0, NY, 2):
            pair = [d[slot, pl.ds(y + h, count, stride=NY), :] for h in range(2)]
            v = jnp.concatenate(pair, 1)
            if padded > count:
                v = jnp.concatenate([v, jnp.zeros((padded - count, 2 * NZ), F32)], 0)
            v_high = v.astype(BF16)
            v_low = (v - v_high.astype(F32)).astype(BF16)
            out = jnp.dot(s_high, v_high, preferred_element_type=F32)
            out += jnp.dot(s_high, v_low, preferred_element_type=F32)
            out += jnp.dot(s_low, v_high, preferred_element_type=F32)
            for h in range(2):
                t[pl.ds(y + h, count, stride=NY), :] = out[:count, h * NZ : (h + 1) * NZ]

    def product_small(d, slot, t):
        count = Q1**3
        parts = [d[slot, pl.ds(n * NY, NY), :] for n in range(count)]
        for m in range(count):
            total = s1[m, 0] * parts[0]
            for n in range(1, count):
                total += s1[m, n] * parts[n]
            t[pl.ds(m * NY, NY), :] = total

    def local_part(level, slot):
        q, d, t, r = (level[name] for name in ("q", "d", "t", "r"))
        p = PENALTY[q]
        level["product"](slot)

        def local(i, carry):
            yl, yh, zl, zh = (p * weights[k] for k in range(2, 6))
            at = plane_at(i, q)
            dv = tiles(d[slot, at, :], q, q)
            lo, hi = dv[0], dv[q - 1]
            y_pair = (
                yl * (lo - jnp.where(row == 0, 0.0, pltpu.roll(hi, 1, 1))),
                yh * (hi - jnp.where(row == NY - 1, 0.0, pltpu.roll(lo, NY - 1, 1))),
            )
            lo, hi = dv[:, 0], dv[:, q - 1]
            z_pair = (
                zl * (lo - jnp.where(lane == 0, 0.0, pltpu.roll(hi, 1, 2))),
                zh * (hi - jnp.where(lane == NZ - 1, 0.0, pltpu.roll(lo, NZ - 1, 2))),
            )
            total = ends_added(tiles(t[at, :], q, q) * c, q, y_pair, z_pair)
            r[at, :] = r[at, :] - total.reshape(q * q * NY, NZ)
            return carry

        lax.fori_loop(0, q, local, 0)
        face = q * q * NY
        for k in range(2):
            at = pl.ds(0 if k == 0 else (q**3) * NY - face, face)
            r[at, :] = r[at, :] - (p * weights[k] * tiles(d[slot, at, :], q * q)).reshape(face, NZ)

    def rims(level, source, put):
        q = level["q"]
        for i in range(q):
            ytile[0, pl.ds(i * q * NY, q, stride=NY), :] = source[0, pl.ds(i * NY, q), :]
            ytile[1, pl.ds(i * q * NY + NY - 1, q, stride=NY), :] = source[1, pl.ds(i * NY, q), :]

        def rim(i, carry):
            for k in range(2):
                at = pl.ds(pl.multiple_of(i * (q * q * NY) + k * q * (q - 1) * NY, NY), q * NY)
                part = PENALTY[q] * weights[2 + k] * tiles(ytile[k, pl.ds(pl.multiple_of(i * (q * NY), NY), q * NY), :], q)
                put(at, part.reshape(q * NY, NZ))
            return carry

        lax.fori_loop(0, q, rim, 0)

    def slab_term(level, source, k, first, count):
        q = level["q"]
        part = PENALTY[q] * weights[k] * tiles(source[k, pl.ds(first * q * NY, count * q * NY), :], count * q)
        return part.reshape(count * q * NY, NZ)

    def step(level, slot, a, b, update, send, settled=False):
        q, d, r, x, inv = (level[name] for name in ("q", "d", "r", "x", "inv"))
        other = lax.rem(slot + 1, SLOTS)

        def put(at, part):
            r[at, :] = r[at, :] + part

        local_part(level, slot)
        for k in range(2):
            cross_do(k, "wait_recv", q, slot, True)
        rims(level, hy.at[slot], put)

        def advance(at):
            value = a * d[slot, at, :] + b * inv[at, :] * r[at, :]
            d[other, at, :] = value
            x[at, :] = x[at, :] + value

        if update and q > 2:

            def inside(i, carry):
                advance(plane_at(i, q))
                return carry

            lax.fori_loop(1, q - 1, inside, 0)

        def slab_face(k, first, count):
            at = face_at(k, q, first, count)
            put(at, slab_term(level, hx.at[slot], k, first, count))
            if update:
                advance(at)

        slab_do(near, "wait_recv", q, d, slot, None, True)
        slab_face(near, 0, q)
        if send:
            send_near(q, d, other)
        pieces = lines(q)
        groups = [[0, 1]] + [[n] for n in range(2, len(pieces))] if len(pieces) > 1 else [[0]]
        for number, group in enumerate(groups):
            for piece in group:
                slab_do(far, "wait_recv", q, d, slot, piece, True)
                slab_face(far, *pieces[piece])
            if send:
                if number == 0:
                    send_cross(q, d, other)
                send_far(q, d, other, group)
        if not settled:
            sent(q, d, slot, False)

    def correct(level, slot, rows, b, slab_put, cross_put):
        q, d, gx, gy = (level[name] for name in ("q", "d", "gx", "gy"))
        p = PENALTY[q]
        face = q * q * NY
        for k in range(2):
            for m in range(2):
                dtile[m, pl.ds(m * (NY - 1), q, stride=NY), :] = hd[slot, 2 * k + m, pl.ds(0, q), :]
            term = p * weights[k] * tiles(d[slot, pl.ds(k * (q**3 - q * q) * NY, face), :], q, q)
            low, high = (p * gw[k, m] * tiles(dtile[m, pl.ds(0, q * NY), :], q) for m in range(2))
            first, last = term[0:1] + low[None], term[q - 1 : q] + high[None]
            term = jnp.concatenate([first, term[1 : q - 1], last] if q > 2 else [first, last], 0)
            at = pl.ds(0, face)
            slab_put(k, at, b * gx[k, at, :] * term.reshape(face, NZ))
        for m in range(2):
            here, theirs = pl.ds(m * (NY - 1), 1), pl.ds((1 - m) * (NY - 1), 1)
            for i in range(q):
                at = pl.ds(i * NY, q)
                term = p * weights[2 + m, here, :] * rows[m, at, :]
                for k in range(2):
                    if i == k * (q - 1):
                        term = term + p * gw[2 + m, k, theirs, :] * hd[slot, 2 * k + m, pl.ds(0, q), :]
                cross_put(m, at, b * gy[m, at, :] * term)

    def planes(q, body):
        def one_plane(i, carry):
            body(plane_at(i, q))
            return carry

        lax.fori_loop(0, q, one_plane, 0)

    def half_round(level, slot, a, b, total):
        q, d, r, x, inv = (level[name] for name in ("q", "d", "r", "x", "inv"))
        other = lax.rem(slot + 1, SLOTS)

        def partial_next(at):
            value = a * d[slot, at, :] + b * inv[at, :] * r[at, :]
            d[other, at, :] = x[at, :] + value if total else value

        def put_both(at, part):
            r[at, :] = r[at, :] + part
            d[other, at, :] = d[other, at, :] + b * inv[at, :] * part

        local_part(level, slot)
        planes(q, partial_next)
        send_all(q, d, other, False)
        arrived_cross(q, slot)
        sent(q, d, other, False)
        rims(level, hy.at[slot], put_both)
        arrived_slab(q, d, slot)
        for k in range(2):
            put_both(face_at(k, q, 0, q), slab_term(level, hx.at[slot], k, 0, q))

    def keep_slab(k, at, part):
        hxl[k, at, :] = part

    def keep_cross(m, at, part):
        hyl[m, at, :] = part

    def double_step(level, slot, first, second, with_corners, total):
        q, d, r, x, inv = (level[name] for name in ("q", "d", "r", "x", "inv"))
        other, third = lax.rem(slot + 1, SLOTS), lax.rem(slot + 2, SLOTS)

        def put(at, part):
            r[at, :] = r[at, :] + part

        def add(at):
            x[at, :] = x[at, :] + d[other, at, :]

        def advance(at):
            value = second[0] * d[other, at, :] + second[1] * inv[at, :] * r[at, :]
            if total:
                d[third, at, :] = x[at, :] + value
            else:
                d[third, at, :] = value
                x[at, :] = x[at, :] + value

        half_round(level, slot, *first, False)
        planes(q, add)
        local_part(level, other)
        arrived_corners(slot)

        correct(level, slot, pack.at[slot], first[1], keep_slab, keep_cross)
        rims(level, hyl, put)
        for k in range(2):
            put(face_at(k, q, 0, q), slab_term(level, hxl, k, 0, q))
        arrived_cross(q, other)
        rims(level, hy.at[other], put)
        arrived_slab(q, d, other)
        for k in range(2):
            put(face_at(k, q, 0, q), slab_term(level, hx.at[other], k, 0, q))
        planes(q, advance)
        send_all(q, d, third, with_corners)
        sent(q, d, slot, True)

    def finish_round(level, slot, a, b):
        q, d = level["q"], level["d"]
        other = lax.rem(slot + 1, SLOTS)
        half_round(level, slot, a, b, True)
        arrived_corners(slot)
        arrived_cross(q, other)
        arrived_slab(q, d, other)

        def add_slab(k, at, part):
            hx[other, k, at, :] = hx[other, k, at, :] + part

        def add_cross(m, at, part):
            hy[other, m, at, :] = hy[other, m, at, :] + part

        correct(level, slot, pack.at[slot], b, add_slab, add_cross)
        sent(q, d, slot, True)

    def lift_slab(qc, qf, slot):
        table = lagrange(qf, qc)
        for k in range(2):
            lines_in = tiles(hx[slot, k, pl.ds(0, qc * qc * NY), :], qc, qc)
            for j in range(qf):
                line = weighted(table[j], [lines_in[n] for n in range(qc)])
                for n in range(qf):
                    hxl[k, pl.ds((j * qf + n) * NY, NY), :] = weighted(table[n], [line[e] for e in range(qc)])

    def spread_table(qc, qf):
        table = lagrange(qf, qc)
        spread = []
        for e in range(qc):
            column = jnp.zeros((NY, NZ), F32)
            for n in range(qf):
                if table[n, e] != 0.0:
                    column = jnp.where(row == n, float(table[n, e]), column)
            spread.append(column)
        return spread

    def lift_line(spread, line):
        value = spread[0] * line[0:1]
        for e in range(1, len(spread)):
            value = value + spread[e] * line[e : e + 1]
        return value

    def lift_cross(qc, qf, slot):
        table, spread = lagrange(qf, qc), spread_table(qc, qf)
        for k in range(2):
            for i in range(qf):
                line = weighted(table[i], [hy[slot, k, pl.ds(a * NY, qc), :] for a in range(qc)])
                hyl[k, pl.ds(i * NY, NY), :] = lift_line(spread, line)

    def lift_corners(qc, qf, slot):
        spread = spread_table(qc, qf)
        for g in range(4):
            hd[slot, g] = lift_line(spread, hd[slot, g])

    def lifted_step(coarse, slot, level, here, factor):
        q, d, r, x, inv = (level[name] for name in ("q", "d", "r", "x", "inv"))
        following = (here + 1) % SLOTS
        prolong(coarse["d"].at[slot], d, here, x, q, coarse["q"])
        local_part(level, here)
        lift_cross(coarse["q"], q, slot)
        lift_slab(coarse["q"], q, slot)

        def put(at, part):
            r[at, :] = r[at, :] + part

        def advance(at):
            value = factor * inv[at, :] * r[at, :]
            d[following, at, :] = value
            x[at, :] = x[at, :] + value

        rims(level, hyl, put)
        for k in range(2):
            put(face_at(k, q, 0, q), slab_term(level, hxl, k, 0, q))
        planes(q, advance)
        send_all(q, d, following, True)

    def lifted_round(coarse, level, here, factor):
        q, d, r, x, inv = (level[name] for name in ("q", "d", "r", "x", "inv"))
        qc, other, spare = coarse["q"], (here + 1) % SLOTS, (here + 3) % SLOTS

        def partial_next(at):
            d[other, at, :] = factor * inv[at, :] * r[at, :]

        def put(at, part):
            r[at, :] = r[at, :] + part

        def put_both(at, part):
            r[at, :] = r[at, :] + part
            d[other, at, :] = d[other, at, :] + factor * inv[at, :] * part

        def add(at):
            x[at, :] = x[at, :] + d[other, at, :]

        prolong(coarse["d"].at[here], d, here, x, q, qc)
        local_part(level, here)
        planes(q, partial_next)
        send_all(q, d, other, False)
        pack_rows(q, d.at[here], pack.at[spare])
        arrived_cross(qc, here)
        lift_cross(qc, q, here)
        arrived_slab(qc, coarse["d"], here)
        lift_slab(qc, q, here)
        sent(q, d, other, False)
        rims(level, hyl, put_both)
        for k in range(2):
            put_both(face_at(k, q, 0, q), slab_term(level, hxl, k, 0, q))
        planes(q, add)
        arrived_corners(here)
        lift_corners(qc, q, here)
        correct(level, here, pack.at[spare], factor, keep_slab, keep_cross)
        rims(level, hyl, put)
        for k in range(2):
            put(face_at(k, q, 0, q), slab_term(level, hxl, k, 0, q))
        sent(qc, coarse["d"], here, True)

    def first_update(level, slot, factor, with_corners):
        q, d, x, r, inv = (level[name] for name in ("q", "d", "x", "r", "inv"))

        def body(i, carry):
            at = plane_at(i, q)
            value = inv[at, :] * r[at, :] * factor
            d[slot, at, :] = value
            x[at, :] = value
            return carry

        lax.fori_loop(0, q, body, 0)
        send_all(q, d, slot, with_corners)

    def opening_step(level, factor, a, b):
        q, d, r, x, inv = (level[name] for name in ("q", "d", "r", "x", "inv"))
        p = PENALTY[q]

        def start(at):
            value = inv[at, :] * r[at, :] * factor
            d[0, at, :] = value
            x[at, :] = value

        def put(at, part):
            r[at, :] = r[at, :] + part

        def advance(at):
            value = a * d[0, at, :] + b * inv[at, :] * r[at, :]
            d[1, at, :] = value
            x[at, :] = x[at, :] + value

        planes(q, start)
        slab_do(far, "wait_send", q, raw, 0, None, False)
        slab_do(near, "wait_send", q, raw, 0, None, False)
        local_part(level, 0)
        coefs_done(range(4, 8))
        for k in range(2):
            own = hc[k, 0]
            y_pair = cross_weights(own, hcc[2 * k], hcc[2 * k + 1])
            z_pair = end_weights(own, hc[k, 1])
            y_pair, z_pair = ([jnp.broadcast_to(p * w, (q, NY, NZ)) for w in pair] for pair in (y_pair, z_pair))
            base = ends_added(tiles(gx5[k], q, q) * own + p * weights[k], q, y_pair, z_pair)
            gx5[k] = (1.0 / base).reshape(q * q * NY, NZ)
        node = lax.broadcasted_iota(jnp.int32, (q, NZ), 0)
        for m in range(2):
            here, theirs = m * (NY - 1), (1 - m) * (NY - 1)
            low, high = (w[theirs : theirs + 1] for w in end_weights(hc[2 + m, 0], hc[2 + m, 1]))
            own = hc[2 + m, 0, pl.ds(theirs, 1), :]
            across = p * weights[2 + m, pl.ds(here, 1), :]
            along = p * (jnp.where(node == 0, low, 0.0) + jnp.where(node == q - 1, high, 0.0))
            for i in range(q):
                at = pl.ds(i * NY, q)
                base = gy5[m, at, :] * own + across + along
                for k in range(2):
                    if i == k * (q - 1):
                        base = base + p * (0.5 * (own + hcc[2 * k + m, pl.ds(theirs, 1), :]))
                gy5[m, at, :] = 1.0 / base
        for k in range(2):
            cross_do(k, "wait_recv", q, 0, True)
        for m in range(2):
            for i in range(q):
                at = pl.ds(i * NY, q)
                hy[0, m, at, :] = gy5[m, at, :] * hy[0, m, at, :] * factor
        rims(level, hy.at[0], put)

        def inside(i, carry):
            advance(plane_at(i, q))
            return carry

        lax.fori_loop(1, q - 1, inside, 0)
        for k in (near, far):
            slab_do(k, "wait_recv", q, raw, 0, None, True)
            hx[0, k] = gx5[k] * hx[0, k] * factor
            at = face_at(k, q, 0, q)
            put(at, slab_term(level, hx.at[0], k, 0, q))
            advance(at)
        send_all(q, d, 1, False)
        for k in range(2):
            cross_do(k, "wait_send", q, 0, False)

            @pl.when(jnp.logical_not(sides[k][2]))
            def _(k=k):
                gx5[k] = jnp.zeros_like(gx5[k])

            @pl.when(jnp.logical_not(sides[2 + k][2]))
            def _(k=k):
                gy5[k] = jnp.zeros_like(gy5[k])

    def pick(k, values):
        out = jnp.float32(values[0])
        for n in range(1, len(values)):
            out = jnp.where(k == n, jnp.float32(values[n]), out)
        return out

    def run(level, exchange, factors, last):
        loop = len(factors) if last else len(factors) - 1

        def body(k, carry):
            a, b = pick(k, [f[0] for f in factors]), pick(k, [f[1] for f in factors])
            step(level, lax.rem(exchange + k, SLOTS), a, b, True, True)
            return carry

        lax.fori_loop(0, loop, body, 0)
        slot = (exchange + loop) % SLOTS
        if last:
            step(level, slot, 0.0, 0.0, False, False)
        else:
            step(level, slot, *factors[-1], True, False)

    def restrict(fine, coarse, qf, qc):
        table = lagrange(qf, qc)

        def body(j, carry):
            rows = [tiles(fine[pl.ds(pl.multiple_of(j * (qf * NY) + i * qf * qf * NY, NY), qf * NY), :], qf) for i in range(qf)]
            for a in range(qc):
                along = weighted(table[:, a], rows)
                for e in range(qc):
                    out = weighted(table[:, e], [along[k] for k in range(qf)])
                    work[pl.ds(pl.multiple_of(j * (qc * qc * NY) + (a * qc + e) * NY, NY), NY), :] = out
            return carry

        lax.fori_loop(0, qf, body, 0)

        def gather(a, carry):
            rows = [work[pl.ds(pl.multiple_of(a * (qc * NY) + j * qc * qc * NY, NY), qc * NY), :] for j in range(qf)]
            for b in range(qc):
                at = pl.ds(pl.multiple_of(a * (qc * qc * NY) + b * qc * NY, NY), qc * NY)
                coarse[at, :] = weighted(table[:, b], rows)
            return carry

        lax.fori_loop(0, qc, gather, 0)

    def prolong(coarse, fine, slot, sum_into, qf, qc):
        table = lagrange(qf, qc)

        def spread(a, carry):
            rows = [coarse[pl.ds(pl.multiple_of(a * (qc * qc * NY) + b * qc * NY, NY), qc * NY), :] for b in range(qc)]
            for j in range(qf):
                at = pl.ds(pl.multiple_of(a * (qc * NY) + j * qc * qc * NY, NY), qc * NY)
                work[at, :] = weighted(table[j], rows)
            return carry

        lax.fori_loop(0, qc, spread, 0)

        def body(j, carry):
            along = []
            for a in range(qc):
                at = pl.ds(pl.multiple_of(j * (qc * qc * NY) + a * qc * NY, NY), qc * NY)
                part = tiles(work[at, :], qc)
                along.append([weighted(table[k], [part[e] for e in range(qc)]) for k in range(qf)])
            for i in range(qf):
                for k in range(qf):
                    value = weighted(table[i], [along[a][k] for a in range(qc)])
                    at = pl.ds(pl.multiple_of(j * (qf * NY) + (i * qf * qf + k) * NY, NY), NY)
                    fine[slot, at, :] = value
                    sum_into[at, :] = sum_into[at, :] + value
            return carry

        lax.fori_loop(0, qf, body, 0)

    five = dict(q=Q5, d=d5, t=t5, r=res, x=sol, inv=inv5, gx=gx5, gy=gy5, product=lambda slot: product_wide(Q5, d5, slot, t5, sh5, sl5))
    three = dict(q=Q3, d=d3, t=t3, r=r3, x=x3, inv=inv3, gx=gx3, gy=gy3, product=lambda slot: product_wide(Q3, d3, slot, t3, sh3, sl3))
    one = dict(q=Q1, d=d1, t=t1, r=r1, x=x1, inv=inv1, gx=gx1, gy=gy1, product=lambda slot: product_small(d1, slot, t1))

    first, pairs = chebyshev_factors(DEGREE, LAMBDA_TOP / 8.0)
    coarse_first, coarse_pairs = chebyshev_factors(COARSE_ITERS, LAMBDA_TOP / 40.0)
    opening_step(five, first, *pairs[0])
    run(five, 1, pairs[1:], True)
    restrict(res, r3, Q5, Q3)
    first_update(three, 3, first, True)
    greeted()
    double_step(three, 3, *pairs, False, False)
    step(three, 5 % SLOTS, 0.0, 0.0, False, False)
    restrict(r3, r1, Q3, Q1)
    first_update(one, 6 % SLOTS, coarse_first, True)

    def coarse_rounds(n, carry):
        factors = [[pick(n, [f[part] for f in coarse_pairs[half:6:2]]) for part in range(2)] for half in range(2)]
        double_step(one, lax.rem(6 + 2 * n, SLOTS), *factors, True, False)
        return carry

    lax.fori_loop(0, 3, coarse_rounds, 0)
    finish_round(one, 12 % SLOTS, *coarse_pairs[6])
    lifted_step(one, 13 % SLOTS, three, 13 % SLOTS, first)
    double_step(three, 14 % SLOTS, *pairs, True, True)
    lifted_round(three, five, 16 % SLOTS, first)
    step(five, 17 % SLOTS, *pairs[0], True, True, settled=True)
    run(five, 18, pairs[1:], True)


def hand_out(sol, res, sol_out, res_out, done):
    rows = Q5**3 * NY // 4
    copies = [
        pltpu.make_async_copy(src.at[pl.ds(n * rows, rows), :], dst.at[pl.ds(n * rows, rows), :], done.at[k, n])
        for k, (src, dst) in enumerate(((sol, sol_out), (res, res_out))) for n in range(4)
    ]
    for copy in copies:
        copy.start()
    for copy in copies:
        copy.wait()


def per_device(right_side, coefficient, bottom_top, stiff_five, stiff_three, stiff_one):
    shape = right_side.shape
    n5, n3, n1 = Q5**3 * NY, Q3**3 * NY, Q1**3 * NY
    vmem = pl.BlockSpec(memory_space=pltpu.VMEM)
    hbm = pl.BlockSpec(memory_space=pltpu.HBM)
    field = lambda n: pltpu.VMEM((n, NZ), F32)
    slots = lambda *n: pltpu.VMEM((SLOTS, *n, NZ), F32)
    two = lambda n: pltpu.VMEM((2, n, NZ), F32)
    dma = pltpu.SemaphoreType.DMA
    sol, res = pl.pallas_call(
        kernel,
        out_shape=[jax.ShapeDtypeStruct((n5, NZ), F32)] * 2,
        in_specs=[hbm] * 6,
        out_specs=[vmem, vmem],
        scratch_shapes=[
            two(NY), pltpu.SMEM((2, NY), jnp.int32), pltpu.VMEM((Q5**3, Q5**3), F32), pltpu.VMEM((Q3**3, Q3**3), F32),
            pltpu.SMEM((Q1**3, Q1**3), F32),
            slots(n5), field(n5), field(n5),
            field(n3), field(n3), slots(n3), field(n3), field(n3),
            field(n1), field(n1), slots(n1), field(n1), field(n1),
            pltpu.VMEM((224, 224), BF16), pltpu.VMEM((224, 224), BF16),
            pltpu.VMEM((64, 64), BF16), pltpu.VMEM((64, 64), BF16),
            field(6 * 16 * NY), pltpu.VMEM((6, NY, NZ), F32),
            slots(2, Q5 * Q5 * NY), slots(2, Q5 * NY), two(Q5 * Q5 * NY), slots(2, Q5 * NY), pltpu.VMEM((4, 2, NY, NZ), F32),
            slots(4, NY), slots(4, NY), two(Q5 * NY),
            two(Q3 * Q3 * NY), two(Q1 * Q1 * NY), two(Q3 * NY), two(Q1 * NY), two(Q3 * NY), two(Q1 * NY),
            pltpu.VMEM((4, 2, NY, NZ), F32), two(Q5 * Q5 * NY), two(Q5 * NY),
            pltpu.VMEM((4, NY, NZ), F32), two(Q5 * Q5 * NY), two(Q5 * NY),
            dma((2, 4, SLOTS)), dma((2, 4, SLOTS)), dma((2, SLOTS)), dma((2, SLOTS)), dma((4, SLOTS)), dma((4, SLOTS)),
            dma((4, 3)), dma((4, 3)), dma((8,)), dma((8,)), dma((6,)),
        ],
        compiler_params=pltpu.CompilerParams(
            collective_id=0, has_side_effects=True, vmem_limit_bytes=48 * 2**20
        ),
    )(
        *(
            pltpu.with_memory_space_constraint(value, pltpu.HBM)
            for value in (
                coefficient.reshape(NY, NZ), bottom_top.reshape(2, NY), right_side.reshape(n5, NZ),
                stiff_five, stiff_three, stiff_one,
            )
        )
    )
    sol, res = pl.pallas_call(
        hand_out,
        out_shape=[jax.ShapeDtypeStruct((n5, NZ), F32)] * 2,
        in_specs=[vmem] * 2,
        out_specs=[hbm, hbm],
        scratch_shapes=[dma((2, 4))],
    )(*(pltpu.with_memory_space_constraint(value, pltpu.VMEM) for value in (sol, res)))
    return sol.reshape(shape), res.reshape(shape)


def solution(mesh):
    field = P(None, None, None, "slab", "cross", None)
    return jax.shard_map(
        per_device,
        mesh=mesh,
        in_specs=(field, P("slab", "cross", None), P(None, "slab", "cross"), P(), P(), P()),
        out_specs=(field, field),
        check_vma=False,
    )
```

```python
import functools

import jax
import jax.numpy as jnp
import numpy as np
from jax import lax
from jax.experimental import pallas as pl
from jax.experimental.pallas import tpu as pltpu
from jax.sharding import PartitionSpec as P

MESH = pl.DeviceIdType.MESH
F32 = jnp.float32
BF16 = jnp.bfloat16
Q5, Q3, Q1 = 6, 4, 2
DEGREE = 3
COARSE_ITERS = 8
LAMBDA_TOP = 2.2
NY, NZ = 8, 128
SLOTS = 4
PENALTY = {Q5: 3.0, Q3: 2.0, Q1: 1.0}


def lagrange(fine_count, coarse_count):
    fine = np.linspace(-1.0, 1.0, fine_count)
    coarse = np.linspace(-1.0, 1.0, coarse_count)
    table = np.ones((fine_count, coarse_count))
    for c in range(coarse_count):
        for o in range(coarse_count):
            if o != c:
                table[:, c] = table[:, c] * (fine - coarse[o]) / (coarse[c] - coarse[o])
    return table.astype(np.float32)


def chebyshev_factors(steps, lowest):
    center = 0.5 * (LAMBDA_TOP + lowest)
    radius = 0.5 * (LAMBDA_TOP - lowest)
    sigma = center / radius
    rho = 1.0 / sigma
    pairs = []
    for _ in range(steps - 1):
        rho_next = 1.0 / (2.0 * sigma - rho)
        pairs.append((rho_next * rho, 2.0 * rho_next / radius))
        rho = rho_next
    return 1.0 / center, pairs


def weighted(table_row, terms):
    total = None
    for value, term in zip(table_row, terms):
        if value == 0.0:
            continue
        part = term if value == 1.0 else float(value) * term
        total = part if total is None else total + part
    return total


def tiles(value, *lead):
    return value.reshape(*lead, NY, NZ)


class Unslotted:
    def __init__(self, ref):
        self.ref, self.at = ref, self

    def __getitem__(self, index):
        return self.ref.at[index[1:]]


def kernel(
    coef_in, ends_in, rhs_in, s5_in, s3_in, s1_in, sol, res,
    mine, ends, s5, s3, s1,
    d5, t5, inv5, x3, r3, d3, t3, inv3, x1, r1, d1, t1, inv1,
    sh5, sl5, sh3, sl3, work, weights, hx, hy, ytile, pack, hc,
    hd, dpack, dtile, gx3, gx1, gy3, gy1, gp3, gp1, gw, hxl, hyl, hcc, gx5, gy5,
    xs, xr, ys, yr, cs, cr, gs, gr, csem, crsem, load,
):
    slab, cross = lax.axis_index("slab"), lax.axis_index("cross")
    ns, nc = lax.axis_size("slab"), lax.axis_size("cross")
    sides = (
        ("slab", slab - 1, slab > 0),
        ("slab", slab + 1, slab < ns - 1),
        ("cross", cross - 1, cross > 0),
        ("cross", cross + 1, cross < nc - 1),
    )
    corners = [
        ({"slab": slab + 2 * k - 1, "cross": cross + 2 * m - 1}, sides[k][2] & sides[2 + m][2])
        for k in range(2) for m in range(2)
    ]

    for k in range(2):

        @pl.when(jnp.logical_not(sides[k][2]))
        def _(k=k):
            hc[k] = jnp.zeros_like(hc[k])
            gw[k] = jnp.zeros_like(gw[k])
            gx3[k] = jnp.zeros_like(gx3[k])
            gx1[k] = jnp.zeros_like(gx1[k])
            for slot in range(SLOTS):
                hx[slot, k] = jnp.zeros_like(hx[slot, k])

        @pl.when(jnp.logical_not(sides[2 + k][2]))
        def _(k=k):
            hc[2 + k] = jnp.zeros_like(hc[2 + k])
            gw[2 + k] = jnp.zeros_like(gw[2 + k])
            gy3[k] = jnp.zeros_like(gy3[k])
            gy1[k] = jnp.zeros_like(gy1[k])
            for slot in range(SLOTS):
                hy[slot, k] = jnp.zeros_like(hy[slot, k])

    for g in range(4):

        @pl.when(jnp.logical_not(corners[g][1]))
        def _(g=g):
            hcc[g] = jnp.zeros_like(hcc[g])
            for slot in range(SLOTS):
                hd[slot, g] = jnp.zeros_like(hd[slot, g])

    barrier = pltpu.get_barrier_semaphore()
    peers = [({axis: index}, there) for axis, index, there in sides] + corners
    for device, there in peers:

        @pl.when(there)
        def _(device=device):
            pl.semaphore_signal(barrier, inc=1, device_id=device, device_id_type=MESH)

    pairs = ((coef_in, mine.at[0]), (s5_in, s5), (s3_in, s3), (rhs_in, res), (ends_in, ends), (s1_in, s1))
    loads = [pltpu.make_async_copy(src, dst, load.at[n]) for n, (src, dst) in enumerate(pairs)]
    for copy in loads:
        copy.start()
    ytile[...] = jnp.zeros_like(ytile)
    dtile[...] = jnp.zeros_like(dtile)
    for copy in loads:
        copy.wait()

    row = lax.broadcasted_iota(jnp.int32, (NY, NZ), 0)
    lane = lax.broadcasted_iota(jnp.int32, (NY, NZ), 1)
    bottom = jnp.zeros((NY, NZ), F32)
    top = jnp.zeros((NY, NZ), F32)
    for y in range(NY):
        bottom = jnp.where(row == y, ends[0, y].astype(F32), bottom)
        top = jnp.where(row == y, ends[1, y].astype(F32), top)
    mine[1] = jnp.where(lane == 0, bottom, jnp.where(lane == NZ - 1, top, 0.0))

    far = lax.rem(slab, 2)
    near = 1 - far

    def lines(q):
        if q < Q5:
            return [(0, q)]
        return [(0, 1), (q - 1, 1)] + [(j, min(2, q - 1 - j)) for j in range(1, q - 1, 2)]

    def groups(q):
        count = len(lines(q))
        return [[0, 1]] + [[n] for n in range(2, count)] if count > 1 else [[0]]

    def face_at(k, q, first, count):
        return pl.ds(pl.multiple_of(k * ((q**3 - q * q) * NY) + first * q * NY, NY), count * q * NY)

    def slab_copy(k, q, d, slot, piece, arriving):
        first, count = (0, q) if piece is None else lines(q)[piece]
        number = 0 if piece is None else piece
        here = k if arriving else 1 - k
        return pltpu.make_async_remote_copy(
            src_ref=d.at[slot, face_at(k, q, first, count), :],
            dst_ref=hx.at[slot, here, pl.ds(first * q * NY, count * q * NY), :],
            send_sem=xs.at[k, number, slot], recv_sem=xr.at[here, number, slot],
            device_id={"slab": slab + 2 * k - 1}, device_id_type=MESH,
        )

    def cross_copy(k, q, slot, arriving):
        here = k if arriving else k ^ 1
        return pltpu.make_async_remote_copy(
            src_ref=pack.at[slot, k, pl.ds(0, q * NY), :], dst_ref=hy.at[slot, here, pl.ds(0, q * NY), :],
            send_sem=ys.at[k, slot], recv_sem=yr.at[here, slot],
            device_id={"cross": sides[2 + k][1]}, device_id_type=MESH,
        )

    def slab_do(k, method, *args):
        index = slab + 2 * k - 1

        @pl.when((index >= 0) & (index < ns))
        def _():
            getattr(slab_copy(k, *args), method)()

    def cross_do(k, method, *args):
        @pl.when(sides[2 + k][2])
        def _():
            getattr(cross_copy(k, *args), method)()

    def send_near(q, d, slot):
        slab_do(near, "start", q, d, slot, None, False)

    def send_far(q, d, slot, pieces):
        for piece in pieces:
            slab_do(far, "start", q, d, slot, piece, False)

    def send_cross(q, d, slot):
        for i in range(q):
            pack[slot, 0, pl.ds(i * NY, q), :] = d[slot, pl.ds(i * q * q * NY, q, stride=NY), :]
            pack[slot, 1, pl.ds(i * NY, q), :] = d[slot, pl.ds((i * q * q + q * (q - 1)) * NY + NY - 1, q, stride=NY), :]
        for k in range(2):
            cross_do(k, "start", q, slot, False)

    def corner_copy(g, slot, arriving):
        here = g if arriving else 3 - g
        return pltpu.make_async_remote_copy(
            src_ref=dpack.at[slot, g], dst_ref=hd.at[slot, here],
            send_sem=cs.at[g, slot], recv_sem=cr.at[here, slot],
            device_id=corners[g][0], device_id_type=MESH,
        )

    def corner_do(g, method, *args):
        @pl.when(corners[g][1])
        def _():
            getattr(corner_copy(g, *args), method)()

    def send_corners(q, d, slot):
        for g in range(4):
            k, m = g // 2, g % 2
            node = k * (q**3 - q * q) + m * (q * q - q)
            dpack[slot, g, pl.ds(0, q), :] = d[slot, pl.ds(node * NY + m * (NY - 1), q, stride=NY), :]
        for g in range(4):
            corner_do(g, "start", slot, False)

    def send_all(q, d, slot, with_corners):
        if with_corners:
            send_corners(q, d, slot)
        send_cross(q, d, slot)
        send_near(q, d, slot)
        send_far(q, d, slot, range(len(lines(q))))

    def arrived_cross(q, slot):
        for k in range(2):
            cross_do(k, "wait_recv", q, slot, True)

    def arrived_slab(q, d, slot):
        slab_do(near, "wait_recv", q, d, slot, None, True)
        for piece in range(len(lines(q))):
            slab_do(far, "wait_recv", q, d, slot, piece, True)

    def arrived_corners(slot):
        for g in range(4):
            corner_do(g, "wait_recv", slot, True)

    def sent(q, d, slot, with_corners):
        slab_do(near, "wait_send", q, d, slot, None, False)
        for piece in range(len(lines(q))):
            slab_do(far, "wait_send", q, d, slot, piece, False)
        for k in range(2):
            cross_do(k, "wait_send", q, slot, False)
        if with_corners:
            for g in range(4):
                corner_do(g, "wait_send", slot, False)

    def pack_rows(q, source, target):
        for i in range(q):
            target[0, pl.ds(i * NY, q), :] = source[pl.ds(i * q * q * NY, q, stride=NY), :]
            target[1, pl.ds(i * NY, q), :] = source[pl.ds((i * q * q + q * (q - 1)) * NY + NY - 1, q, stride=NY), :]

    pack_rows(Q5, res, pack.at[0])
    pl.semaphore_wait(barrier, sum(there.astype(jnp.int32) for _, there in peers))

    def coef_copy(k, arriving):
        if k < 4:
            here = k if arriving else k ^ 1
            src, dst = mine, hc.at[here]
        else:
            here = k if arriving else 11 - k
            src, dst = mine.at[0], hcc.at[here - 4]
        return pltpu.make_async_remote_copy(
            src_ref=src, dst_ref=dst, send_sem=csem.at[k], recv_sem=crsem.at[here],
            device_id=peers[k][0], device_id_type=MESH,
        )

    for k in (2, 3, 0, 1, 4, 5, 6, 7):

        @pl.when(peers[k][1])
        def _(k=k):
            coef_copy(k, False).start()

    raw = Unslotted(res)
    for k in range(2):
        cross_do(k, "start", Q5, 0, False)
    send_near(Q5, raw, 0)
    send_far(Q5, raw, 0, range(len(lines(Q5))))

    def split(table, high, low, count):
        value = table[...]
        high[...] = jnp.zeros_like(high)
        low[...] = jnp.zeros_like(low)
        top = value.astype(BF16)
        high[pl.ds(0, count), pl.ds(0, count)] = top
        low[pl.ds(0, count), pl.ds(0, count)] = (value - top.astype(F32)).astype(BF16)

    split(s5, sh5, sl5, Q5**3)
    split(s3, sh3, sl3, Q3**3)

    def spread_diagonal(table, inv, count):
        value = table[...]
        same = lax.broadcasted_iota(jnp.int32, value.shape, 0) == lax.broadcasted_iota(jnp.int32, value.shape, 1)
        column = jnp.sum(jnp.where(same, value, 0.0), axis=1, keepdims=True)
        wide = jnp.broadcast_to(column, (count, NZ))
        for y in range(NY):
            inv[pl.ds(y, count, stride=NY), :] = wide

    spread_diagonal(s5, inv5, Q5**3)
    spread_diagonal(s3, inv3, Q3**3)
    for n in range(Q1**3):
        inv1[pl.ds(n * NY, NY), :] = jnp.full((NY, NZ), s1[n, n])
    for k in range(2):
        gx5[k] = inv5[face_at(1 - k, Q5, 0, Q5), :]
        for i in range(Q5):
            node = i * Q5 * Q5 + (1 - k) * Q5 * (Q5 - 1)
            gy5[k, pl.ds(i * NY, Q5), :] = inv5[pl.ds(node * NY, Q5, stride=NY), :]

    def coefs_done(ks):
        for k in ks:

            @pl.when(peers[k][1])
            def _(k=k):
                coef_copy(k, True).wait_recv()
                coef_copy(k, False).wait_send()

    coefs_done(range(4))
    c = mine[0]

    def cross_weights(own, below, above):
        before = jnp.where(row == 0, pltpu.roll(below, 1, 0), pltpu.roll(own, 1, 0))
        after = jnp.where(row == NY - 1, pltpu.roll(above, NY - 1, 0), pltpu.roll(own, NY - 1, 0))
        return 0.5 * (own + before), 0.5 * (own + after)

    def end_weights(own, flags):
        low = jnp.where(lane == 0, flags * own, 0.5 * (own + pltpu.roll(own, 1, 1)))
        high = jnp.where(lane == NZ - 1, flags * own, 0.5 * (own + pltpu.roll(own, NZ - 1, 1)))
        return low, high

    weights[0] = 0.5 * (c + hc[0, 0])
    weights[1] = 0.5 * (c + hc[1, 0])
    weights[2], weights[3] = cross_weights(c, hc[2, 0], hc[3, 0])
    weights[4], weights[5] = end_weights(c, mine[1])

    def ends_added(base, q, y_pair, z_pair):
        first = base[0:1] + y_pair[0][None]
        last = base[q - 1 : q] + y_pair[1][None]
        base = jnp.concatenate([first, base[1 : q - 1], last] if q > 2 else [first, last], 0)
        first = base[:, 0:1] + z_pair[0][:, None]
        last = base[:, q - 1 : q] + z_pair[1][:, None]
        return jnp.concatenate([first, base[:, 1 : q - 1], last] if q > 2 else [first, last], 1)

    def slab_weight(i, q):
        return jnp.where(i == 0, PENALTY[q] * weights[0], 0.0) + jnp.where(i == q - 1, PENALTY[q] * weights[1], 0.0)

    def plane_at(i, q):
        return pl.ds(pl.multiple_of(i * (q * q * NY), NY), q * q * NY)

    def invert(q, inv):
        yl, yh, zl, zh = (jnp.broadcast_to(PENALTY[q] * weights[k], (q, NY, NZ)) for k in range(2, 6))

        def body(i, carry):
            at = plane_at(i, q)
            base = tiles(inv[at, :], q, q) * c + slab_weight(i, q)
            base = ends_added(base, q, (yl, yh), (zl, zh))
            inv[at, :] = (1.0 / base).reshape(q * q * NY, NZ)
            return carry

        lax.fori_loop(0, q, body, 0)

    invert(Q5, inv5)

    def product_wide(q, d, slot, t, high, low):
        count = q**3
        padded = high.shape[0]
        s_high, s_low = high[...], low[...]
        for y in range(0, NY, 2):
            pair = [d[slot, pl.ds(y + h, count, stride=NY), :] for h in range(2)]
            v = jnp.concatenate(pair, 1)
            if padded > count:
                v = jnp.concatenate([v, jnp.zeros((padded - count, 2 * NZ), F32)], 0)
            v_high = v.astype(BF16)
            v_low = (v - v_high.astype(F32)).astype(BF16)
            out = jnp.dot(s_high, v_high, preferred_element_type=F32)
            out += jnp.dot(s_high, v_low, preferred_element_type=F32)
            out += jnp.dot(s_low, v_high, preferred_element_type=F32)
            for h in range(2):
                t[pl.ds(y + h, count, stride=NY), :] = out[:count, h * NZ : (h + 1) * NZ]

    def product_small(d, slot, t):
        count = Q1**3
        parts = [d[slot, pl.ds(n * NY, NY), :] for n in range(count)]
        for m in range(count):
            total = s1[m, 0] * parts[0]
            for n in range(1, count):
                total += s1[m, n] * parts[n]
            t[pl.ds(m * NY, NY), :] = total

    def local_part(level, slot):
        q, d, t, r = (level[name] for name in ("q", "d", "t", "r"))
        p = PENALTY[q]
        level["product"](slot)

        def local(i, carry):
            yl, yh, zl, zh = (p * weights[k] for k in range(2, 6))
            at = plane_at(i, q)
            dv = tiles(d[slot, at, :], q, q)
            lo, hi = dv[0], dv[q - 1]
            y_pair = (
                yl * (lo - jnp.where(row == 0, 0.0, pltpu.roll(hi, 1, 1))),
                yh * (hi - jnp.where(row == NY - 1, 0.0, pltpu.roll(lo, NY - 1, 1))),
            )
            lo, hi = dv[:, 0], dv[:, q - 1]
            z_pair = (
                zl * (lo - jnp.where(lane == 0, 0.0, pltpu.roll(hi, 1, 2))),
                zh * (hi - jnp.where(lane == NZ - 1, 0.0, pltpu.roll(lo, NZ - 1, 2))),
            )
            total = ends_added(tiles(t[at, :], q, q) * c, q, y_pair, z_pair)
            r[at, :] = r[at, :] - total.reshape(q * q * NY, NZ)
            return carry

        lax.fori_loop(0, q, local, 0)
        face = q * q * NY
        for k in range(2):
            at = pl.ds(0 if k == 0 else (q**3) * NY - face, face)
            r[at, :] = r[at, :] - (p * weights[k] * tiles(d[slot, at, :], q * q)).reshape(face, NZ)

    def rims(level, source, put):
        q = level["q"]
        for i in range(q):
            ytile[0, pl.ds(i * q * NY, q, stride=NY), :] = source[0, pl.ds(i * NY, q), :]
            ytile[1, pl.ds(i * q * NY + NY - 1, q, stride=NY), :] = source[1, pl.ds(i * NY, q), :]

        def rim(i, carry):
            for k in range(2):
                at = pl.ds(pl.multiple_of(i * (q * q * NY) + k * q * (q - 1) * NY, NY), q * NY)
                part = PENALTY[q] * weights[2 + k] * tiles(ytile[k, pl.ds(pl.multiple_of(i * (q * NY), NY), q * NY), :], q)
                put(at, part.reshape(q * NY, NZ))
            return carry

        lax.fori_loop(0, q, rim, 0)

    def slab_term(level, source, k, first, count):
        q = level["q"]
        part = PENALTY[q] * weights[k] * tiles(source[k, pl.ds(first * q * NY, count * q * NY), :], count * q)
        return part.reshape(count * q * NY, NZ)

    def step(level, slot, a, b, update, send, settled=False, meanwhile=None):
        q, d, r, x, inv = (level[name] for name in ("q", "d", "r", "x", "inv"))
        other = lax.rem(slot + 1, SLOTS)

        def put(at, part):
            r[at, :] = r[at, :] + part

        local_part(level, slot)
        for k in range(2):
            cross_do(k, "wait_recv", q, slot, True)
        rims(level, hy.at[slot], put)

        def advance(at):
            value = a * d[slot, at, :] + b * inv[at, :] * r[at, :]
            d[other, at, :] = value
            x[at, :] = x[at, :] + value

        if update and q > 2:

            def inside(i, carry):
                advance(plane_at(i, q))
                return carry

            lax.fori_loop(1, q - 1, inside, 0)

        def slab_face(k, first, count):
            at = face_at(k, q, first, count)
            put(at, slab_term(level, hx.at[slot], k, first, count))
            if update:
                advance(at)

        slab_do(near, "wait_recv", q, d, slot, None, True)
        slab_face(near, 0, q)
        if send:
            send_near(q, d, other)
        if meanwhile is not None:
            meanwhile()
        for number, group in enumerate(groups(q)):
            for piece in group:
                slab_do(far, "wait_recv", q, d, slot, piece, True)
                slab_face(far, *lines(q)[piece])
            if send:
                if number == 0:
                    send_cross(q, d, other)
                send_far(q, d, other, group)
        if not settled:
            sent(q, d, slot, False)

    def correct(level, slot, rows, b, slab_put, cross_put):
        q, d, gx, gy = (level[name] for name in ("q", "d", "gx", "gy"))
        p = PENALTY[q]
        face = q * q * NY
        for k in range(2):
            for m in range(2):
                dtile[m, pl.ds(m * (NY - 1), q, stride=NY), :] = hd[slot, 2 * k + m, pl.ds(0, q), :]
            term = p * weights[k] * tiles(d[slot, pl.ds(k * (q**3 - q * q) * NY, face), :], q, q)
            low, high = (p * gw[k, m] * tiles(dtile[m, pl.ds(0, q * NY), :], q) for m in range(2))
            first, last = term[0:1] + low[None], term[q - 1 : q] + high[None]
            term = jnp.concatenate([first, term[1 : q - 1], last] if q > 2 else [first, last], 0)
            at = pl.ds(0, face)
            slab_put(k, at, b * gx[k, at, :] * term.reshape(face, NZ))
        for m in range(2):
            here, theirs = pl.ds(m * (NY - 1), 1), pl.ds((1 - m) * (NY - 1), 1)
            for i in range(q):
                at = pl.ds(i * NY, q)
                term = p * weights[2 + m, here, :] * rows[m, at, :]
                for k in range(2):
                    if i == k * (q - 1):
                        term = term + p * gw[2 + m, k, theirs, :] * hd[slot, 2 * k + m, pl.ds(0, q), :]
                cross_put(m, at, b * gy[m, at, :] * term)

    def planes(q, body):
        def one_plane(i, carry):
            body(plane_at(i, q))
            return carry

        lax.fori_loop(0, q, one_plane, 0)

    def half_round(level, slot, a, b, total):
        q, d, r, x, inv = (level[name] for name in ("q", "d", "r", "x", "inv"))
        other = lax.rem(slot + 1, SLOTS)

        def partial_next(at):
            value = a * d[slot, at, :] + b * inv[at, :] * r[at, :]
            d[other, at, :] = x[at, :] + value if total else value

        def put_both(at, part):
            r[at, :] = r[at, :] + part
            d[other, at, :] = d[other, at, :] + b * inv[at, :] * part

        local_part(level, slot)
        planes(q, partial_next)
        send_all(q, d, other, False)
        arrived_cross(q, slot)
        sent(q, d, other, False)
        rims(level, hy.at[slot], put_both)
        arrived_slab(q, d, slot)
        for k in range(2):
            put_both(face_at(k, q, 0, q), slab_term(level, hx.at[slot], k, 0, q))

    def keep_slab(k, at, part):
        hxl[k, at, :] = part

    def keep_cross(m, at, part):
        hyl[m, at, :] = part

    def double_step(level, slot, first, second, with_corners, total):
        q, d, r, x, inv = (level[name] for name in ("q", "d", "r", "x", "inv"))
        other, third = lax.rem(slot + 1, SLOTS), lax.rem(slot + 2, SLOTS)

        def put(at, part):
            r[at, :] = r[at, :] + part

        def add(at):
            x[at, :] = x[at, :] + d[other, at, :]

        def advance(at):
            value = second[0] * d[other, at, :] + second[1] * inv[at, :] * r[at, :]
            if total:
                d[third, at, :] = x[at, :] + value
            else:
                d[third, at, :] = value
                x[at, :] = x[at, :] + value

        half_round(level, slot, *first, False)
        planes(q, add)
        local_part(level, other)
        arrived_corners(slot)

        correct(level, slot, pack.at[slot], first[1], keep_slab, keep_cross)
        rims(level, hyl, put)
        for k in range(2):
            put(face_at(k, q, 0, q), slab_term(level, hxl, k, 0, q))
        arrived_cross(q, other)
        rims(level, hy.at[other], put)
        arrived_slab(q, d, other)
        for k in range(2):
            put(face_at(k, q, 0, q), slab_term(level, hx.at[other], k, 0, q))
        planes(q, advance)
        send_all(q, d, third, with_corners)
        sent(q, d, slot, True)

    def finish_round(level, slot, a, b):
        q, d = level["q"], level["d"]
        other = lax.rem(slot + 1, SLOTS)
        half_round(level, slot, a, b, True)
        arrived_corners(slot)
        arrived_cross(q, other)
        arrived_slab(q, d, other)

        def add_slab(k, at, part):
            hx[other, k, at, :] = hx[other, k, at, :] + part

        def add_cross(m, at, part):
            hy[other, m, at, :] = hy[other, m, at, :] + part

        correct(level, slot, pack.at[slot], b, add_slab, add_cross)
        sent(q, d, slot, True)

    def lift_slab(qc, qf, slot):
        table = lagrange(qf, qc)
        for k in range(2):
            lines_in = tiles(hx[slot, k, pl.ds(0, qc * qc * NY), :], qc, qc)
            for j in range(qf):
                line = weighted(table[j], [lines_in[n] for n in range(qc)])
                for n in range(qf):
                    hxl[k, pl.ds((j * qf + n) * NY, NY), :] = weighted(table[n], [line[e] for e in range(qc)])

    def spread_table(qc, qf):
        table = lagrange(qf, qc)
        spread = []
        for e in range(qc):
            column = jnp.zeros((NY, NZ), F32)
            for n in range(qf):
                if table[n, e] != 0.0:
                    column = jnp.where(row == n, float(table[n, e]), column)
            spread.append(column)
        return spread

    def lift_line(spread, line):
        value = spread[0] * line[0:1]
        for e in range(1, len(spread)):
            value = value + spread[e] * line[e : e + 1]
        return value

    def lift_cross(qc, qf, slot):
        table, spread = lagrange(qf, qc), spread_table(qc, qf)
        for k in range(2):
            for i in range(qf):
                line = weighted(table[i], [hy[slot, k, pl.ds(a * NY, qc), :] for a in range(qc)])
                hyl[k, pl.ds(i * NY, NY), :] = lift_line(spread, line)

    def lift_corners(qc, qf, slot):
        spread = spread_table(qc, qf)
        for g in range(4):
            hd[slot, g] = lift_line(spread, hd[slot, g])

    def lifted_step(coarse, slot, level, here, factor):
        q, d, r, x, inv = (level[name] for name in ("q", "d", "r", "x", "inv"))
        following = (here + 1) % SLOTS
        prolong(coarse["d"].at[slot], d, here, x, q, coarse["q"])
        local_part(level, here)
        lift_cross(coarse["q"], q, slot)
        lift_slab(coarse["q"], q, slot)

        def put(at, part):
            r[at, :] = r[at, :] + part

        def advance(at):
            value = factor * inv[at, :] * r[at, :]
            d[following, at, :] = value
            x[at, :] = x[at, :] + value

        rims(level, hyl, put)
        for k in range(2):
            put(face_at(k, q, 0, q), slab_term(level, hxl, k, 0, q))
        planes(q, advance)
        send_all(q, d, following, True)

    def lifted_round(coarse, level, here, factor):
        q, d, r, x, inv = (level[name] for name in ("q", "d", "r", "x", "inv"))
        qc, other, spare = coarse["q"], (here + 1) % SLOTS, (here + 3) % SLOTS

        def partial_next(at):
            d[other, at, :] = factor * inv[at, :] * r[at, :]

        def put(at, part):
            r[at, :] = r[at, :] + part

        def put_both(at, part):
            r[at, :] = r[at, :] + part
            d[other, at, :] = d[other, at, :] + factor * inv[at, :] * part

        def add(at):
            x[at, :] = x[at, :] + d[other, at, :]

        prolong(coarse["d"].at[here], d, here, x, q, qc)
        local_part(level, here)
        planes(q, partial_next)
        send_all(q, d, other, False)
        pack_rows(q, d.at[here], pack.at[spare])
        arrived_cross(qc, here)
        lift_cross(qc, q, here)
        arrived_slab(qc, coarse["d"], here)
        lift_slab(qc, q, here)
        sent(q, d, other, False)
        rims(level, hyl, put_both)
        for k in range(2):
            put_both(face_at(k, q, 0, q), slab_term(level, hxl, k, 0, q))
        planes(q, add)
        arrived_corners(here)
        lift_corners(qc, q, here)
        correct(level, here, pack.at[spare], factor, keep_slab, keep_cross)
        rims(level, hyl, put)
        for k in range(2):
            put(face_at(k, q, 0, q), slab_term(level, hxl, k, 0, q))
        sent(qc, coarse["d"], here, True)

    def first_update(level, slot, factor, with_corners):
        q, d, x, r, inv = (level[name] for name in ("q", "d", "x", "r", "inv"))

        def body(i, carry):
            at = plane_at(i, q)
            value = inv[at, :] * r[at, :] * factor
            d[slot, at, :] = value
            x[at, :] = value
            return carry

        lax.fori_loop(0, q, body, 0)
        send_all(q, d, slot, with_corners)

    def opening_step(level, factor, a, b):
        q, d, r, x, inv = (level[name] for name in ("q", "d", "r", "x", "inv"))
        p = PENALTY[q]

        def start(at):
            value = inv[at, :] * r[at, :] * factor
            d[0, at, :] = value
            x[at, :] = value

        def put(at, part):
            r[at, :] = r[at, :] + part

        def advance(at):
            value = a * d[0, at, :] + b * inv[at, :] * r[at, :]
            d[1, at, :] = value
            x[at, :] = x[at, :] + value

        planes(q, start)
        slab_do(near, "wait_send", q, raw, 0, None, False)
        for piece in range(len(lines(q))):
            slab_do(far, "wait_send", q, raw, 0, piece, False)
        local_part(level, 0)
        coefs_done(range(4, 8))
        for k in range(2):
            own = hc[k, 0]
            y_pair = cross_weights(own, hcc[2 * k], hcc[2 * k + 1])
            z_pair = end_weights(own, hc[k, 1])
            y_pair, z_pair = ([jnp.broadcast_to(p * w, (q, NY, NZ)) for w in pair] for pair in (y_pair, z_pair))
            base = ends_added(tiles(gx5[k], q, q) * own + p * weights[k], q, y_pair, z_pair)
            gx5[k] = (1.0 / base).reshape(q * q * NY, NZ)
        node = lax.broadcasted_iota(jnp.int32, (q, NZ), 0)
        for m in range(2):
            here, theirs = m * (NY - 1), (1 - m) * (NY - 1)
            low, high = (w[theirs : theirs + 1] for w in end_weights(hc[2 + m, 0], hc[2 + m, 1]))
            own = hc[2 + m, 0, pl.ds(theirs, 1), :]
            across = p * weights[2 + m, pl.ds(here, 1), :]
            along = p * (jnp.where(node == 0, low, 0.0) + jnp.where(node == q - 1, high, 0.0))
            for i in range(q):
                at = pl.ds(i * NY, q)
                base = gy5[m, at, :] * own + across + along
                for k in range(2):
                    if i == k * (q - 1):
                        base = base + p * (0.5 * (own + hcc[2 * k + m, pl.ds(theirs, 1), :]))
                gy5[m, at, :] = 1.0 / base
        for k in range(2):
            cross_do(k, "wait_recv", q, 0, True)
        for m in range(2):
            for i in range(q):
                at = pl.ds(i * NY, q)
                hy[0, m, at, :] = gy5[m, at, :] * hy[0, m, at, :] * factor
        rims(level, hy.at[0], put)

        def inside(i, carry):
            advance(plane_at(i, q))
            return carry

        lax.fori_loop(1, q - 1, inside, 0)

        def slab_face(k, first, count):
            inside_face = pl.ds(first * q * NY, count * q * NY)
            hx[0, k, inside_face, :] = gx5[k, inside_face, :] * hx[0, k, inside_face, :] * factor
            at = face_at(k, q, first, count)
            put(at, slab_term(level, hx.at[0], k, first, count))
            advance(at)

        slab_do(near, "wait_recv", q, raw, 0, None, True)
        slab_face(near, 0, q)
        send_near(q, d, 1)
        for number, group in enumerate(groups(q)):
            for piece in group:
                slab_do(far, "wait_recv", q, raw, 0, piece, True)
                slab_face(far, *lines(q)[piece])
            if number == 0:
                send_cross(q, d, 1)
            send_far(q, d, 1, group)
        for k in range(2):
            cross_do(k, "wait_send", q, 0, False)

            @pl.when(jnp.logical_not(sides[k][2]))
            def _(k=k):
                gx5[k] = jnp.zeros_like(gx5[k])

            @pl.when(jnp.logical_not(sides[2 + k][2]))
            def _(k=k):
                gy5[k] = jnp.zeros_like(gy5[k])

    def pick(k, values):
        out = jnp.float32(values[0])
        for n in range(1, len(values)):
            out = jnp.where(k == n, jnp.float32(values[n]), out)
        return out

    def run(level, exchange, factors, last, meanwhile=None):
        loop = len(factors) if last else len(factors) - 1

        def body(k, carry):
            a, b = pick(k, [f[0] for f in factors]), pick(k, [f[1] for f in factors])
            step(level, lax.rem(exchange + k, SLOTS), a, b, True, True)
            return carry

        lax.fori_loop(0, loop, body, 0)
        slot = (exchange + loop) % SLOTS
        if last:
            step(level, slot, 0.0, 0.0, False, False, meanwhile=meanwhile)
        else:
            step(level, slot, *factors[-1], True, False)

    def restrict(fine, coarse, qf, qc):
        table = lagrange(qf, qc)

        def body(j, carry):
            rows = [tiles(fine[pl.ds(pl.multiple_of(j * (qf * NY) + i * qf * qf * NY, NY), qf * NY), :], qf) for i in range(qf)]
            for a in range(qc):
                along = weighted(table[:, a], rows)
                for e in range(qc):
                    out = weighted(table[:, e], [along[k] for k in range(qf)])
                    work[pl.ds(pl.multiple_of(j * (qc * qc * NY) + (a * qc + e) * NY, NY), NY), :] = out
            return carry

        lax.fori_loop(0, qf, body, 0)

        def gather(a, carry):
            rows = [work[pl.ds(pl.multiple_of(a * (qc * NY) + j * qc * qc * NY, NY), qc * NY), :] for j in range(qf)]
            for b in range(qc):
                at = pl.ds(pl.multiple_of(a * (qc * qc * NY) + b * qc * NY, NY), qc * NY)
                coarse[at, :] = weighted(table[:, b], rows)
            return carry

        lax.fori_loop(0, qc, gather, 0)

    def restrict_face(slot, k, coarse, qf, qc):
        table = lagrange(qf, qc)
        lines_in = tiles(hx[slot, k, pl.ds(0, qf * qf * NY), :], qf, qf)
        weight = PENALTY[qf] * weights[k]
        for b in range(qc):
            line = weighted(table[:, b], [lines_in[j] for j in range(qf)])
            for e in range(qc):
                value = weight * weighted(table[:, e], [line[n] for n in range(qf)])
                at = pl.ds(pl.multiple_of(k * ((qc**3 - qc * qc) * NY) + (b * qc + e) * NY, NY), NY)
                coarse[at, :] = coarse[at, :] + value

    def prolong(coarse, fine, slot, sum_into, qf, qc):
        table = lagrange(qf, qc)

        def spread(a, carry):
            rows = [coarse[pl.ds(pl.multiple_of(a * (qc * qc * NY) + b * qc * NY, NY), qc * NY), :] for b in range(qc)]
            for j in range(qf):
                at = pl.ds(pl.multiple_of(a * (qc * NY) + j * qc * qc * NY, NY), qc * NY)
                work[at, :] = weighted(table[j], rows)
            return carry

        lax.fori_loop(0, qc, spread, 0)

        def body(j, carry):
            along = []
            for a in range(qc):
                at = pl.ds(pl.multiple_of(j * (qc * qc * NY) + a * qc * NY, NY), qc * NY)
                part = tiles(work[at, :], qc)
                along.append([weighted(table[k], [part[e] for e in range(qc)]) for k in range(qf)])
            for i in range(qf):
                for k in range(qf):
                    value = weighted(table[i], [along[a][k] for a in range(qc)])
                    at = pl.ds(pl.multiple_of(j * (qf * NY) + (i * qf * qf + k) * NY, NY), NY)
                    fine[slot, at, :] = value
                    sum_into[at, :] = sum_into[at, :] + value
            return carry

        lax.fori_loop(0, qf, body, 0)

    five = dict(q=Q5, d=d5, t=t5, r=res, x=sol, inv=inv5, gx=gx5, gy=gy5, product=lambda slot: product_wide(Q5, d5, slot, t5, sh5, sl5))
    three = dict(q=Q3, d=d3, t=t3, r=r3, x=x3, inv=inv3, gx=gx3, gy=gy3, product=lambda slot: product_wide(Q3, d3, slot, t3, sh3, sl3))
    one = dict(q=Q1, d=d1, t=t1, r=r1, x=x1, inv=inv1, gx=gx1, gy=gy1, product=lambda slot: product_small(d1, slot, t1))

    first, pairs = chebyshev_factors(DEGREE, LAMBDA_TOP / 8.0)
    coarse_first, coarse_pairs = chebyshev_factors(COARSE_ITERS, LAMBDA_TOP / 40.0)
    invert(Q3, inv3)
    invert(Q1, inv1)

    pack_rows(Q3, inv3, gp3)
    pack_rows(Q1, inv1, gp1)

    def greet_copy(k, n, arriving):
        here = k if arriving else k ^ 1
        if n == 0:
            src, dst = weights.at[pl.ds(2 if k < 2 else 0, 2)], gw.at[here]
        elif k < 2:
            q, inv, target = ((Q3, inv3, gx3), (Q1, inv1, gx1))[n - 1]
            src, dst = inv.at[pl.ds(k * (q**3 - q * q) * NY, q * q * NY), :], target.at[here]
        else:
            source, target = ((gp3, gy3), (gp1, gy1))[n - 1]
            src, dst = source.at[k - 2], target.at[here - 2]
        return pltpu.make_async_remote_copy(
            src_ref=src, dst_ref=dst, send_sem=gs.at[k, n], recv_sem=gr.at[here, n],
            device_id={sides[k][0]: sides[k][1]}, device_id_type=MESH,
        )

    for k in (2, 3, 0, 1):

        @pl.when(sides[k][2])
        def _(k=k):
            for n in range(3):
                greet_copy(k, n, False).start()

    opening_step(five, first, *pairs[0])

    def greeted():
        for k in range(4):

            @pl.when(sides[k][2])
            def _(k=k):
                for n in range(3):
                    greet_copy(k, n, True).wait_recv()
                    greet_copy(k, n, False).wait_send()

    run(five, 1, pairs[1:], True, lambda: restrict(res, r3, Q5, Q3))
    restrict_face(2, far, r3, Q5, Q3)
    first_update(three, 3, first, True)
    greeted()
    double_step(three, 3, *pairs, False, False)
    step(three, 5 % SLOTS, 0.0, 0.0, False, False)
    restrict(r3, r1, Q3, Q1)
    first_update(one, 6 % SLOTS, coarse_first, True)

    def coarse_rounds(n, carry):
        factors = [[pick(n, [f[part] for f in coarse_pairs[half:6:2]]) for part in range(2)] for half in range(2)]
        double_step(one, lax.rem(6 + 2 * n, SLOTS), *factors, True, False)
        return carry

    lax.fori_loop(0, 3, coarse_rounds, 0)
    finish_round(one, 12 % SLOTS, *coarse_pairs[6])
    lifted_step(one, 13 % SLOTS, three, 13 % SLOTS, first)
    double_step(three, 14 % SLOTS, *pairs, True, True)
    lifted_round(three, five, 16 % SLOTS, first)
    step(five, 17 % SLOTS, *pairs[0], True, True, settled=True)
    run(five, 18, pairs[1:], True)


def hand_out(sol, res, sol_out, res_out, done):
    rows = Q5**3 * NY // 4
    copies = [
        pltpu.make_async_copy(src.at[pl.ds(n * rows, rows), :], dst.at[pl.ds(n * rows, rows), :], done.at[k, n])
        for k, (src, dst) in enumerate(((sol, sol_out), (res, res_out))) for n in range(4)
    ]
    for copy in copies:
        copy.start()
    for copy in copies:
        copy.wait()


def per_device(right_side, coefficient, bottom_top, stiff_five, stiff_three, stiff_one):
    shape = right_side.shape
    n5, n3, n1 = Q5**3 * NY, Q3**3 * NY, Q1**3 * NY
    vmem = pl.BlockSpec(memory_space=pltpu.VMEM)
    hbm = pl.BlockSpec(memory_space=pltpu.HBM)
    field = lambda n: pltpu.VMEM((n, NZ), F32)
    slots = lambda *n: pltpu.VMEM((SLOTS, *n, NZ), F32)
    two = lambda n: pltpu.VMEM((2, n, NZ), F32)
    dma = pltpu.SemaphoreType.DMA
    sol, res = pl.pallas_call(
        kernel,
        out_shape=[jax.ShapeDtypeStruct((n5, NZ), F32)] * 2,
        in_specs=[hbm] * 6,
        out_specs=[vmem, vmem],
        scratch_shapes=[
            two(NY), pltpu.SMEM((2, NY), jnp.int32), pltpu.VMEM((Q5**3, Q5**3), F32), pltpu.VMEM((Q3**3, Q3**3), F32),
            pltpu.SMEM((Q1**3, Q1**3), F32),
            slots(n5), field(n5), field(n5),
            field(n3), field(n3), slots(n3), field(n3), field(n3),
            field(n1), field(n1), slots(n1), field(n1), field(n1),
            pltpu.VMEM((224, 224), BF16), pltpu.VMEM((224, 224), BF16),
            pltpu.VMEM((64, 64), BF16), pltpu.VMEM((64, 64), BF16),
            field(6 * 16 * NY), pltpu.VMEM((6, NY, NZ), F32),
            slots(2, Q5 * Q5 * NY), slots(2, Q5 * NY), two(Q5 * Q5 * NY), slots(2, Q5 * NY), pltpu.VMEM((4, 2, NY, NZ), F32),
            slots(4, NY), slots(4, NY), two(Q5 * NY),
            two(Q3 * Q3 * NY), two(Q1 * Q1 * NY), two(Q3 * NY), two(Q1 * NY), two(Q3 * NY), two(Q1 * NY),
            pltpu.VMEM((4, 2, NY, NZ), F32), two(Q5 * Q5 * NY), two(Q5 * NY),
            pltpu.VMEM((4, NY, NZ), F32), two(Q5 * Q5 * NY), two(Q5 * NY),
            dma((2, 4, SLOTS)), dma((2, 4, SLOTS)), dma((2, SLOTS)), dma((2, SLOTS)), dma((4, SLOTS)), dma((4, SLOTS)),
            dma((4, 3)), dma((4, 3)), dma((8,)), dma((8,)), dma((6,)),
        ],
        compiler_params=pltpu.CompilerParams(
            collective_id=0, has_side_effects=True, vmem_limit_bytes=48 * 2**20
        ),
    )(
        *(
            pltpu.with_memory_space_constraint(value, pltpu.HBM)
            for value in (
                coefficient.reshape(NY, NZ), bottom_top.reshape(2, NY), right_side.reshape(n5, NZ),
                stiff_five, stiff_three, stiff_one,
            )
        )
    )
    sol, res = pl.pallas_call(
        hand_out,
        out_shape=[jax.ShapeDtypeStruct((n5, NZ), F32)] * 2,
        in_specs=[vmem] * 2,
        out_specs=[hbm, hbm],
        scratch_shapes=[dma((2, 4))],
    )(*(pltpu.with_memory_space_constraint(value, pltpu.VMEM) for value in (sol, res)))
    return sol.reshape(shape), res.reshape(shape)


def solution(mesh):
    field = P(None, None, None, "slab", "cross", None)
    return jax.shard_map(
        per_device,
        mesh=mesh,
        in_specs=(field, P("slab", "cross", None), P(None, "slab", "cross"), P(), P(), P()),
        out_specs=(field, field),
        check_vma=False,
    )
```

```python
import functools

import jax
import jax.numpy as jnp
import numpy as np
from jax import lax
from jax.experimental import pallas as pl
from jax.experimental.pallas import tpu as pltpu
from jax.sharding import PartitionSpec as P

MESH = pl.DeviceIdType.MESH
F32 = jnp.float32
BF16 = jnp.bfloat16
Q5, Q3, Q1 = 6, 4, 2
DEGREE = 3
COARSE_ITERS = 8
LAMBDA_TOP = 2.2
NY, NZ = 8, 128
SLOTS = 4
PENALTY = {Q5: 3.0, Q3: 2.0, Q1: 1.0}


def lagrange(fine_count, coarse_count):
    fine = np.linspace(-1.0, 1.0, fine_count)
    coarse = np.linspace(-1.0, 1.0, coarse_count)
    table = np.ones((fine_count, coarse_count))
    for c in range(coarse_count):
        for o in range(coarse_count):
            if o != c:
                table[:, c] = table[:, c] * (fine - coarse[o]) / (coarse[c] - coarse[o])
    return table.astype(np.float32)


def chebyshev_factors(steps, lowest):
    center = 0.5 * (LAMBDA_TOP + lowest)
    radius = 0.5 * (LAMBDA_TOP - lowest)
    sigma = center / radius
    rho = 1.0 / sigma
    pairs = []
    for _ in range(steps - 1):
        rho_next = 1.0 / (2.0 * sigma - rho)
        pairs.append((rho_next * rho, 2.0 * rho_next / radius))
        rho = rho_next
    return 1.0 / center, pairs


def weighted(table_row, terms):
    total = None
    for value, term in zip(table_row, terms):
        if value == 0.0:
            continue
        part = term if value == 1.0 else float(value) * term
        total = part if total is None else total + part
    return total


def tiles(value, *lead):
    return value.reshape(*lead, NY, NZ)


class Unslotted:
    def __init__(self, ref):
        self.ref, self.at = ref, self

    def __getitem__(self, index):
        return self.ref.at[index[1:]]


def kernel(
    coef_in, ends_in, rhs_in, s5_in, s3_in, s1_in, sol, res,
    mine, ends, s5, s3, s1,
    d5, t5, inv5, x3, r3, d3, t3, inv3, x1, r1, d1, t1, inv1,
    sh5, sl5, sh3, sl3, work, weights, hx, hy, ytile, pack, hc,
    hd, dpack, dtile, gx3, gx1, gy3, gy1, gw, hxl, hyl, hcc, gx5, gy5,
    xs, xr, ys, yr, cs, cr, csem, crsem, load,
):
    slab, cross = lax.axis_index("slab"), lax.axis_index("cross")
    ns, nc = lax.axis_size("slab"), lax.axis_size("cross")
    sides = (
        ("slab", slab - 1, slab > 0),
        ("slab", slab + 1, slab < ns - 1),
        ("cross", cross - 1, cross > 0),
        ("cross", cross + 1, cross < nc - 1),
    )
    corners = [
        ({"slab": slab + 2 * k - 1, "cross": cross + 2 * m - 1}, sides[k][2] & sides[2 + m][2])
        for k in range(2) for m in range(2)
    ]

    for k in range(2):

        @pl.when(jnp.logical_not(sides[k][2]))
        def _(k=k):
            hc[k] = jnp.zeros_like(hc[k])
            for slot in range(SLOTS):
                hx[slot, k] = jnp.zeros_like(hx[slot, k])

        @pl.when(jnp.logical_not(sides[2 + k][2]))
        def _(k=k):
            hc[2 + k] = jnp.zeros_like(hc[2 + k])
            for slot in range(SLOTS):
                hy[slot, k] = jnp.zeros_like(hy[slot, k])

    for g in range(4):

        @pl.when(jnp.logical_not(corners[g][1]))
        def _(g=g):
            hcc[g] = jnp.zeros_like(hcc[g])
            for slot in range(SLOTS):
                hd[slot, g] = jnp.zeros_like(hd[slot, g])

    barrier = pltpu.get_barrier_semaphore()
    peers = [({axis: index}, there) for axis, index, there in sides] + corners
    for device, there in peers:

        @pl.when(there)
        def _(device=device):
            pl.semaphore_signal(barrier, inc=1, device_id=device, device_id_type=MESH)

    pairs = ((coef_in, mine.at[0]), (s5_in, s5), (s3_in, s3), (rhs_in, res), (ends_in, ends), (s1_in, s1))
    loads = [pltpu.make_async_copy(src, dst, load.at[n]) for n, (src, dst) in enumerate(pairs)]
    for copy in loads:
        copy.start()
    ytile[...] = jnp.zeros_like(ytile)
    dtile[...] = jnp.zeros_like(dtile)
    for copy in loads:
        copy.wait()

    row = lax.broadcasted_iota(jnp.int32, (NY, NZ), 0)
    lane = lax.broadcasted_iota(jnp.int32, (NY, NZ), 1)
    bottom = jnp.zeros((NY, NZ), F32)
    top = jnp.zeros((NY, NZ), F32)
    for y in range(NY):
        bottom = jnp.where(row == y, ends[0, y].astype(F32), bottom)
        top = jnp.where(row == y, ends[1, y].astype(F32), top)
    mine[1] = jnp.where(lane == 0, bottom, jnp.where(lane == NZ - 1, top, 0.0))

    far = lax.rem(slab, 2)
    near = 1 - far

    def lines(q):
        if q < Q5:
            return [(0, q)]
        return [(0, 1), (q - 1, 1)] + [(j, min(2, q - 1 - j)) for j in range(1, q - 1, 2)]

    def groups(q):
        count = len(lines(q))
        return [[0, 1]] + [[n] for n in range(2, count)] if count > 1 else [[0]]

    def face_at(k, q, first, count):
        return pl.ds(pl.multiple_of(k * ((q**3 - q * q) * NY) + first * q * NY, NY), count * q * NY)

    def slab_copy(k, q, d, slot, piece, arriving):
        first, count = (0, q) if piece is None else lines(q)[piece]
        number = 0 if piece is None else piece
        here = k if arriving else 1 - k
        return pltpu.make_async_remote_copy(
            src_ref=d.at[slot, face_at(k, q, first, count), :],
            dst_ref=hx.at[slot, here, pl.ds(first * q * NY, count * q * NY), :],
            send_sem=xs.at[k, number, slot], recv_sem=xr.at[here, number, slot],
            device_id={"slab": slab + 2 * k - 1}, device_id_type=MESH,
        )

    def cross_copy(k, q, slot, arriving):
        here = k if arriving else k ^ 1
        return pltpu.make_async_remote_copy(
            src_ref=pack.at[slot, k, pl.ds(0, q * NY), :], dst_ref=hy.at[slot, here, pl.ds(0, q * NY), :],
            send_sem=ys.at[k, slot], recv_sem=yr.at[here, slot],
            device_id={"cross": sides[2 + k][1]}, device_id_type=MESH,
        )

    def slab_do(k, method, *args):
        index = slab + 2 * k - 1

        @pl.when((index >= 0) & (index < ns))
        def _():
            getattr(slab_copy(k, *args), method)()

    def cross_do(k, method, *args):
        @pl.when(sides[2 + k][2])
        def _():
            getattr(cross_copy(k, *args), method)()

    def send_near(q, d, slot):
        slab_do(near, "start", q, d, slot, None, False)

    def send_far(q, d, slot, pieces):
        for piece in pieces:
            slab_do(far, "start", q, d, slot, piece, False)

    def send_cross(q, d, slot):
        for i in range(q):
            pack[slot, 0, pl.ds(i * NY, q), :] = d[slot, pl.ds(i * q * q * NY, q, stride=NY), :]
            pack[slot, 1, pl.ds(i * NY, q), :] = d[slot, pl.ds((i * q * q + q * (q - 1)) * NY + NY - 1, q, stride=NY), :]
        for k in range(2):
            cross_do(k, "start", q, slot, False)

    def corner_copy(g, slot, arriving):
        here = g if arriving else 3 - g
        return pltpu.make_async_remote_copy(
            src_ref=dpack.at[slot, g], dst_ref=hd.at[slot, here],
            send_sem=cs.at[g, slot], recv_sem=cr.at[here, slot],
            device_id=corners[g][0], device_id_type=MESH,
        )

    def corner_do(g, method, *args):
        @pl.when(corners[g][1])
        def _():
            getattr(corner_copy(g, *args), method)()

    def send_corners(q, d, slot):
        for g in range(4):
            k, m = g // 2, g % 2
            node = k * (q**3 - q * q) + m * (q * q - q)
            dpack[slot, g, pl.ds(0, q), :] = d[slot, pl.ds(node * NY + m * (NY - 1), q, stride=NY), :]
        for g in range(4):
            corner_do(g, "start", slot, False)

    def send_all(q, d, slot, with_corners):
        if with_corners:
            send_corners(q, d, slot)
        send_cross(q, d, slot)
        send_near(q, d, slot)
        send_far(q, d, slot, range(len(lines(q))))

    def arrived_cross(q, slot):
        for k in range(2):
            cross_do(k, "wait_recv", q, slot, True)

    def arrived_slab(q, d, slot):
        slab_do(near, "wait_recv", q, d, slot, None, True)
        for piece in range(len(lines(q))):
            slab_do(far, "wait_recv", q, d, slot, piece, True)

    def arrived_corners(slot):
        for g in range(4):
            corner_do(g, "wait_recv", slot, True)

    def sent(q, d, slot, with_corners):
        slab_do(near, "wait_send", q, d, slot, None, False)
        for piece in range(len(lines(q))):
            slab_do(far, "wait_send", q, d, slot, piece, False)
        for k in range(2):
            cross_do(k, "wait_send", q, slot, False)
        if with_corners:
            for g in range(4):
                corner_do(g, "wait_send", slot, False)

    def pack_rows(q, source, target):
        for i in range(q):
            target[0, pl.ds(i * NY, q), :] = source[pl.ds(i * q * q * NY, q, stride=NY), :]
            target[1, pl.ds(i * NY, q), :] = source[pl.ds((i * q * q + q * (q - 1)) * NY + NY - 1, q, stride=NY), :]

    pack_rows(Q5, res, pack.at[0])
    pl.semaphore_wait(barrier, sum(there.astype(jnp.int32) for _, there in peers))

    def coef_copy(k, arriving):
        if k < 4:
            here = k if arriving else k ^ 1
            src, dst = mine, hc.at[here]
        else:
            here = k if arriving else 11 - k
            src, dst = mine.at[0], hcc.at[here - 4]
        return pltpu.make_async_remote_copy(
            src_ref=src, dst_ref=dst, send_sem=csem.at[k], recv_sem=crsem.at[here],
            device_id=peers[k][0], device_id_type=MESH,
        )

    for k in (2, 3, 0, 1, 4, 5, 6, 7):

        @pl.when(peers[k][1])
        def _(k=k):
            coef_copy(k, False).start()

    raw = Unslotted(res)
    for k in range(2):
        cross_do(k, "start", Q5, 0, False)
    send_near(Q5, raw, 0)
    send_far(Q5, raw, 0, range(len(lines(Q5))))

    def split(table, high, low, count):
        value = table[...]
        high[...] = jnp.zeros_like(high)
        low[...] = jnp.zeros_like(low)
        top = value.astype(BF16)
        high[pl.ds(0, count), pl.ds(0, count)] = top
        low[pl.ds(0, count), pl.ds(0, count)] = (value - top.astype(F32)).astype(BF16)

    split(s5, sh5, sl5, Q5**3)
    split(s3, sh3, sl3, Q3**3)

    def spread_diagonal(table, inv, count):
        value = table[...]
        same = lax.broadcasted_iota(jnp.int32, value.shape, 0) == lax.broadcasted_iota(jnp.int32, value.shape, 1)
        column = jnp.sum(jnp.where(same, value, 0.0), axis=1, keepdims=True)
        wide = jnp.broadcast_to(column, (count, NZ))
        for y in range(NY):
            inv[pl.ds(y, count, stride=NY), :] = wide

    spread_diagonal(s5, inv5, Q5**3)
    spread_diagonal(s3, inv3, Q3**3)
    for n in range(Q1**3):
        inv1[pl.ds(n * NY, NY), :] = jnp.full((NY, NZ), s1[n, n])
    for q, inv, gx, gy in ((Q5, inv5, gx5, gy5), (Q3, inv3, gx3, gy3), (Q1, inv1, gx1, gy1)):
        for k in range(2):
            gx[k] = inv[face_at(1 - k, q, 0, q), :]
            for i in range(q):
                node = i * q * q + (1 - k) * q * (q - 1)
                gy[k, pl.ds(i * NY, q), :] = inv[pl.ds(node * NY, q, stride=NY), :]

    def coefs_done(ks):
        for k in ks:

            @pl.when(peers[k][1])
            def _(k=k):
                coef_copy(k, True).wait_recv()
                coef_copy(k, False).wait_send()

    coefs_done(range(4))
    c = mine[0]

    def cross_weights(own, below, above):
        before = jnp.where(row == 0, pltpu.roll(below, 1, 0), pltpu.roll(own, 1, 0))
        after = jnp.where(row == NY - 1, pltpu.roll(above, NY - 1, 0), pltpu.roll(own, NY - 1, 0))
        return 0.5 * (own + before), 0.5 * (own + after)

    def end_weights(own, flags):
        low = jnp.where(lane == 0, flags * own, 0.5 * (own + pltpu.roll(own, 1, 1)))
        high = jnp.where(lane == NZ - 1, flags * own, 0.5 * (own + pltpu.roll(own, NZ - 1, 1)))
        return low, high

    weights[0] = 0.5 * (c + hc[0, 0])
    weights[1] = 0.5 * (c + hc[1, 0])
    weights[2], weights[3] = cross_weights(c, hc[2, 0], hc[3, 0])
    weights[4], weights[5] = end_weights(c, mine[1])

    def ends_added(base, q, y_pair, z_pair):
        first = base[0:1] + y_pair[0][None]
        last = base[q - 1 : q] + y_pair[1][None]
        base = jnp.concatenate([first, base[1 : q - 1], last] if q > 2 else [first, last], 0)
        first = base[:, 0:1] + z_pair[0][:, None]
        last = base[:, q - 1 : q] + z_pair[1][:, None]
        return jnp.concatenate([first, base[:, 1 : q - 1], last] if q > 2 else [first, last], 1)

    def slab_weight(i, q):
        return jnp.where(i == 0, PENALTY[q] * weights[0], 0.0) + jnp.where(i == q - 1, PENALTY[q] * weights[1], 0.0)

    def plane_at(i, q):
        return pl.ds(pl.multiple_of(i * (q * q * NY), NY), q * q * NY)

    def invert(q, inv):
        yl, yh, zl, zh = (jnp.broadcast_to(PENALTY[q] * weights[k], (q, NY, NZ)) for k in range(2, 6))

        def body(i, carry):
            at = plane_at(i, q)
            base = tiles(inv[at, :], q, q) * c + slab_weight(i, q)
            base = ends_added(base, q, (yl, yh), (zl, zh))
            inv[at, :] = (1.0 / base).reshape(q * q * NY, NZ)
            return carry

        lax.fori_loop(0, q, body, 0)

    invert(Q5, inv5)

    def product_wide(q, d, slot, t, high, low):
        count = q**3
        padded = high.shape[0]
        s_high, s_low = high[...], low[...]
        for y in range(0, NY, 2):
            pair = [d[slot, pl.ds(y + h, count, stride=NY), :] for h in range(2)]
            v = jnp.concatenate(pair, 1)
            if padded > count:
                v = jnp.concatenate([v, jnp.zeros((padded - count, 2 * NZ), F32)], 0)
            v_high = v.astype(BF16)
            v_low = (v - v_high.astype(F32)).astype(BF16)
            out = jnp.dot(s_high, v_high, preferred_element_type=F32)
            out += jnp.dot(s_high, v_low, preferred_element_type=F32)
            out += jnp.dot(s_low, v_high, preferred_element_type=F32)
            for h in range(2):
                t[pl.ds(y + h, count, stride=NY), :] = out[:count, h * NZ : (h + 1) * NZ]

    def product_small(d, slot, t):
        count = Q1**3
        parts = [d[slot, pl.ds(n * NY, NY), :] for n in range(count)]
        for m in range(count):
            total = s1[m, 0] * parts[0]
            for n in range(1, count):
                total += s1[m, n] * parts[n]
            t[pl.ds(m * NY, NY), :] = total

    def local_part(level, slot):
        q, d, t, r = (level[name] for name in ("q", "d", "t", "r"))
        p = PENALTY[q]
        level["product"](slot)

        def local(i, carry):
            yl, yh, zl, zh = (p * weights[k] for k in range(2, 6))
            at = plane_at(i, q)
            dv = tiles(d[slot, at, :], q, q)
            lo, hi = dv[0], dv[q - 1]
            y_pair = (
                yl * (lo - jnp.where(row == 0, 0.0, pltpu.roll(hi, 1, 1))),
                yh * (hi - jnp.where(row == NY - 1, 0.0, pltpu.roll(lo, NY - 1, 1))),
            )
            lo, hi = dv[:, 0], dv[:, q - 1]
            z_pair = (
                zl * (lo - jnp.where(lane == 0, 0.0, pltpu.roll(hi, 1, 2))),
                zh * (hi - jnp.where(lane == NZ - 1, 0.0, pltpu.roll(lo, NZ - 1, 2))),
            )
            total = ends_added(tiles(t[at, :], q, q) * c, q, y_pair, z_pair)
            r[at, :] = r[at, :] - total.reshape(q * q * NY, NZ)
            return carry

        lax.fori_loop(0, q, local, 0)
        face = q * q * NY
        for k in range(2):
            at = pl.ds(0 if k == 0 else (q**3) * NY - face, face)
            r[at, :] = r[at, :] - (p * weights[k] * tiles(d[slot, at, :], q * q)).reshape(face, NZ)

    def rims(level, source, put):
        q = level["q"]
        for i in range(q):
            ytile[0, pl.ds(i * q * NY, q, stride=NY), :] = source[0, pl.ds(i * NY, q), :]
            ytile[1, pl.ds(i * q * NY + NY - 1, q, stride=NY), :] = source[1, pl.ds(i * NY, q), :]

        def rim(i, carry):
            for k in range(2):
                at = pl.ds(pl.multiple_of(i * (q * q * NY) + k * q * (q - 1) * NY, NY), q * NY)
                part = PENALTY[q] * weights[2 + k] * tiles(ytile[k, pl.ds(pl.multiple_of(i * (q * NY), NY), q * NY), :], q)
                put(at, part.reshape(q * NY, NZ))
            return carry

        lax.fori_loop(0, q, rim, 0)

    def slab_term(level, source, k, first, count):
        q = level["q"]
        part = PENALTY[q] * weights[k] * tiles(source[k, pl.ds(first * q * NY, count * q * NY), :], count * q)
        return part.reshape(count * q * NY, NZ)

    def step(level, slot, a, b, update, send, settled=False, meanwhile=None):
        q, d, r, x, inv = (level[name] for name in ("q", "d", "r", "x", "inv"))
        other = lax.rem(slot + 1, SLOTS)

        def put(at, part):
            r[at, :] = r[at, :] + part

        local_part(level, slot)
        for k in range(2):
            cross_do(k, "wait_recv", q, slot, True)
        rims(level, hy.at[slot], put)

        def advance(at):
            value = a * d[slot, at, :] + b * inv[at, :] * r[at, :]
            d[other, at, :] = value
            x[at, :] = x[at, :] + value

        if update and q > 2:

            def inside(i, carry):
                advance(plane_at(i, q))
                return carry

            lax.fori_loop(1, q - 1, inside, 0)

        def slab_face(k, first, count):
            at = face_at(k, q, first, count)
            put(at, slab_term(level, hx.at[slot], k, first, count))
            if update:
                advance(at)

        slab_do(near, "wait_recv", q, d, slot, None, True)
        slab_face(near, 0, q)
        if send:
            send_near(q, d, other)
        if meanwhile is not None:
            meanwhile()
        for number, group in enumerate(groups(q)):
            for piece in group:
                slab_do(far, "wait_recv", q, d, slot, piece, True)
                slab_face(far, *lines(q)[piece])
            if send:
                if number == 0:
                    send_cross(q, d, other)
                send_far(q, d, other, group)
        if not settled:
            sent(q, d, slot, False)

    def correct(level, slot, rows, b, slab_put, cross_put):
        q, d, gx, gy = (level[name] for name in ("q", "d", "gx", "gy"))
        p = PENALTY[q]
        face = q * q * NY
        for k in range(2):
            for m in range(2):
                dtile[m, pl.ds(m * (NY - 1), q, stride=NY), :] = hd[slot, 2 * k + m, pl.ds(0, q), :]
            term = p * weights[k] * tiles(d[slot, pl.ds(k * (q**3 - q * q) * NY, face), :], q, q)
            low, high = (p * gw[k, m] * tiles(dtile[m, pl.ds(0, q * NY), :], q) for m in range(2))
            first, last = term[0:1] + low[None], term[q - 1 : q] + high[None]
            term = jnp.concatenate([first, term[1 : q - 1], last] if q > 2 else [first, last], 0)
            at = pl.ds(0, face)
            slab_put(k, at, b * gx[k, at, :] * term.reshape(face, NZ))
        for m in range(2):
            here, theirs = pl.ds(m * (NY - 1), 1), pl.ds((1 - m) * (NY - 1), 1)
            for i in range(q):
                at = pl.ds(i * NY, q)
                term = p * weights[2 + m, here, :] * rows[m, at, :]
                for k in range(2):
                    if i == k * (q - 1):
                        term = term + p * gw[2 + m, k, theirs, :] * hd[slot, 2 * k + m, pl.ds(0, q), :]
                cross_put(m, at, b * gy[m, at, :] * term)

    def planes(q, body):
        def one_plane(i, carry):
            body(plane_at(i, q))
            return carry

        lax.fori_loop(0, q, one_plane, 0)

    def half_round(level, slot, a, b, total):
        q, d, r, x, inv = (level[name] for name in ("q", "d", "r", "x", "inv"))
        other = lax.rem(slot + 1, SLOTS)

        def partial_next(at):
            value = a * d[slot, at, :] + b * inv[at, :] * r[at, :]
            d[other, at, :] = x[at, :] + value if total else value

        def put_both(at, part):
            r[at, :] = r[at, :] + part
            d[other, at, :] = d[other, at, :] + b * inv[at, :] * part

        local_part(level, slot)
        planes(q, partial_next)
        send_all(q, d, other, False)
        arrived_cross(q, slot)
        sent(q, d, other, False)
        rims(level, hy.at[slot], put_both)
        arrived_slab(q, d, slot)
        for k in range(2):
            put_both(face_at(k, q, 0, q), slab_term(level, hx.at[slot], k, 0, q))

    def keep_slab(k, at, part):
        hxl[k, at, :] = part

    def keep_cross(m, at, part):
        hyl[m, at, :] = part

    def double_step(level, slot, first, second, with_corners, total):
        q, d, r, x, inv = (level[name] for name in ("q", "d", "r", "x", "inv"))
        other, third = lax.rem(slot + 1, SLOTS), lax.rem(slot + 2, SLOTS)

        def put(at, part):
            r[at, :] = r[at, :] + part

        def add(at):
            x[at, :] = x[at, :] + d[other, at, :]

        def advance(at):
            value = second[0] * d[other, at, :] + second[1] * inv[at, :] * r[at, :]
            if total:
                d[third, at, :] = x[at, :] + value
            else:
                d[third, at, :] = value
                x[at, :] = x[at, :] + value

        half_round(level, slot, *first, False)
        planes(q, add)
        local_part(level, other)
        arrived_corners(slot)

        correct(level, slot, pack.at[slot], first[1], keep_slab, keep_cross)
        rims(level, hyl, put)
        for k in range(2):
            put(face_at(k, q, 0, q), slab_term(level, hxl, k, 0, q))
        arrived_cross(q, other)
        rims(level, hy.at[other], put)
        arrived_slab(q, d, other)
        for k in range(2):
            put(face_at(k, q, 0, q), slab_term(level, hx.at[other], k, 0, q))
        planes(q, advance)
        send_all(q, d, third, with_corners)
        sent(q, d, slot, True)

    def finish_round(level, slot, a, b):
        q, d = level["q"], level["d"]
        other = lax.rem(slot + 1, SLOTS)
        half_round(level, slot, a, b, True)
        arrived_corners(slot)
        arrived_cross(q, other)
        arrived_slab(q, d, other)

        def add_slab(k, at, part):
            hx[other, k, at, :] = hx[other, k, at, :] + part

        def add_cross(m, at, part):
            hy[other, m, at, :] = hy[other, m, at, :] + part

        correct(level, slot, pack.at[slot], b, add_slab, add_cross)
        sent(q, d, slot, True)

    def lift_slab(qc, qf, slot):
        table = lagrange(qf, qc)
        for k in range(2):
            lines_in = tiles(hx[slot, k, pl.ds(0, qc * qc * NY), :], qc, qc)
            for j in range(qf):
                line = weighted(table[j], [lines_in[n] for n in range(qc)])
                for n in range(qf):
                    hxl[k, pl.ds((j * qf + n) * NY, NY), :] = weighted(table[n], [line[e] for e in range(qc)])

    def spread_table(qc, qf):
        table = lagrange(qf, qc)
        spread = []
        for e in range(qc):
            column = jnp.zeros((NY, NZ), F32)
            for n in range(qf):
                if table[n, e] != 0.0:
                    column = jnp.where(row == n, float(table[n, e]), column)
            spread.append(column)
        return spread

    def lift_line(spread, line):
        value = spread[0] * line[0:1]
        for e in range(1, len(spread)):
            value = value + spread[e] * line[e : e + 1]
        return value

    def lift_cross(qc, qf, slot):
        table, spread = lagrange(qf, qc), spread_table(qc, qf)
        for k in range(2):
            for i in range(qf):
                line = weighted(table[i], [hy[slot, k, pl.ds(a * NY, qc), :] for a in range(qc)])
                hyl[k, pl.ds(i * NY, NY), :] = lift_line(spread, line)

    def lift_corners(qc, qf, slot):
        spread = spread_table(qc, qf)
        for g in range(4):
            hd[slot, g] = lift_line(spread, hd[slot, g])

    def lifted_step(coarse, slot, level, here, factor):
        q, d, r, x, inv = (level[name] for name in ("q", "d", "r", "x", "inv"))
        following = (here + 1) % SLOTS
        prolong(coarse["d"].at[slot], d, here, x, q, coarse["q"])
        local_part(level, here)
        lift_cross(coarse["q"], q, slot)
        lift_slab(coarse["q"], q, slot)

        def put(at, part):
            r[at, :] = r[at, :] + part

        def advance(at):
            value = factor * inv[at, :] * r[at, :]
            d[following, at, :] = value
            x[at, :] = x[at, :] + value

        rims(level, hyl, put)
        for k in range(2):
            put(face_at(k, q, 0, q), slab_term(level, hxl, k, 0, q))
        planes(q, advance)
        send_all(q, d, following, True)

    def lifted_round(coarse, level, here, factor):
        q, d, r, x, inv = (level[name] for name in ("q", "d", "r", "x", "inv"))
        qc, other, spare = coarse["q"], (here + 1) % SLOTS, (here + 3) % SLOTS

        def partial_next(at):
            d[other, at, :] = factor * inv[at, :] * r[at, :]

        def put(at, part):
            r[at, :] = r[at, :] + part

        def put_both(at, part):
            r[at, :] = r[at, :] + part
            d[other, at, :] = d[other, at, :] + factor * inv[at, :] * part

        def add(at):
            x[at, :] = x[at, :] + d[other, at, :]

        prolong(coarse["d"].at[here], d, here, x, q, qc)
        local_part(level, here)
        planes(q, partial_next)
        send_all(q, d, other, False)
        pack_rows(q, d.at[here], pack.at[spare])
        arrived_cross(qc, here)
        lift_cross(qc, q, here)
        arrived_slab(qc, coarse["d"], here)
        lift_slab(qc, q, here)
        sent(q, d, other, False)
        rims(level, hyl, put_both)
        for k in range(2):
            put_both(face_at(k, q, 0, q), slab_term(level, hxl, k, 0, q))
        planes(q, add)
        arrived_corners(here)
        lift_corners(qc, q, here)
        correct(level, here, pack.at[spare], factor, keep_slab, keep_cross)
        rims(level, hyl, put)
        for k in range(2):
            put(face_at(k, q, 0, q), slab_term(level, hxl, k, 0, q))
        sent(qc, coarse["d"], here, True)

    def first_update(level, slot, factor, with_corners):
        q, d, x, r, inv = (level[name] for name in ("q", "d", "x", "r", "inv"))

        def body(i, carry):
            at = plane_at(i, q)
            value = inv[at, :] * r[at, :] * factor
            d[slot, at, :] = value
            x[at, :] = value
            return carry

        lax.fori_loop(0, q, body, 0)
        send_all(q, d, slot, with_corners)

    def neighbours_inverse(q, gx, gy):
        p = PENALTY[q]
        for k in range(2):
            own = hc[k, 0]
            y_pair, z_pair = (
                [jnp.broadcast_to(p * w, (q, NY, NZ)) for w in pair] for pair in ((gw[k, 0], gw[k, 1]), end_weights(own, hc[k, 1]))
            )
            base = ends_added(tiles(gx[k], q, q) * own + p * weights[k], q, y_pair, z_pair)
            gx[k] = (1.0 / base).reshape(q * q * NY, NZ)
        node = lax.broadcasted_iota(jnp.int32, (q, NZ), 0)
        for m in range(2):
            here, theirs = m * (NY - 1), (1 - m) * (NY - 1)
            low, high = (w[theirs : theirs + 1] for w in end_weights(hc[2 + m, 0], hc[2 + m, 1]))
            own = hc[2 + m, 0, pl.ds(theirs, 1), :]
            across = p * weights[2 + m, pl.ds(here, 1), :]
            along = p * (jnp.where(node == 0, low, 0.0) + jnp.where(node == q - 1, high, 0.0))
            for i in range(q):
                at = pl.ds(i * NY, q)
                base = gy[m, at, :] * own + across + along
                for k in range(2):
                    if i == k * (q - 1):
                        base = base + p * gw[2 + m, k, pl.ds(theirs, 1), :]
                gy[m, at, :] = 1.0 / base

    def zero_missing(gx, gy):
        for k in range(2):

            @pl.when(jnp.logical_not(sides[k][2]))
            def _(k=k):
                gx[k] = jnp.zeros_like(gx[k])

            @pl.when(jnp.logical_not(sides[2 + k][2]))
            def _(k=k):
                gy[k] = jnp.zeros_like(gy[k])

    def opening_step(level, factor, a, b):
        q, d, r, x, inv = (level[name] for name in ("q", "d", "r", "x", "inv"))
        p = PENALTY[q]

        def start(at):
            value = inv[at, :] * r[at, :] * factor
            d[0, at, :] = value
            x[at, :] = value

        def put(at, part):
            r[at, :] = r[at, :] + part

        def advance(at):
            value = a * d[0, at, :] + b * inv[at, :] * r[at, :]
            d[1, at, :] = value
            x[at, :] = x[at, :] + value

        planes(q, start)
        slab_do(near, "wait_send", q, raw, 0, None, False)
        for piece in range(len(lines(q))):
            slab_do(far, "wait_send", q, raw, 0, piece, False)
        local_part(level, 0)
        coefs_done(range(4, 8))
        for k in range(2):
            gw[k, 0], gw[k, 1] = cross_weights(hc[k, 0], hcc[2 * k], hcc[2 * k + 1])
            for m in range(2):
                gw[2 + m, k] = 0.5 * (hc[2 + m, 0] + hcc[2 * k + m])
        neighbours_inverse(q, gx5, gy5)
        for k in range(2):
            cross_do(k, "wait_recv", q, 0, True)
        for m in range(2):
            for i in range(q):
                at = pl.ds(i * NY, q)
                hy[0, m, at, :] = gy5[m, at, :] * hy[0, m, at, :] * factor
        rims(level, hy.at[0], put)

        def inside(i, carry):
            advance(plane_at(i, q))
            return carry

        lax.fori_loop(1, q - 1, inside, 0)

        def slab_face(k, first, count):
            inside_face = pl.ds(first * q * NY, count * q * NY)
            hx[0, k, inside_face, :] = gx5[k, inside_face, :] * hx[0, k, inside_face, :] * factor
            at = face_at(k, q, first, count)
            put(at, slab_term(level, hx.at[0], k, first, count))
            advance(at)

        slab_do(near, "wait_recv", q, raw, 0, None, True)
        slab_face(near, 0, q)
        send_near(q, d, 1)
        for number, group in enumerate(groups(q)):
            for piece in group:
                slab_do(far, "wait_recv", q, raw, 0, piece, True)
                slab_face(far, *lines(q)[piece])
            if number == 0:
                send_cross(q, d, 1)
            send_far(q, d, 1, group)
        for k in range(2):
            cross_do(k, "wait_send", q, 0, False)
        zero_missing(gx5, gy5)

    def pick(k, values):
        out = jnp.float32(values[0])
        for n in range(1, len(values)):
            out = jnp.where(k == n, jnp.float32(values[n]), out)
        return out

    def run(level, exchange, factors, last):
        loop = len(factors) if last else len(factors) - 1

        def body(k, carry):
            a, b = pick(k, [f[0] for f in factors]), pick(k, [f[1] for f in factors])
            step(level, lax.rem(exchange + k, SLOTS), a, b, True, True)
            return carry

        lax.fori_loop(0, loop, body, 0)
        slot = (exchange + loop) % SLOTS
        if last:
            step(level, slot, 0.0, 0.0, False, False)
        else:
            step(level, slot, *factors[-1], True, False)

    def restrict(fine, coarse, qf, qc):
        table = lagrange(qf, qc)

        def body(j, carry):
            rows = [tiles(fine[pl.ds(pl.multiple_of(j * (qf * NY) + i * qf * qf * NY, NY), qf * NY), :], qf) for i in range(qf)]
            for a in range(qc):
                along = weighted(table[:, a], rows)
                for e in range(qc):
                    out = weighted(table[:, e], [along[k] for k in range(qf)])
                    work[pl.ds(pl.multiple_of(j * (qc * qc * NY) + (a * qc + e) * NY, NY), NY), :] = out
            return carry

        lax.fori_loop(0, qf, body, 0)

        def gather(a, carry):
            rows = [work[pl.ds(pl.multiple_of(a * (qc * NY) + j * qc * qc * NY, NY), qc * NY), :] for j in range(qf)]
            for b in range(qc):
                at = pl.ds(pl.multiple_of(a * (qc * qc * NY) + b * qc * NY, NY), qc * NY)
                coarse[at, :] = weighted(table[:, b], rows)
            return carry

        lax.fori_loop(0, qc, gather, 0)

    def restrict_face(slot, k, coarse, qf, qc):
        table = lagrange(qf, qc)
        lines_in = tiles(hx[slot, k, pl.ds(0, qf * qf * NY), :], qf, qf)
        weight = PENALTY[qf] * weights[k]
        for b in range(qc):
            line = weighted(table[:, b], [lines_in[j] for j in range(qf)])
            for e in range(qc):
                value = weight * weighted(table[:, e], [line[n] for n in range(qf)])
                at = pl.ds(pl.multiple_of(k * ((qc**3 - qc * qc) * NY) + (b * qc + e) * NY, NY), NY)
                coarse[at, :] = coarse[at, :] + value

    def prolong(coarse, fine, slot, sum_into, qf, qc):
        table = lagrange(qf, qc)

        def spread(a, carry):
            rows = [coarse[pl.ds(pl.multiple_of(a * (qc * qc * NY) + b * qc * NY, NY), qc * NY), :] for b in range(qc)]
            for j in range(qf):
                at = pl.ds(pl.multiple_of(a * (qc * NY) + j * qc * qc * NY, NY), qc * NY)
                work[at, :] = weighted(table[j], rows)
            return carry

        lax.fori_loop(0, qc, spread, 0)

        def body(j, carry):
            along = []
            for a in range(qc):
                at = pl.ds(pl.multiple_of(j * (qc * qc * NY) + a * qc * NY, NY), qc * NY)
                part = tiles(work[at, :], qc)
                along.append([weighted(table[k], [part[e] for e in range(qc)]) for k in range(qf)])
            for i in range(qf):
                for k in range(qf):
                    value = weighted(table[i], [along[a][k] for a in range(qc)])
                    at = pl.ds(pl.multiple_of(j * (qf * NY) + (i * qf * qf + k) * NY, NY), NY)
                    fine[slot, at, :] = value
                    sum_into[at, :] = sum_into[at, :] + value
            return carry

        lax.fori_loop(0, qf, body, 0)

    five = dict(q=Q5, d=d5, t=t5, r=res, x=sol, inv=inv5, gx=gx5, gy=gy5, product=lambda slot: product_wide(Q5, d5, slot, t5, sh5, sl5))
    three = dict(q=Q3, d=d3, t=t3, r=r3, x=x3, inv=inv3, gx=gx3, gy=gy3, product=lambda slot: product_wide(Q3, d3, slot, t3, sh3, sl3))
    one = dict(q=Q1, d=d1, t=t1, r=r1, x=x1, inv=inv1, gx=gx1, gy=gy1, product=lambda slot: product_small(d1, slot, t1))

    first, pairs = chebyshev_factors(DEGREE, LAMBDA_TOP / 8.0)
    coarse_first, coarse_pairs = chebyshev_factors(COARSE_ITERS, LAMBDA_TOP / 40.0)
    opening_step(five, first, *pairs[0])

    def prepare():
        invert(Q3, inv3)
        invert(Q1, inv1)
        for q, gx, gy in ((Q3, gx3, gy3), (Q1, gx1, gy1)):
            neighbours_inverse(q, gx, gy)
            zero_missing(gx, gy)

    step(five, 1, *pairs[1], True, True, meanwhile=prepare)
    step(five, 2, 0.0, 0.0, False, False, meanwhile=lambda: restrict(res, r3, Q5, Q3))
    restrict_face(2, far, r3, Q5, Q3)
    first_update(three, 3, first, True)
    double_step(three, 3, *pairs, False, False)
    step(three, 5 % SLOTS, 0.0, 0.0, False, False)
    restrict(r3, r1, Q3, Q1)
    first_update(one, 6 % SLOTS, coarse_first, True)

    def coarse_rounds(n, carry):
        factors = [[pick(n, [f[part] for f in coarse_pairs[half:6:2]]) for part in range(2)] for half in range(2)]
        double_step(one, lax.rem(6 + 2 * n, SLOTS), *factors, True, False)
        return carry

    lax.fori_loop(0, 3, coarse_rounds, 0)
    finish_round(one, 12 % SLOTS, *coarse_pairs[6])
    lifted_step(one, 13 % SLOTS, three, 13 % SLOTS, first)
    double_step(three, 14 % SLOTS, *pairs, True, True)
    lifted_round(three, five, 16 % SLOTS, first)
    step(five, 17 % SLOTS, *pairs[0], True, True, settled=True)
    run(five, 18, pairs[1:], True)


def hand_out(sol, res, sol_out, res_out, done):
    rows = Q5**3 * NY // 4
    copies = [
        pltpu.make_async_copy(src.at[pl.ds(n * rows, rows), :], dst.at[pl.ds(n * rows, rows), :], done.at[k, n])
        for k, (src, dst) in enumerate(((sol, sol_out), (res, res_out))) for n in range(4)
    ]
    for copy in copies:
        copy.start()
    for copy in copies:
        copy.wait()


def per_device(right_side, coefficient, bottom_top, stiff_five, stiff_three, stiff_one):
    shape = right_side.shape
    n5, n3, n1 = Q5**3 * NY, Q3**3 * NY, Q1**3 * NY
    vmem = pl.BlockSpec(memory_space=pltpu.VMEM)
    hbm = pl.BlockSpec(memory_space=pltpu.HBM)
    field = lambda n: pltpu.VMEM((n, NZ), F32)
    slots = lambda *n: pltpu.VMEM((SLOTS, *n, NZ), F32)
    two = lambda n: pltpu.VMEM((2, n, NZ), F32)
    dma = pltpu.SemaphoreType.DMA
    sol, res = pl.pallas_call(
        kernel,
        out_shape=[jax.ShapeDtypeStruct((n5, NZ), F32)] * 2,
        in_specs=[hbm] * 6,
        out_specs=[vmem, vmem],
        scratch_shapes=[
            two(NY), pltpu.SMEM((2, NY), jnp.int32), pltpu.VMEM((Q5**3, Q5**3), F32), pltpu.VMEM((Q3**3, Q3**3), F32),
            pltpu.SMEM((Q1**3, Q1**3), F32),
            slots(n5), field(n5), field(n5),
            field(n3), field(n3), slots(n3), field(n3), field(n3),
            field(n1), field(n1), slots(n1), field(n1), field(n1),
            pltpu.VMEM((224, 224), BF16), pltpu.VMEM((224, 224), BF16),
            pltpu.VMEM((64, 64), BF16), pltpu.VMEM((64, 64), BF16),
            field(6 * 16 * NY), pltpu.VMEM((6, NY, NZ), F32),
            slots(2, Q5 * Q5 * NY), slots(2, Q5 * NY), two(Q5 * Q5 * NY), slots(2, Q5 * NY), pltpu.VMEM((4, 2, NY, NZ), F32),
            slots(4, NY), slots(4, NY), two(Q5 * NY),
            two(Q3 * Q3 * NY), two(Q1 * Q1 * NY), two(Q3 * NY), two(Q1 * NY),
            pltpu.VMEM((4, 2, NY, NZ), F32), two(Q5 * Q5 * NY), two(Q5 * NY),
            pltpu.VMEM((4, NY, NZ), F32), two(Q5 * Q5 * NY), two(Q5 * NY),
            dma((2, 4, SLOTS)), dma((2, 4, SLOTS)), dma((2, SLOTS)), dma((2, SLOTS)), dma((4, SLOTS)), dma((4, SLOTS)),
            dma((8,)), dma((8,)), dma((6,)),
        ],
        compiler_params=pltpu.CompilerParams(
            collective_id=0, has_side_effects=True, vmem_limit_bytes=48 * 2**20
        ),
    )(
        *(
            pltpu.with_memory_space_constraint(value, pltpu.HBM)
            for value in (
                coefficient.reshape(NY, NZ), bottom_top.reshape(2, NY), right_side.reshape(n5, NZ),
                stiff_five, stiff_three, stiff_one,
            )
        )
    )
    sol, res = pl.pallas_call(
        hand_out,
        out_shape=[jax.ShapeDtypeStruct((n5, NZ), F32)] * 2,
        in_specs=[vmem] * 2,
        out_specs=[hbm, hbm],
        scratch_shapes=[dma((2, 4))],
    )(*(pltpu.with_memory_space_constraint(value, pltpu.VMEM) for value in (sol, res)))
    return sol.reshape(shape), res.reshape(shape)


def solution(mesh):
    field = P(None, None, None, "slab", "cross", None)
    return jax.shard_map(
        per_device,
        mesh=mesh,
        in_specs=(field, P("slab", "cross", None), P(None, "slab", "cross"), P(), P(), P()),
        out_specs=(field, field),
        check_vma=False,
    )
```

```python
import functools

import jax
import jax.numpy as jnp
import numpy as np
from jax import lax
from jax.experimental import pallas as pl
from jax.experimental.pallas import tpu as pltpu
from jax.sharding import PartitionSpec as P

MESH = pl.DeviceIdType.MESH
F32 = jnp.float32
BF16 = jnp.bfloat16
Q5, Q3, Q1 = 6, 4, 2
DEGREE = 3
COARSE_ITERS = 8
LAMBDA_TOP = 2.2
NY, NZ = 8, 128
SLOTS = 4
PENALTY = {Q5: 3.0, Q3: 2.0, Q1: 1.0}


def lagrange(fine_count, coarse_count):
    fine = np.linspace(-1.0, 1.0, fine_count)
    coarse = np.linspace(-1.0, 1.0, coarse_count)
    table = np.ones((fine_count, coarse_count))
    for c in range(coarse_count):
        for o in range(coarse_count):
            if o != c:
                table[:, c] = table[:, c] * (fine - coarse[o]) / (coarse[c] - coarse[o])
    return table.astype(np.float32)


def chebyshev_factors(steps, lowest):
    center = 0.5 * (LAMBDA_TOP + lowest)
    radius = 0.5 * (LAMBDA_TOP - lowest)
    sigma = center / radius
    rho = 1.0 / sigma
    pairs = []
    for _ in range(steps - 1):
        rho_next = 1.0 / (2.0 * sigma - rho)
        pairs.append((rho_next * rho, 2.0 * rho_next / radius))
        rho = rho_next
    return 1.0 / center, pairs


def weighted(table_row, terms):
    total = None
    for value, term in zip(table_row, terms):
        if value == 0.0:
            continue
        part = term if value == 1.0 else float(value) * term
        total = part if total is None else total + part
    return total


def tiles(value, *lead):
    return value.reshape(*lead, NY, NZ)


class Unslotted:
    def __init__(self, ref):
        self.ref, self.at = ref, self

    def __getitem__(self, index):
        return self.ref.at[index[1:]]


def kernel(
    coef_in, ends_in, rhs_in, s5_in, s3_in, s1_in, sol, res,
    mine, ends, s5, s3, s1,
    d5, t5, inv5, x3, r3, d3, t3, inv3, x1, r1, d1, t1, inv1,
    sh5, sl5, sh3, sl3, work, weights, hx, hy, ytile, pack, hc,
    hd, dpack, dtile, gx3, gx1, gy3, gy1, gw, hxl, hyl, hcc, gx5, gy5,
    xs, xr, ys, yr, cs, cr, csem, crsem, load,
):
    slab, cross = lax.axis_index("slab"), lax.axis_index("cross")
    ns, nc = lax.axis_size("slab"), lax.axis_size("cross")
    sides = (
        ("slab", slab - 1, slab > 0),
        ("slab", slab + 1, slab < ns - 1),
        ("cross", cross - 1, cross > 0),
        ("cross", cross + 1, cross < nc - 1),
    )
    corners = [
        ({"slab": slab + 2 * k - 1, "cross": cross + 2 * m - 1}, sides[k][2] & sides[2 + m][2])
        for k in range(2) for m in range(2)
    ]

    for k in range(2):

        @pl.when(jnp.logical_not(sides[k][2]))
        def _(k=k):
            hc[k] = jnp.zeros_like(hc[k])
            for slot in range(SLOTS):
                hx[slot, k] = jnp.zeros_like(hx[slot, k])

        @pl.when(jnp.logical_not(sides[2 + k][2]))
        def _(k=k):
            hc[2 + k] = jnp.zeros_like(hc[2 + k])
            for slot in range(SLOTS):
                hy[slot, k] = jnp.zeros_like(hy[slot, k])

    for g in range(4):

        @pl.when(jnp.logical_not(corners[g][1]))
        def _(g=g):
            hcc[g] = jnp.zeros_like(hcc[g])
            for slot in range(SLOTS):
                hd[slot, g] = jnp.zeros_like(hd[slot, g])

    barrier = pltpu.get_barrier_semaphore()
    peers = [({axis: index}, there) for axis, index, there in sides] + corners
    for device, there in peers:

        @pl.when(there)
        def _(device=device):
            pl.semaphore_signal(barrier, inc=1, device_id=device, device_id_type=MESH)

    pairs = ((coef_in, mine.at[0]), (s5_in, s5), (s3_in, s3), (rhs_in, res), (ends_in, ends), (s1_in, s1))
    loads = [pltpu.make_async_copy(src, dst, load.at[n]) for n, (src, dst) in enumerate(pairs)]
    for copy in loads:
        copy.start()
    ytile[...] = jnp.zeros_like(ytile)
    dtile[...] = jnp.zeros_like(dtile)
    for copy in loads:
        copy.wait()

    row = lax.broadcasted_iota(jnp.int32, (NY, NZ), 0)
    lane = lax.broadcasted_iota(jnp.int32, (NY, NZ), 1)
    bottom = jnp.zeros((NY, NZ), F32)
    top = jnp.zeros((NY, NZ), F32)
    for y in range(NY):
        bottom = jnp.where(row == y, ends[0, y].astype(F32), bottom)
        top = jnp.where(row == y, ends[1, y].astype(F32), top)
    mine[1] = jnp.where(lane == 0, bottom, jnp.where(lane == NZ - 1, top, 0.0))

    far = lax.rem(slab, 2)
    near = 1 - far

    def lines(q):
        if q < Q5:
            return [(0, q)]
        return [(0, 1), (q - 1, 1)] + [(j, min(2, q - 1 - j)) for j in range(1, q - 1, 2)]

    def groups(q):
        count = len(lines(q))
        return [[0, 1]] + [[n] for n in range(2, count)] if count > 1 else [[0]]

    def face_at(k, q, first, count):
        return pl.ds(pl.multiple_of(k * ((q**3 - q * q) * NY) + first * q * NY, NY), count * q * NY)

    def slab_copy(k, q, d, slot, piece, arriving):
        first, count = (0, q) if piece is None else lines(q)[piece]
        number = 0 if piece is None else piece
        here = k if arriving else 1 - k
        return pltpu.make_async_remote_copy(
            src_ref=d.at[slot, face_at(k, q, first, count), :],
            dst_ref=hx.at[slot, here, pl.ds(first * q * NY, count * q * NY), :],
            send_sem=xs.at[k, number, slot], recv_sem=xr.at[here, number, slot],
            device_id={"slab": slab + 2 * k - 1}, device_id_type=MESH,
        )

    def cross_copy(k, q, slot, arriving):
        here = k if arriving else k ^ 1
        return pltpu.make_async_remote_copy(
            src_ref=pack.at[slot, k, pl.ds(0, q * NY), :], dst_ref=hy.at[slot, here, pl.ds(0, q * NY), :],
            send_sem=ys.at[k, slot], recv_sem=yr.at[here, slot],
            device_id={"cross": sides[2 + k][1]}, device_id_type=MESH,
        )

    def slab_do(k, method, *args):
        index = slab + 2 * k - 1

        @pl.when((index >= 0) & (index < ns))
        def _():
            getattr(slab_copy(k, *args), method)()

    def cross_do(k, method, *args):
        @pl.when(sides[2 + k][2])
        def _():
            getattr(cross_copy(k, *args), method)()

    def send_near(q, d, slot):
        slab_do(near, "start", q, d, slot, None, False)

    def send_far(q, d, slot, pieces):
        for piece in pieces:
            slab_do(far, "start", q, d, slot, piece, False)

    def send_cross(q, d, slot):
        for i in range(q):
            pack[slot, 0, pl.ds(i * NY, q), :] = d[slot, pl.ds(i * q * q * NY, q, stride=NY), :]
            pack[slot, 1, pl.ds(i * NY, q), :] = d[slot, pl.ds((i * q * q + q * (q - 1)) * NY + NY - 1, q, stride=NY), :]
        for k in range(2):
            cross_do(k, "start", q, slot, False)

    def corner_copy(g, slot, arriving):
        here = g if arriving else 3 - g
        return pltpu.make_async_remote_copy(
            src_ref=dpack.at[slot, g], dst_ref=hd.at[slot, here],
            send_sem=cs.at[g, slot], recv_sem=cr.at[here, slot],
            device_id=corners[g][0], device_id_type=MESH,
        )

    def corner_do(g, method, *args):
        @pl.when(corners[g][1])
        def _():
            getattr(corner_copy(g, *args), method)()

    def send_corners(q, d, slot):
        for g in range(4):
            k, m = g // 2, g % 2
            node = k * (q**3 - q * q) + m * (q * q - q)
            dpack[slot, g, pl.ds(0, q), :] = d[slot, pl.ds(node * NY + m * (NY - 1), q, stride=NY), :]
        for g in range(4):
            corner_do(g, "start", slot, False)

    def send_all(q, d, slot, with_corners):
        if with_corners:
            send_corners(q, d, slot)
        send_cross(q, d, slot)
        send_near(q, d, slot)
        send_far(q, d, slot, range(len(lines(q))))

    def arrived_cross(q, slot):
        for k in range(2):
            cross_do(k, "wait_recv", q, slot, True)

    def arrived_slab(q, d, slot):
        slab_do(near, "wait_recv", q, d, slot, None, True)
        for piece in range(len(lines(q))):
            slab_do(far, "wait_recv", q, d, slot, piece, True)

    def arrived_corners(slot):
        for g in range(4):
            corner_do(g, "wait_recv", slot, True)

    def sent(q, d, slot, with_corners):
        slab_do(near, "wait_send", q, d, slot, None, False)
        for piece in range(len(lines(q))):
            slab_do(far, "wait_send", q, d, slot, piece, False)
        for k in range(2):
            cross_do(k, "wait_send", q, slot, False)
        if with_corners:
            for g in range(4):
                corner_do(g, "wait_send", slot, False)

    def pack_rows(q, source, target):
        for i in range(q):
            target[0, pl.ds(i * NY, q), :] = source[pl.ds(i * q * q * NY, q, stride=NY), :]
            target[1, pl.ds(i * NY, q), :] = source[pl.ds((i * q * q + q * (q - 1)) * NY + NY - 1, q, stride=NY), :]

    for i in range(Q5):
        for m in range(2):
            nodes = [i * Q5 * Q5 + m * Q5 * (Q5 - 1) + n for n in range(Q5)]
            ends_of = [res[pl.ds(node * NY, NY), :][m * (NY - 1) : m * (NY - 1) + 1] for node in nodes]
            pack[0, m, pl.ds(i * NY, Q5), :] = jnp.concatenate(ends_of, 0)
    pl.semaphore_wait(barrier, sum(there.astype(jnp.int32) for _, there in peers))

    def coef_copy(k, arriving):
        if k < 4:
            here = k if arriving else k ^ 1
            src, dst = mine, hc.at[here]
        else:
            here = k if arriving else 11 - k
            src, dst = mine.at[0], hcc.at[here - 4]
        return pltpu.make_async_remote_copy(
            src_ref=src, dst_ref=dst, send_sem=csem.at[k], recv_sem=crsem.at[here],
            device_id=peers[k][0], device_id_type=MESH,
        )

    for k in (2, 3, 0, 1, 4, 5, 6, 7):

        @pl.when(peers[k][1])
        def _(k=k):
            coef_copy(k, False).start()

    raw = Unslotted(res)
    for k in range(2):
        cross_do(k, "start", Q5, 0, False)
    send_near(Q5, raw, 0)
    send_far(Q5, raw, 0, range(len(lines(Q5))))

    def split(table, high, low, count):
        value = table[...]
        high[...] = jnp.zeros_like(high)
        low[...] = jnp.zeros_like(low)
        top = value.astype(BF16)
        high[pl.ds(0, count), pl.ds(0, count)] = top
        low[pl.ds(0, count), pl.ds(0, count)] = (value - top.astype(F32)).astype(BF16)

    split(s5, sh5, sl5, Q5**3)
    split(s3, sh3, sl3, Q3**3)

    def spread_diagonal(table, inv, count):
        value = table[...]
        same = lax.broadcasted_iota(jnp.int32, value.shape, 0) == lax.broadcasted_iota(jnp.int32, value.shape, 1)
        column = jnp.sum(jnp.where(same, value, 0.0), axis=1, keepdims=True)
        wide = jnp.broadcast_to(column, (count, NZ))
        for y in range(NY):
            inv[pl.ds(y, count, stride=NY), :] = wide

    spread_diagonal(s5, inv5, Q5**3)
    spread_diagonal(s3, inv3, Q3**3)
    for n in range(Q1**3):
        inv1[pl.ds(n * NY, NY), :] = jnp.full((NY, NZ), s1[n, n])
    for q, inv, gx, gy in ((Q5, inv5, gx5, gy5), (Q3, inv3, gx3, gy3), (Q1, inv1, gx1, gy1)):
        for k in range(2):
            gx[k] = inv[face_at(1 - k, q, 0, q), :]
            for i in range(q):
                node = i * q * q + (1 - k) * q * (q - 1)
                gy[k, pl.ds(i * NY, q), :] = inv[pl.ds(node * NY, q, stride=NY), :]

    def coefs_done(ks):
        for k in ks:

            @pl.when(peers[k][1])
            def _(k=k):
                coef_copy(k, True).wait_recv()
                coef_copy(k, False).wait_send()

    coefs_done(range(4))
    c = mine[0]

    def cross_weights(own, below, above):
        before = jnp.where(row == 0, pltpu.roll(below, 1, 0), pltpu.roll(own, 1, 0))
        after = jnp.where(row == NY - 1, pltpu.roll(above, NY - 1, 0), pltpu.roll(own, NY - 1, 0))
        return 0.5 * (own + before), 0.5 * (own + after)

    def end_weights(own, flags):
        low = jnp.where(lane == 0, flags * own, 0.5 * (own + pltpu.roll(own, 1, 1)))
        high = jnp.where(lane == NZ - 1, flags * own, 0.5 * (own + pltpu.roll(own, NZ - 1, 1)))
        return low, high

    weights[0] = 0.5 * (c + hc[0, 0])
    weights[1] = 0.5 * (c + hc[1, 0])
    weights[2], weights[3] = cross_weights(c, hc[2, 0], hc[3, 0])
    weights[4], weights[5] = end_weights(c, mine[1])

    def ends_added(base, q, y_pair, z_pair):
        first = base[0:1] + y_pair[0][None]
        last = base[q - 1 : q] + y_pair[1][None]
        base = jnp.concatenate([first, base[1 : q - 1], last] if q > 2 else [first, last], 0)
        first = base[:, 0:1] + z_pair[0][:, None]
        last = base[:, q - 1 : q] + z_pair[1][:, None]
        return jnp.concatenate([first, base[:, 1 : q - 1], last] if q > 2 else [first, last], 1)

    def slab_weight(i, q):
        return jnp.where(i == 0, PENALTY[q] * weights[0], 0.0) + jnp.where(i == q - 1, PENALTY[q] * weights[1], 0.0)

    def plane_at(i, q):
        return pl.ds(pl.multiple_of(i * (q * q * NY), NY), q * q * NY)

    def invert(q, inv):
        yl, yh, zl, zh = (jnp.broadcast_to(PENALTY[q] * weights[k], (q, NY, NZ)) for k in range(2, 6))

        def body(i, carry):
            at = plane_at(i, q)
            base = tiles(inv[at, :], q, q) * c + slab_weight(i, q)
            base = ends_added(base, q, (yl, yh), (zl, zh))
            inv[at, :] = (1.0 / base).reshape(q * q * NY, NZ)
            return carry

        lax.fori_loop(0, q, body, 0)

    invert(Q5, inv5)

    def product_wide(q, d, slot, t, high, low):
        count = q**3
        padded = high.shape[0]
        s_high, s_low = high[...], low[...]
        for y in range(0, NY, 2):
            pair = [d[slot, pl.ds(y + h, count, stride=NY), :] for h in range(2)]
            v = jnp.concatenate(pair, 1)
            if padded > count:
                v = jnp.concatenate([v, jnp.zeros((padded - count, 2 * NZ), F32)], 0)
            v_high = v.astype(BF16)
            v_low = (v - v_high.astype(F32)).astype(BF16)
            out = jnp.dot(s_high, v_high, preferred_element_type=F32)
            out += jnp.dot(s_high, v_low, preferred_element_type=F32)
            out += jnp.dot(s_low, v_high, preferred_element_type=F32)
            for h in range(2):
                t[pl.ds(y + h, count, stride=NY), :] = out[:count, h * NZ : (h + 1) * NZ]

    def product_small(d, slot, t):
        count = Q1**3
        parts = [d[slot, pl.ds(n * NY, NY), :] for n in range(count)]
        for m in range(count):
            total = s1[m, 0] * parts[0]
            for n in range(1, count):
                total += s1[m, n] * parts[n]
            t[pl.ds(m * NY, NY), :] = total

    def local_part(level, slot):
        q, d, t, r = (level[name] for name in ("q", "d", "t", "r"))
        p = PENALTY[q]
        level["product"](slot)

        def local(i, carry):
            yl, yh, zl, zh = (p * weights[k] for k in range(2, 6))
            at = plane_at(i, q)
            dv = tiles(d[slot, at, :], q, q)
            lo, hi = dv[0], dv[q - 1]
            y_pair = (
                yl * (lo - jnp.where(row == 0, 0.0, pltpu.roll(hi, 1, 1))),
                yh * (hi - jnp.where(row == NY - 1, 0.0, pltpu.roll(lo, NY - 1, 1))),
            )
            lo, hi = dv[:, 0], dv[:, q - 1]
            z_pair = (
                zl * (lo - jnp.where(lane == 0, 0.0, pltpu.roll(hi, 1, 2))),
                zh * (hi - jnp.where(lane == NZ - 1, 0.0, pltpu.roll(lo, NZ - 1, 2))),
            )
            total = ends_added(tiles(t[at, :], q, q) * c, q, y_pair, z_pair)
            r[at, :] = r[at, :] - total.reshape(q * q * NY, NZ)
            return carry

        lax.fori_loop(0, q, local, 0)
        face = q * q * NY
        for k in range(2):
            at = pl.ds(0 if k == 0 else (q**3) * NY - face, face)
            r[at, :] = r[at, :] - (p * weights[k] * tiles(d[slot, at, :], q * q)).reshape(face, NZ)

    def rims(level, source, put):
        q = level["q"]
        for i in range(q):
            ytile[0, pl.ds(i * q * NY, q, stride=NY), :] = source[0, pl.ds(i * NY, q), :]
            ytile[1, pl.ds(i * q * NY + NY - 1, q, stride=NY), :] = source[1, pl.ds(i * NY, q), :]

        def rim(i, carry):
            for k in range(2):
                at = pl.ds(pl.multiple_of(i * (q * q * NY) + k * q * (q - 1) * NY, NY), q * NY)
                part = PENALTY[q] * weights[2 + k] * tiles(ytile[k, pl.ds(pl.multiple_of(i * (q * NY), NY), q * NY), :], q)
                put(at, part.reshape(q * NY, NZ))
            return carry

        lax.fori_loop(0, q, rim, 0)

    def slab_term(level, source, k, first, count):
        q = level["q"]
        part = PENALTY[q] * weights[k] * tiles(source[k, pl.ds(first * q * NY, count * q * NY), :], count * q)
        return part.reshape(count * q * NY, NZ)

    def step(level, slot, a, b, update, send, settled=False, meanwhile=None):
        q, d, r, x, inv = (level[name] for name in ("q", "d", "r", "x", "inv"))
        other = lax.rem(slot + 1, SLOTS)

        def put(at, part):
            r[at, :] = r[at, :] + part

        local_part(level, slot)
        for k in range(2):
            cross_do(k, "wait_recv", q, slot, True)
        rims(level, hy.at[slot], put)

        def advance(at):
            value = a * d[slot, at, :] + b * inv[at, :] * r[at, :]
            d[other, at, :] = value
            x[at, :] = x[at, :] + value

        if update and q > 2:

            def inside(i, carry):
                advance(plane_at(i, q))
                return carry

            lax.fori_loop(1, q - 1, inside, 0)

        def slab_face(k, first, count):
            at = face_at(k, q, first, count)
            put(at, slab_term(level, hx.at[slot], k, first, count))
            if update:
                advance(at)

        slab_do(near, "wait_recv", q, d, slot, None, True)
        slab_face(near, 0, q)
        if send:
            send_near(q, d, other)
        if meanwhile is not None:
            meanwhile()
        for number, group in enumerate(groups(q)):
            for piece in group:
                slab_do(far, "wait_recv", q, d, slot, piece, True)
                slab_face(far, *lines(q)[piece])
            if send:
                if number == 0:
                    send_cross(q, d, other)
                send_far(q, d, other, group)
        if not settled:
            sent(q, d, slot, False)

    def correct(level, slot, rows, b, slab_put, cross_put):
        q, d, gx, gy = (level[name] for name in ("q", "d", "gx", "gy"))
        p = PENALTY[q]
        face = q * q * NY
        for k in range(2):
            for m in range(2):
                dtile[m, pl.ds(m * (NY - 1), q, stride=NY), :] = hd[slot, 2 * k + m, pl.ds(0, q), :]
            term = p * weights[k] * tiles(d[slot, pl.ds(k * (q**3 - q * q) * NY, face), :], q, q)
            low, high = (p * gw[k, m] * tiles(dtile[m, pl.ds(0, q * NY), :], q) for m in range(2))
            first, last = term[0:1] + low[None], term[q - 1 : q] + high[None]
            term = jnp.concatenate([first, term[1 : q - 1], last] if q > 2 else [first, last], 0)
            at = pl.ds(0, face)
            slab_put(k, at, b * gx[k, at, :] * term.reshape(face, NZ))
        for m in range(2):
            here, theirs = pl.ds(m * (NY - 1), 1), pl.ds((1 - m) * (NY - 1), 1)
            for i in range(q):
                at = pl.ds(i * NY, q)
                term = p * weights[2 + m, here, :] * rows[m, at, :]
                for k in range(2):
                    if i == k * (q - 1):
                        term = term + p * gw[2 + m, k, theirs, :] * hd[slot, 2 * k + m, pl.ds(0, q), :]
                cross_put(m, at, b * gy[m, at, :] * term)

    def planes(q, body):
        def one_plane(i, carry):
            body(plane_at(i, q))
            return carry

        lax.fori_loop(0, q, one_plane, 0)

    def half_round(level, slot, a, b, total):
        q, d, r, x, inv = (level[name] for name in ("q", "d", "r", "x", "inv"))
        other = lax.rem(slot + 1, SLOTS)

        def partial_next(at):
            value = a * d[slot, at, :] + b * inv[at, :] * r[at, :]
            d[other, at, :] = x[at, :] + value if total else value

        def put_both(at, part):
            r[at, :] = r[at, :] + part
            d[other, at, :] = d[other, at, :] + b * inv[at, :] * part

        local_part(level, slot)
        planes(q, partial_next)
        send_all(q, d, other, False)
        arrived_cross(q, slot)
        sent(q, d, other, False)
        rims(level, hy.at[slot], put_both)
        arrived_slab(q, d, slot)
        for k in range(2):
            put_both(face_at(k, q, 0, q), slab_term(level, hx.at[slot], k, 0, q))

    def keep_slab(k, at, part):
        hxl[k, at, :] = part

    def keep_cross(m, at, part):
        hyl[m, at, :] = part

    def double_step(level, slot, first, second, with_corners, total):
        q, d, r, x, inv = (level[name] for name in ("q", "d", "r", "x", "inv"))
        other, third = lax.rem(slot + 1, SLOTS), lax.rem(slot + 2, SLOTS)

        def put(at, part):
            r[at, :] = r[at, :] + part

        def add(at):
            x[at, :] = x[at, :] + d[other, at, :]

        def advance(at):
            value = second[0] * d[other, at, :] + second[1] * inv[at, :] * r[at, :]
            if total:
                d[third, at, :] = x[at, :] + value
            else:
                d[third, at, :] = value
                x[at, :] = x[at, :] + value

        half_round(level, slot, *first, False)
        planes(q, add)
        local_part(level, other)
        arrived_corners(slot)

        correct(level, slot, pack.at[slot], first[1], keep_slab, keep_cross)
        rims(level, hyl, put)
        for k in range(2):
            put(face_at(k, q, 0, q), slab_term(level, hxl, k, 0, q))
        arrived_cross(q, other)
        rims(level, hy.at[other], put)
        arrived_slab(q, d, other)
        for k in range(2):
            put(face_at(k, q, 0, q), slab_term(level, hx.at[other], k, 0, q))
        planes(q, advance)
        send_all(q, d, third, with_corners)
        sent(q, d, slot, True)

    def finish_round(level, slot, a, b):
        q, d = level["q"], level["d"]
        other = lax.rem(slot + 1, SLOTS)
        half_round(level, slot, a, b, True)
        arrived_corners(slot)
        arrived_cross(q, other)
        arrived_slab(q, d, other)

        def add_slab(k, at, part):
            hx[other, k, at, :] = hx[other, k, at, :] + part

        def add_cross(m, at, part):
            hy[other, m, at, :] = hy[other, m, at, :] + part

        correct(level, slot, pack.at[slot], b, add_slab, add_cross)
        sent(q, d, slot, True)

    def lift_slab(qc, qf, slot):
        table = lagrange(qf, qc)
        for k in range(2):
            lines_in = tiles(hx[slot, k, pl.ds(0, qc * qc * NY), :], qc, qc)
            for j in range(qf):
                line = weighted(table[j], [lines_in[n] for n in range(qc)])
                for n in range(qf):
                    hxl[k, pl.ds((j * qf + n) * NY, NY), :] = weighted(table[n], [line[e] for e in range(qc)])

    def spread_table(qc, qf):
        table = lagrange(qf, qc)
        spread = []
        for e in range(qc):
            column = jnp.zeros((NY, NZ), F32)
            for n in range(qf):
                if table[n, e] != 0.0:
                    column = jnp.where(row == n, float(table[n, e]), column)
            spread.append(column)
        return spread

    def lift_line(spread, line):
        value = spread[0] * line[0:1]
        for e in range(1, len(spread)):
            value = value + spread[e] * line[e : e + 1]
        return value

    def lift_cross(qc, qf, slot):
        table, spread = lagrange(qf, qc), spread_table(qc, qf)
        for k in range(2):
            for i in range(qf):
                line = weighted(table[i], [hy[slot, k, pl.ds(a * NY, qc), :] for a in range(qc)])
                hyl[k, pl.ds(i * NY, NY), :] = lift_line(spread, line)

    def lift_corners(qc, qf, slot):
        spread = spread_table(qc, qf)
        for g in range(4):
            hd[slot, g] = lift_line(spread, hd[slot, g])

    def lifted_step(coarse, slot, level, here, factor):
        q, d, r, x, inv = (level[name] for name in ("q", "d", "r", "x", "inv"))
        following = (here + 1) % SLOTS
        prolong(coarse["d"].at[slot], d, here, x, q, coarse["q"])
        local_part(level, here)
        lift_cross(coarse["q"], q, slot)
        lift_slab(coarse["q"], q, slot)

        def put(at, part):
            r[at, :] = r[at, :] + part

        def advance(at):
            value = factor * inv[at, :] * r[at, :]
            d[following, at, :] = value
            x[at, :] = x[at, :] + value

        rims(level, hyl, put)
        for k in range(2):
            put(face_at(k, q, 0, q), slab_term(level, hxl, k, 0, q))
        planes(q, advance)
        send_all(q, d, following, True)

    def lifted_round(coarse, level, here, factor):
        q, d, r, x, inv = (level[name] for name in ("q", "d", "r", "x", "inv"))
        qc, other, spare = coarse["q"], (here + 1) % SLOTS, (here + 3) % SLOTS

        def partial_next(at):
            d[other, at, :] = factor * inv[at, :] * r[at, :]

        def put(at, part):
            r[at, :] = r[at, :] + part

        def put_both(at, part):
            r[at, :] = r[at, :] + part
            d[other, at, :] = d[other, at, :] + factor * inv[at, :] * part

        def add(at):
            x[at, :] = x[at, :] + d[other, at, :]

        prolong(coarse["d"].at[here], d, here, x, q, qc)
        local_part(level, here)
        planes(q, partial_next)
        send_all(q, d, other, False)
        pack_rows(q, d.at[here], pack.at[spare])
        arrived_cross(qc, here)
        lift_cross(qc, q, here)
        arrived_slab(qc, coarse["d"], here)
        lift_slab(qc, q, here)
        sent(q, d, other, False)
        rims(level, hyl, put_both)
        for k in range(2):
            put_both(face_at(k, q, 0, q), slab_term(level, hxl, k, 0, q))
        planes(q, add)
        arrived_corners(here)
        lift_corners(qc, q, here)
        correct(level, here, pack.at[spare], factor, keep_slab, keep_cross)
        rims(level, hyl, put)
        for k in range(2):
            put(face_at(k, q, 0, q), slab_term(level, hxl, k, 0, q))
        sent(qc, coarse["d"], here, True)

    def first_update(level, slot, factor, with_corners):
        q, d, x, r, inv = (level[name] for name in ("q", "d", "x", "r", "inv"))

        def body(i, carry):
            at = plane_at(i, q)
            value = inv[at, :] * r[at, :] * factor
            d[slot, at, :] = value
            x[at, :] = value
            return carry

        lax.fori_loop(0, q, body, 0)
        send_all(q, d, slot, with_corners)

    def neighbours_inverse(q, gx, gy):
        p = PENALTY[q]
        for k in range(2):
            own = hc[k, 0]
            y_pair, z_pair = (
                [jnp.broadcast_to(p * w, (q, NY, NZ)) for w in pair] for pair in ((gw[k, 0], gw[k, 1]), end_weights(own, hc[k, 1]))
            )
            base = ends_added(tiles(gx[k], q, q) * own + p * weights[k], q, y_pair, z_pair)
            gx[k] = (1.0 / base).reshape(q * q * NY, NZ)
        node = lax.broadcasted_iota(jnp.int32, (q, NZ), 0)
        for m in range(2):
            here, theirs = m * (NY - 1), (1 - m) * (NY - 1)
            low, high = (w[theirs : theirs + 1] for w in end_weights(hc[2 + m, 0], hc[2 + m, 1]))
            own = hc[2 + m, 0, pl.ds(theirs, 1), :]
            across = p * weights[2 + m, pl.ds(here, 1), :]
            along = p * (jnp.where(node == 0, low, 0.0) + jnp.where(node == q - 1, high, 0.0))
            for i in range(q):
                at = pl.ds(i * NY, q)
                base = gy[m, at, :] * own + across + along
                for k in range(2):
                    if i == k * (q - 1):
                        base = base + p * gw[2 + m, k, pl.ds(theirs, 1), :]
                gy[m, at, :] = 1.0 / base

    def zero_missing(gx, gy):
        for k in range(2):

            @pl.when(jnp.logical_not(sides[k][2]))
            def _(k=k):
                gx[k] = jnp.zeros_like(gx[k])

            @pl.when(jnp.logical_not(sides[2 + k][2]))
            def _(k=k):
                gy[k] = jnp.zeros_like(gy[k])

    def opening_step(level, factor, a, b):
        q, d, r, x, inv = (level[name] for name in ("q", "d", "r", "x", "inv"))
        p = PENALTY[q]

        def start(at):
            value = inv[at, :] * r[at, :] * factor
            d[0, at, :] = value
            x[at, :] = value

        def put(at, part):
            r[at, :] = r[at, :] + part

        def advance(at):
            value = a * d[0, at, :] + b * inv[at, :] * r[at, :]
            d[1, at, :] = value
            x[at, :] = x[at, :] + value

        planes(q, start)
        slab_do(near, "wait_send", q, raw, 0, None, False)
        for piece in range(len(lines(q))):
            slab_do(far, "wait_send", q, raw, 0, piece, False)
        local_part(level, 0)
        coefs_done(range(4, 8))
        for k in range(2):
            gw[k, 0], gw[k, 1] = cross_weights(hc[k, 0], hcc[2 * k], hcc[2 * k + 1])
            for m in range(2):
                gw[2 + m, k] = 0.5 * (hc[2 + m, 0] + hcc[2 * k + m])
        neighbours_inverse(q, gx5, gy5)
        for k in range(2):
            cross_do(k, "wait_recv", q, 0, True)
        for m in range(2):
            for i in range(q):
                at = pl.ds(i * NY, q)
                hy[0, m, at, :] = gy5[m, at, :] * hy[0, m, at, :] * factor
        rims(level, hy.at[0], put)

        def inside(i, carry):
            advance(plane_at(i, q))
            return carry

        lax.fori_loop(1, q - 1, inside, 0)

        def slab_face(k, first, count):
            inside_face = pl.ds(first * q * NY, count * q * NY)
            hx[0, k, inside_face, :] = gx5[k, inside_face, :] * hx[0, k, inside_face, :] * factor
            at = face_at(k, q, first, count)
            put(at, slab_term(level, hx.at[0], k, first, count))
            advance(at)

        slab_do(near, "wait_recv", q, raw, 0, None, True)
        slab_face(near, 0, q)
        send_near(q, d, 1)
        for number, group in enumerate(groups(q)):
            for piece in group:
                slab_do(far, "wait_recv", q, raw, 0, piece, True)
                slab_face(far, *lines(q)[piece])
            if number == 0:
                send_cross(q, d, 1)
            send_far(q, d, 1, group)
        for k in range(2):
            cross_do(k, "wait_send", q, 0, False)
        zero_missing(gx5, gy5)

    def pick(k, values):
        out = jnp.float32(values[0])
        for n in range(1, len(values)):
            out = jnp.where(k == n, jnp.float32(values[n]), out)
        return out

    def run(level, exchange, factors, last):
        loop = len(factors) if last else len(factors) - 1

        def body(k, carry):
            a, b = pick(k, [f[0] for f in factors]), pick(k, [f[1] for f in factors])
            step(level, lax.rem(exchange + k, SLOTS), a, b, True, True)
            return carry

        lax.fori_loop(0, loop, body, 0)
        slot = (exchange + loop) % SLOTS
        if last:
            step(level, slot, 0.0, 0.0, False, False)
        else:
            step(level, slot, *factors[-1], True, False)

    def restrict(fine, coarse, qf, qc):
        table = lagrange(qf, qc)

        def body(j, carry):
            rows = [tiles(fine[pl.ds(pl.multiple_of(j * (qf * NY) + i * qf * qf * NY, NY), qf * NY), :], qf) for i in range(qf)]
            for a in range(qc):
                along = weighted(table[:, a], rows)
                for e in range(qc):
                    out = weighted(table[:, e], [along[k] for k in range(qf)])
                    work[pl.ds(pl.multiple_of(j * (qc * qc * NY) + (a * qc + e) * NY, NY), NY), :] = out
            return carry

        lax.fori_loop(0, qf, body, 0)

        def gather(a, carry):
            rows = [work[pl.ds(pl.multiple_of(a * (qc * NY) + j * qc * qc * NY, NY), qc * NY), :] for j in range(qf)]
            for b in range(qc):
                at = pl.ds(pl.multiple_of(a * (qc * qc * NY) + b * qc * NY, NY), qc * NY)
                coarse[at, :] = weighted(table[:, b], rows)
            return carry

        lax.fori_loop(0, qc, gather, 0)

    def restrict_face(slot, k, coarse, qf, qc):
        table = lagrange(qf, qc)
        lines_in = tiles(hx[slot, k, pl.ds(0, qf * qf * NY), :], qf, qf)
        weight = PENALTY[qf] * weights[k]
        for b in range(qc):
            line = weighted(table[:, b], [lines_in[j] for j in range(qf)])
            for e in range(qc):
                value = weight * weighted(table[:, e], [line[n] for n in range(qf)])
                at = pl.ds(pl.multiple_of(k * ((qc**3 - qc * qc) * NY) + (b * qc + e) * NY, NY), NY)
                coarse[at, :] = coarse[at, :] + value

    def prolong(coarse, fine, slot, sum_into, qf, qc):
        table = lagrange(qf, qc)

        def spread(a, carry):
            rows = [coarse[pl.ds(pl.multiple_of(a * (qc * qc * NY) + b * qc * NY, NY), qc * NY), :] for b in range(qc)]
            for j in range(qf):
                at = pl.ds(pl.multiple_of(a * (qc * NY) + j * qc * qc * NY, NY), qc * NY)
                work[at, :] = weighted(table[j], rows)
            return carry

        lax.fori_loop(0, qc, spread, 0)

        def body(j, carry):
            along = []
            for a in range(qc):
                at = pl.ds(pl.multiple_of(j * (qc * qc * NY) + a * qc * NY, NY), qc * NY)
                part = tiles(work[at, :], qc)
                along.append([weighted(table[k], [part[e] for e in range(qc)]) for k in range(qf)])
            for i in range(qf):
                for k in range(qf):
                    value = weighted(table[i], [along[a][k] for a in range(qc)])
                    at = pl.ds(pl.multiple_of(j * (qf * NY) + (i * qf * qf + k) * NY, NY), NY)
                    fine[slot, at, :] = value
                    sum_into[at, :] = sum_into[at, :] + value
            return carry

        lax.fori_loop(0, qf, body, 0)

    five = dict(q=Q5, d=d5, t=t5, r=res, x=sol, inv=inv5, gx=gx5, gy=gy5, product=lambda slot: product_wide(Q5, d5, slot, t5, sh5, sl5))
    three = dict(q=Q3, d=d3, t=t3, r=r3, x=x3, inv=inv3, gx=gx3, gy=gy3, product=lambda slot: product_wide(Q3, d3, slot, t3, sh3, sl3))
    one = dict(q=Q1, d=d1, t=t1, r=r1, x=x1, inv=inv1, gx=gx1, gy=gy1, product=lambda slot: product_small(d1, slot, t1))

    first, pairs = chebyshev_factors(DEGREE, LAMBDA_TOP / 8.0)
    coarse_first, coarse_pairs = chebyshev_factors(COARSE_ITERS, LAMBDA_TOP / 40.0)
    opening_step(five, first, *pairs[0])

    def prepare():
        invert(Q3, inv3)
        invert(Q1, inv1)
        for q, gx, gy in ((Q3, gx3, gy3), (Q1, gx1, gy1)):
            neighbours_inverse(q, gx, gy)
            zero_missing(gx, gy)

    step(five, 1, *pairs[1], True, True, meanwhile=prepare)
    step(five, 2, 0.0, 0.0, False, False, meanwhile=lambda: restrict(res, r3, Q5, Q3))
    restrict_face(2, far, r3, Q5, Q3)
    first_update(three, 3, first, True)
    double_step(three, 3, *pairs, False, False)
    step(three, 5 % SLOTS, 0.0, 0.0, False, False)
    restrict(r3, r1, Q3, Q1)
    first_update(one, 6 % SLOTS, coarse_first, True)

    def coarse_rounds(n, carry):
        factors = [[pick(n, [f[part] for f in coarse_pairs[half:6:2]]) for part in range(2)] for half in range(2)]
        double_step(one, lax.rem(6 + 2 * n, SLOTS), *factors, True, False)
        return carry

    lax.fori_loop(0, 3, coarse_rounds, 0)
    finish_round(one, 12 % SLOTS, *coarse_pairs[6])
    lifted_step(one, 13 % SLOTS, three, 13 % SLOTS, first)
    double_step(three, 14 % SLOTS, *pairs, True, True)
    lifted_round(three, five, 16 % SLOTS, first)
    step(five, 17 % SLOTS, *pairs[0], True, True, settled=True)
    run(five, 18, pairs[1:], True)


def hand_out(sol, res, sol_out, res_out, done):
    rows = Q5**3 * NY // 4
    copies = [
        pltpu.make_async_copy(src.at[pl.ds(n * rows, rows), :], dst.at[pl.ds(n * rows, rows), :], done.at[k, n])
        for k, (src, dst) in enumerate(((sol, sol_out), (res, res_out))) for n in range(4)
    ]
    for copy in copies:
        copy.start()
    for copy in copies:
        copy.wait()


def per_device(right_side, coefficient, bottom_top, stiff_five, stiff_three, stiff_one):
    shape = right_side.shape
    n5, n3, n1 = Q5**3 * NY, Q3**3 * NY, Q1**3 * NY
    vmem = pl.BlockSpec(memory_space=pltpu.VMEM)
    hbm = pl.BlockSpec(memory_space=pltpu.HBM)
    field = lambda n: pltpu.VMEM((n, NZ), F32)
    slots = lambda *n: pltpu.VMEM((SLOTS, *n, NZ), F32)
    two = lambda n: pltpu.VMEM((2, n, NZ), F32)
    dma = pltpu.SemaphoreType.DMA
    sol, res = pl.pallas_call(
        kernel,
        out_shape=[jax.ShapeDtypeStruct((n5, NZ), F32)] * 2,
        in_specs=[hbm] * 6,
        out_specs=[vmem, vmem],
        scratch_shapes=[
            two(NY), pltpu.SMEM((2, NY), jnp.int32), pltpu.VMEM((Q5**3, Q5**3), F32), pltpu.VMEM((Q3**3, Q3**3), F32),
            pltpu.SMEM((Q1**3, Q1**3), F32),
            slots(n5 + 16), field(n5), field(n5 + 16),
            field(n3), field(n3), slots(n3 + 32), field(n3), field(n3 + 32),
            field(n1), field(n1), slots(n1 + 48), field(n1), field(n1 + 48),
            pltpu.VMEM((224, 224), BF16), pltpu.VMEM((224, 224), BF16),
            pltpu.VMEM((64, 64), BF16), pltpu.VMEM((64, 64), BF16),
            field(6 * 16 * NY), pltpu.VMEM((6, NY, NZ), F32),
            slots(2, Q5 * Q5 * NY), slots(2, Q5 * NY), two(Q5 * Q5 * NY + 24), slots(2, Q5 * NY), pltpu.VMEM((4, 2, NY, NZ), F32),
            slots(4, NY), slots(4, NY), two(8 * NY),
            two(Q3 * Q3 * NY), two(Q1 * Q1 * NY), two(Q3 * NY), two(Q1 * NY),
            pltpu.VMEM((4, 2, NY, NZ), F32), two(Q5 * Q5 * NY), two(Q5 * NY),
            pltpu.VMEM((4, NY, NZ), F32), two(Q5 * Q5 * NY), two(Q5 * NY),
            dma((2, 4, SLOTS)), dma((2, 4, SLOTS)), dma((2, SLOTS)), dma((2, SLOTS)), dma((4, SLOTS)), dma((4, SLOTS)),
            dma((8,)), dma((8,)), dma((6,)),
        ],
        compiler_params=pltpu.CompilerParams(
            collective_id=0, has_side_effects=True, vmem_limit_bytes=48 * 2**20
        ),
    )(
        *(
            pltpu.with_memory_space_constraint(value, pltpu.HBM)
            for value in (
                coefficient.reshape(NY, NZ), bottom_top.reshape(2, NY), right_side.reshape(n5, NZ),
                stiff_five, stiff_three, stiff_one,
            )
        )
    )
    sol, res = pl.pallas_call(
        hand_out,
        out_shape=[jax.ShapeDtypeStruct((n5, NZ), F32)] * 2,
        in_specs=[vmem] * 2,
        out_specs=[hbm, hbm],
        scratch_shapes=[dma((2, 4))],
    )(*(pltpu.with_memory_space_constraint(value, pltpu.VMEM) for value in (sol, res)))
    return sol.reshape(shape), res.reshape(shape)


def solution(mesh):
    field = P(None, None, None, "slab", "cross", None)
    return jax.shard_map(
        per_device,
        mesh=mesh,
        in_specs=(field, P("slab", "cross", None), P(None, "slab", "cross"), P(), P(), P()),
        out_specs=(field, field),
        check_vma=False,
    )
```

```python
import functools

import jax
import jax.numpy as jnp
import numpy as np
from jax import lax
from jax.experimental import pallas as pl
from jax.experimental.pallas import tpu as pltpu
from jax.sharding import PartitionSpec as P

MESH = pl.DeviceIdType.MESH
F32 = jnp.float32
BF16 = jnp.bfloat16
Q5, Q3, Q1 = 6, 4, 2
DEGREE = 3
COARSE_ITERS = 8
LAMBDA_TOP = 2.2
NY, NZ = 8, 128
SLOTS = 4
PENALTY = {Q5: 3.0, Q3: 2.0, Q1: 1.0}


def lagrange(fine_count, coarse_count):
    fine = np.linspace(-1.0, 1.0, fine_count)
    coarse = np.linspace(-1.0, 1.0, coarse_count)
    table = np.ones((fine_count, coarse_count))
    for c in range(coarse_count):
        for o in range(coarse_count):
            if o != c:
                table[:, c] = table[:, c] * (fine - coarse[o]) / (coarse[c] - coarse[o])
    return table.astype(np.float32)


def chebyshev_factors(steps, lowest):
    center = 0.5 * (LAMBDA_TOP + lowest)
    radius = 0.5 * (LAMBDA_TOP - lowest)
    sigma = center / radius
    rho = 1.0 / sigma
    pairs = []
    for _ in range(steps - 1):
        rho_next = 1.0 / (2.0 * sigma - rho)
        pairs.append((rho_next * rho, 2.0 * rho_next / radius))
        rho = rho_next
    return 1.0 / center, pairs


def weighted(table_row, terms):
    total = None
    for value, term in zip(table_row, terms):
        if value == 0.0:
            continue
        part = term if value == 1.0 else float(value) * term
        total = part if total is None else total + part
    return total


def tiles(value, *lead):
    return value.reshape(*lead, NY, NZ)


class Unslotted:
    def __init__(self, ref):
        self.ref, self.at = ref, self

    def __getitem__(self, index):
        return self.ref.at[index[1:]]


def kernel(
    coef_in, ends_in, rhs_in, s5_in, s3_in, s1_in, sol, res,
    mine, ends, s5, s3, s1,
    d5, t5, inv5, x3, r3, d3, t3, inv3, x1, r1, d1, t1, inv1,
    sh5, sl5, sh3, sl3, work, weights, hx, hy, ytile, pack, hc,
    hd, dpack, dtile, gx3, gx1, gy3, gy1, gw, hxl, hyl, hcc, gx5, gy5,
    xs, xr, ys, yr, cs, cr, csem, crsem, load,
):
    slab, cross = lax.axis_index("slab"), lax.axis_index("cross")
    ns, nc = lax.axis_size("slab"), lax.axis_size("cross")
    sides = (
        ("slab", slab - 1, slab > 0),
        ("slab", slab + 1, slab < ns - 1),
        ("cross", cross - 1, cross > 0),
        ("cross", cross + 1, cross < nc - 1),
    )
    corners = [
        ({"slab": slab + 2 * k - 1, "cross": cross + 2 * m - 1}, sides[k][2] & sides[2 + m][2])
        for k in range(2) for m in range(2)
    ]

    for k in range(2):

        @pl.when(jnp.logical_not(sides[k][2]))
        def _(k=k):
            hc[k] = jnp.zeros_like(hc[k])
            for slot in range(SLOTS):
                hx[slot, k] = jnp.zeros_like(hx[slot, k])

        @pl.when(jnp.logical_not(sides[2 + k][2]))
        def _(k=k):
            hc[2 + k] = jnp.zeros_like(hc[2 + k])
            for slot in range(SLOTS):
                hy[slot, k] = jnp.zeros_like(hy[slot, k])

    for g in range(4):

        @pl.when(jnp.logical_not(corners[g][1]))
        def _(g=g):
            hcc[g] = jnp.zeros_like(hcc[g])
            for slot in range(SLOTS):
                hd[slot, g] = jnp.zeros_like(hd[slot, g])

    barrier = pltpu.get_barrier_semaphore()
    peers = [({axis: index}, there) for axis, index, there in sides] + corners
    for device, there in peers:

        @pl.when(there)
        def _(device=device):
            pl.semaphore_signal(barrier, inc=1, device_id=device, device_id_type=MESH)

    pairs = ((coef_in, mine.at[0]), (s5_in, s5), (s3_in, s3), (rhs_in, res), (ends_in, ends), (s1_in, s1))
    loads = [pltpu.make_async_copy(src, dst, load.at[n]) for n, (src, dst) in enumerate(pairs)]
    for copy in loads:
        copy.start()
    ytile[...] = jnp.zeros_like(ytile)
    dtile[...] = jnp.zeros_like(dtile)
    for copy in loads:
        copy.wait()

    row = lax.broadcasted_iota(jnp.int32, (NY, NZ), 0)
    lane = lax.broadcasted_iota(jnp.int32, (NY, NZ), 1)
    bottom = jnp.zeros((NY, NZ), F32)
    top = jnp.zeros((NY, NZ), F32)
    for y in range(NY):
        bottom = jnp.where(row == y, ends[0, y].astype(F32), bottom)
        top = jnp.where(row == y, ends[1, y].astype(F32), top)
    mine[1] = jnp.where(lane == 0, bottom, jnp.where(lane == NZ - 1, top, 0.0))

    far = lax.rem(slab, 2)
    near = 1 - far

    def lines(q):
        if q < Q5:
            return [(0, q)]
        return [(0, 1), (q - 1, 1)] + [(j, min(2, q - 1 - j)) for j in range(1, q - 1, 2)]

    def groups(q):
        count = len(lines(q))
        return [[0, 1]] + [[n] for n in range(2, count)] if count > 1 else [[0]]

    def face_at(k, q, first, count):
        return pl.ds(pl.multiple_of(k * ((q**3 - q * q) * NY) + first * q * NY, NY), count * q * NY)

    def slab_copy(k, q, d, slot, piece, arriving):
        first, count = (0, q) if piece is None else lines(q)[piece]
        number = 0 if piece is None else piece
        here = k if arriving else 1 - k
        return pltpu.make_async_remote_copy(
            src_ref=d.at[slot, face_at(k, q, first, count), :],
            dst_ref=hx.at[slot, here, pl.ds(first * q * NY, count * q * NY), :],
            send_sem=xs.at[k, number, slot], recv_sem=xr.at[here, number, slot],
            device_id={"slab": slab + 2 * k - 1}, device_id_type=MESH,
        )

    def cross_copy(k, q, slot, arriving):
        here = k if arriving else k ^ 1
        return pltpu.make_async_remote_copy(
            src_ref=pack.at[slot, k, pl.ds(0, q * NY), :], dst_ref=hy.at[slot, here, pl.ds(0, q * NY), :],
            send_sem=ys.at[k, slot], recv_sem=yr.at[here, slot],
            device_id={"cross": sides[2 + k][1]}, device_id_type=MESH,
        )

    def slab_do(k, method, *args):
        index = slab + 2 * k - 1

        @pl.when((index >= 0) & (index < ns))
        def _():
            getattr(slab_copy(k, *args), method)()

    def cross_do(k, method, *args):
        @pl.when(sides[2 + k][2])
        def _():
            getattr(cross_copy(k, *args), method)()

    def send_near(q, d, slot):
        slab_do(near, "start", q, d, slot, None, False)

    def send_far(q, d, slot, pieces):
        for piece in pieces:
            slab_do(far, "start", q, d, slot, piece, False)

    def send_cross(q, d, slot):
        for i in range(q):
            pack[slot, 0, pl.ds(i * NY, q), :] = d[slot, pl.ds(i * q * q * NY, q, stride=NY), :]
            pack[slot, 1, pl.ds(i * NY, q), :] = d[slot, pl.ds((i * q * q + q * (q - 1)) * NY + NY - 1, q, stride=NY), :]
        for k in range(2):
            cross_do(k, "start", q, slot, False)

    def corner_copy(g, slot, arriving):
        here = g if arriving else 3 - g
        return pltpu.make_async_remote_copy(
            src_ref=dpack.at[slot, g], dst_ref=hd.at[slot, here],
            send_sem=cs.at[g, slot], recv_sem=cr.at[here, slot],
            device_id=corners[g][0], device_id_type=MESH,
        )

    def corner_do(g, method, *args):
        @pl.when(corners[g][1])
        def _():
            getattr(corner_copy(g, *args), method)()

    def send_corners(q, d, slot):
        for g in range(4):
            k, m = g // 2, g % 2
            node = k * (q**3 - q * q) + m * (q * q - q)
            dpack[slot, g, pl.ds(0, q), :] = d[slot, pl.ds(node * NY + m * (NY - 1), q, stride=NY), :]
        for g in range(4):
            corner_do(g, "start", slot, False)

    def send_all(q, d, slot, with_corners):
        if with_corners:
            send_corners(q, d, slot)
        send_cross(q, d, slot)
        send_near(q, d, slot)
        send_far(q, d, slot, range(len(lines(q))))

    def arrived_cross(q, slot):
        for k in range(2):
            cross_do(k, "wait_recv", q, slot, True)

    def arrived_slab(q, d, slot):
        slab_do(near, "wait_recv", q, d, slot, None, True)
        for piece in range(len(lines(q))):
            slab_do(far, "wait_recv", q, d, slot, piece, True)

    def arrived_corners(slot):
        for g in range(4):
            corner_do(g, "wait_recv", slot, True)

    def sent(q, d, slot, with_corners):
        slab_do(near, "wait_send", q, d, slot, None, False)
        for piece in range(len(lines(q))):
            slab_do(far, "wait_send", q, d, slot, piece, False)
        for k in range(2):
            cross_do(k, "wait_send", q, slot, False)
        if with_corners:
            for g in range(4):
                corner_do(g, "wait_send", slot, False)

    def pack_rows(q, source, target):
        for i in range(q):
            target[0, pl.ds(i * NY, q), :] = source[pl.ds(i * q * q * NY, q, stride=NY), :]
            target[1, pl.ds(i * NY, q), :] = source[pl.ds((i * q * q + q * (q - 1)) * NY + NY - 1, q, stride=NY), :]

    for i in range(Q5):
        for m in range(2):
            nodes = [i * Q5 * Q5 + m * Q5 * (Q5 - 1) + n for n in range(Q5)]
            ends_of = [res[pl.ds(node * NY, NY), :][m * (NY - 1) : m * (NY - 1) + 1] for node in nodes]
            pack[0, m, pl.ds(i * NY, Q5), :] = jnp.concatenate(ends_of, 0)
    pl.semaphore_wait(barrier, sum(there.astype(jnp.int32) for _, there in peers))

    def coef_copy(k, arriving):
        if k < 4:
            here = k if arriving else k ^ 1
            src, dst = mine, hc.at[here]
        else:
            here = k if arriving else 11 - k
            src, dst = mine.at[0], hcc.at[here - 4]
        return pltpu.make_async_remote_copy(
            src_ref=src, dst_ref=dst, send_sem=csem.at[k], recv_sem=crsem.at[here],
            device_id=peers[k][0], device_id_type=MESH,
        )

    for k in (2, 3, 0, 1, 4, 5, 6, 7):

        @pl.when(peers[k][1])
        def _(k=k):
            coef_copy(k, False).start()

    raw = Unslotted(res)
    for k in range(2):
        cross_do(k, "start", Q5, 0, False)
    send_near(Q5, raw, 0)
    send_far(Q5, raw, 0, range(len(lines(Q5))))

    def split(table, high, low, count):
        value = table[...]
        high[...] = jnp.zeros_like(high)
        low[...] = jnp.zeros_like(low)
        top = value.astype(BF16)
        high[pl.ds(0, count), pl.ds(0, count)] = top
        low[pl.ds(0, count), pl.ds(0, count)] = (value - top.astype(F32)).astype(BF16)

    split(s5, sh5, sl5, Q5**3)
    split(s3, sh3, sl3, Q3**3)

    def spread_diagonal(table, inv, count):
        value = table[...]
        same = lax.broadcasted_iota(jnp.int32, value.shape, 0) == lax.broadcasted_iota(jnp.int32, value.shape, 1)
        column = jnp.sum(jnp.where(same, value, 0.0), axis=1, keepdims=True)
        wide = jnp.broadcast_to(column, (count, NZ))
        for y in range(NY):
            inv[pl.ds(y, count, stride=NY), :] = wide

    spread_diagonal(s5, inv5, Q5**3)
    spread_diagonal(s3, inv3, Q3**3)
    for n in range(Q1**3):
        inv1[pl.ds(n * NY, NY), :] = jnp.full((NY, NZ), s1[n, n])
    for q, inv, gx, gy in ((Q5, inv5, gx5, gy5), (Q3, inv3, gx3, gy3), (Q1, inv1, gx1, gy1)):
        for k in range(2):
            gx[k] = inv[face_at(1 - k, q, 0, q), :]
            for i in range(q):
                node = i * q * q + (1 - k) * q * (q - 1)
                gy[k, pl.ds(i * NY, q), :] = inv[pl.ds(node * NY, q, stride=NY), :]

    def coefs_done(ks):
        for k in ks:

            @pl.when(peers[k][1])
            def _(k=k):
                coef_copy(k, True).wait_recv()
                coef_copy(k, False).wait_send()

    coefs_done(range(4))
    c = mine[0]

    def cross_weights(own, below, above):
        before = jnp.where(row == 0, pltpu.roll(below, 1, 0), pltpu.roll(own, 1, 0))
        after = jnp.where(row == NY - 1, pltpu.roll(above, NY - 1, 0), pltpu.roll(own, NY - 1, 0))
        return 0.5 * (own + before), 0.5 * (own + after)

    def end_weights(own, flags):
        low = jnp.where(lane == 0, flags * own, 0.5 * (own + pltpu.roll(own, 1, 1)))
        high = jnp.where(lane == NZ - 1, flags * own, 0.5 * (own + pltpu.roll(own, NZ - 1, 1)))
        return low, high

    weights[0] = 0.5 * (c + hc[0, 0])
    weights[1] = 0.5 * (c + hc[1, 0])
    weights[2], weights[3] = cross_weights(c, hc[2, 0], hc[3, 0])
    weights[4], weights[5] = end_weights(c, mine[1])

    def ends_added(base, q, y_pair, z_pair):
        first = base[0:1] + y_pair[0][None]
        last = base[q - 1 : q] + y_pair[1][None]
        base = jnp.concatenate([first, base[1 : q - 1], last] if q > 2 else [first, last], 0)
        first = base[:, 0:1] + z_pair[0][:, None]
        last = base[:, q - 1 : q] + z_pair[1][:, None]
        return jnp.concatenate([first, base[:, 1 : q - 1], last] if q > 2 else [first, last], 1)

    def slab_weight(i, q):
        return jnp.where(i == 0, PENALTY[q] * weights[0], 0.0) + jnp.where(i == q - 1, PENALTY[q] * weights[1], 0.0)

    def plane_at(i, q):
        return pl.ds(pl.multiple_of(i * (q * q * NY), NY), q * q * NY)

    def invert(q, inv):
        yl, yh, zl, zh = (jnp.broadcast_to(PENALTY[q] * weights[k], (q, NY, NZ)) for k in range(2, 6))

        def body(i, carry):
            at = plane_at(i, q)
            base = tiles(inv[at, :], q, q) * c + slab_weight(i, q)
            base = ends_added(base, q, (yl, yh), (zl, zh))
            inv[at, :] = (1.0 / base).reshape(q * q * NY, NZ)
            return carry

        lax.fori_loop(0, q, body, 0)

    invert(Q5, inv5)

    def product_wide(q, d, slot, t, high, low):
        count = q**3
        padded = high.shape[0]
        s_high, s_low = high[...], low[...]
        for y in range(0, NY, 2):
            pair = [d[slot, pl.ds(y + h, count, stride=NY), :] for h in range(2)]
            v = jnp.concatenate(pair, 1)
            if padded > count:
                v = jnp.concatenate([v, jnp.zeros((padded - count, 2 * NZ), F32)], 0)
            v_high = v.astype(BF16)
            v_low = (v - v_high.astype(F32)).astype(BF16)
            out = jnp.dot(s_high, v_high, preferred_element_type=F32)
            out += jnp.dot(s_high, v_low, preferred_element_type=F32)
            out += jnp.dot(s_low, v_high, preferred_element_type=F32)
            for h in range(2):
                t[pl.ds(y + h, count, stride=NY), :] = out[:count, h * NZ : (h + 1) * NZ]

    def product_small(d, slot, t):
        count = Q1**3
        parts = [d[slot, pl.ds(n * NY, NY), :] for n in range(count)]
        for m in range(count):
            total = s1[m, 0] * parts[0]
            for n in range(1, count):
                total += s1[m, n] * parts[n]
            t[pl.ds(m * NY, NY), :] = total

    def local_part(level, slot):
        q, d, t, r = (level[name] for name in ("q", "d", "t", "r"))
        p = PENALTY[q]
        level["product"](slot)

        def local(i, carry):
            yl, yh, zl, zh = (p * weights[k] for k in range(2, 6))
            at = plane_at(i, q)
            dv = tiles(d[slot, at, :], q, q)
            lo, hi = dv[0], dv[q - 1]
            y_pair = (
                yl * (lo - jnp.where(row == 0, 0.0, pltpu.roll(hi, 1, 1))),
                yh * (hi - jnp.where(row == NY - 1, 0.0, pltpu.roll(lo, NY - 1, 1))),
            )
            lo, hi = dv[:, 0], dv[:, q - 1]
            z_pair = (
                zl * (lo - jnp.where(lane == 0, 0.0, pltpu.roll(hi, 1, 2))),
                zh * (hi - jnp.where(lane == NZ - 1, 0.0, pltpu.roll(lo, NZ - 1, 2))),
            )
            total = ends_added(tiles(t[at, :], q, q) * c, q, y_pair, z_pair)
            r[at, :] = r[at, :] - total.reshape(q * q * NY, NZ)
            return carry

        lax.fori_loop(0, q, local, 0)
        face = q * q * NY
        for k in range(2):
            at = pl.ds(0 if k == 0 else (q**3) * NY - face, face)
            r[at, :] = r[at, :] - (p * weights[k] * tiles(d[slot, at, :], q * q)).reshape(face, NZ)

    def rims(level, source, put):
        q = level["q"]
        for i in range(q):
            ytile[0, pl.ds(i * q * NY, q, stride=NY), :] = source[0, pl.ds(i * NY, q), :]
            ytile[1, pl.ds(i * q * NY + NY - 1, q, stride=NY), :] = source[1, pl.ds(i * NY, q), :]

        def rim(i, carry):
            for k in range(2):
                at = pl.ds(pl.multiple_of(i * (q * q * NY) + k * q * (q - 1) * NY, NY), q * NY)
                part = PENALTY[q] * weights[2 + k] * tiles(ytile[k, pl.ds(pl.multiple_of(i * (q * NY), NY), q * NY), :], q)
                put(at, part.reshape(q * NY, NZ))
            return carry

        lax.fori_loop(0, q, rim, 0)

    def slab_term(level, source, k, first, count):
        q = level["q"]
        part = PENALTY[q] * weights[k] * tiles(source[k, pl.ds(first * q * NY, count * q * NY), :], count * q)
        return part.reshape(count * q * NY, NZ)

    def step(level, slot, a, b, update, send, settled=False, meanwhile=None):
        q, d, r, x, inv = (level[name] for name in ("q", "d", "r", "x", "inv"))
        other = lax.rem(slot + 1, SLOTS)

        def put(at, part):
            r[at, :] = r[at, :] + part

        local_part(level, slot)
        for k in range(2):
            cross_do(k, "wait_recv", q, slot, True)
        rims(level, hy.at[slot], put)

        def advance(at):
            value = a * d[slot, at, :] + b * inv[at, :] * r[at, :]
            d[other, at, :] = value
            x[at, :] = x[at, :] + value

        if update and q > 2:

            def inside(i, carry):
                advance(plane_at(i, q))
                return carry

            lax.fori_loop(1, q - 1, inside, 0)

        def slab_face(k, first, count):
            at = face_at(k, q, first, count)
            put(at, slab_term(level, hx.at[slot], k, first, count))
            if update:
                advance(at)

        slab_do(near, "wait_recv", q, d, slot, None, True)
        slab_face(near, 0, q)
        if send:
            send_near(q, d, other)
        if meanwhile is not None:
            meanwhile()
        for number, group in enumerate(groups(q)):
            for piece in group:
                slab_do(far, "wait_recv", q, d, slot, piece, True)
                slab_face(far, *lines(q)[piece])
            if send:
                if number == 0:
                    send_cross(q, d, other)
                send_far(q, d, other, group)
        if not settled:
            sent(q, d, slot, False)

    def correct(level, slot, rows, b, slab_put, cross_put):
        q, d, gx, gy = (level[name] for name in ("q", "d", "gx", "gy"))
        p = PENALTY[q]
        face = q * q * NY
        for k in range(2):
            for m in range(2):
                dtile[m, pl.ds(m * (NY - 1), q, stride=NY), :] = hd[slot, 2 * k + m, pl.ds(0, q), :]
            term = p * weights[k] * tiles(d[slot, pl.ds(k * (q**3 - q * q) * NY, face), :], q, q)
            low, high = (p * gw[k, m] * tiles(dtile[m, pl.ds(0, q * NY), :], q) for m in range(2))
            first, last = term[0:1] + low[None], term[q - 1 : q] + high[None]
            term = jnp.concatenate([first, term[1 : q - 1], last] if q > 2 else [first, last], 0)
            at = pl.ds(0, face)
            slab_put(k, at, b * gx[k, at, :] * term.reshape(face, NZ))
        for m in range(2):
            here, theirs = pl.ds(m * (NY - 1), 1), pl.ds((1 - m) * (NY - 1), 1)
            for i in range(q):
                at = pl.ds(i * NY, q)
                term = p * weights[2 + m, here, :] * rows[m, at, :]
                for k in range(2):
                    if i == k * (q - 1):
                        term = term + p * gw[2 + m, k, theirs, :] * hd[slot, 2 * k + m, pl.ds(0, q), :]
                cross_put(m, at, b * gy[m, at, :] * term)

    def planes(q, body):
        def one_plane(i, carry):
            body(plane_at(i, q))
            return carry

        lax.fori_loop(0, q, one_plane, 0)

    def half_round(level, slot, a, b, total):
        q, d, r, x, inv = (level[name] for name in ("q", "d", "r", "x", "inv"))
        other = lax.rem(slot + 1, SLOTS)

        def partial_next(at):
            value = a * d[slot, at, :] + b * inv[at, :] * r[at, :]
            d[other, at, :] = x[at, :] + value if total else value

        def put_both(at, part):
            r[at, :] = r[at, :] + part
            d[other, at, :] = d[other, at, :] + b * inv[at, :] * part

        local_part(level, slot)
        planes(q, partial_next)
        send_all(q, d, other, False)
        arrived_cross(q, slot)
        sent(q, d, other, False)
        rims(level, hy.at[slot], put_both)
        arrived_slab(q, d, slot)
        for k in range(2):
            put_both(face_at(k, q, 0, q), slab_term(level, hx.at[slot], k, 0, q))

    def keep_slab(k, at, part):
        hxl[k, at, :] = part

    def keep_cross(m, at, part):
        hyl[m, at, :] = part

    def double_step(level, slot, first, second, with_corners, total):
        q, d, r, x, inv = (level[name] for name in ("q", "d", "r", "x", "inv"))
        other, third = lax.rem(slot + 1, SLOTS), lax.rem(slot + 2, SLOTS)

        def put(at, part):
            r[at, :] = r[at, :] + part

        def add(at):
            x[at, :] = x[at, :] + d[other, at, :]

        def advance(at):
            value = second[0] * d[other, at, :] + second[1] * inv[at, :] * r[at, :]
            if total:
                d[third, at, :] = x[at, :] + value
            else:
                d[third, at, :] = value
                x[at, :] = x[at, :] + value

        half_round(level, slot, *first, False)
        planes(q, add)
        local_part(level, other)
        arrived_corners(slot)

        correct(level, slot, pack.at[slot], first[1], keep_slab, keep_cross)
        rims(level, hyl, put)
        for k in range(2):
            put(face_at(k, q, 0, q), slab_term(level, hxl, k, 0, q))
        arrived_cross(q, other)
        rims(level, hy.at[other], put)
        arrived_slab(q, d, other)
        for k in range(2):
            put(face_at(k, q, 0, q), slab_term(level, hx.at[other], k, 0, q))
        planes(q, advance)
        send_all(q, d, third, with_corners)
        sent(q, d, slot, True)

    def finish_round(level, slot, a, b):
        q, d = level["q"], level["d"]
        other = lax.rem(slot + 1, SLOTS)
        half_round(level, slot, a, b, True)
        arrived_corners(slot)
        arrived_cross(q, other)
        arrived_slab(q, d, other)

        def add_slab(k, at, part):
            hx[other, k, at, :] = hx[other, k, at, :] + part

        def add_cross(m, at, part):
            hy[other, m, at, :] = hy[other, m, at, :] + part

        correct(level, slot, pack.at[slot], b, add_slab, add_cross)
        sent(q, d, slot, True)

    def lift_slab(qc, qf, slot):
        table = lagrange(qf, qc)
        for k in range(2):
            lines_in = tiles(hx[slot, k, pl.ds(0, qc * qc * NY), :], qc, qc)
            for j in range(qf):
                line = weighted(table[j], [lines_in[n] for n in range(qc)])
                for n in range(qf):
                    hxl[k, pl.ds((j * qf + n) * NY, NY), :] = weighted(table[n], [line[e] for e in range(qc)])

    def spread_table(qc, qf):
        table = lagrange(qf, qc)
        spread = []
        for e in range(qc):
            column = jnp.zeros((NY, NZ), F32)
            for n in range(qf):
                if table[n, e] != 0.0:
                    column = jnp.where(row == n, float(table[n, e]), column)
            spread.append(column)
        return spread

    def lift_line(spread, line):
        value = spread[0] * line[0:1]
        for e in range(1, len(spread)):
            value = value + spread[e] * line[e : e + 1]
        return value

    def lift_cross(qc, qf, slot):
        table, spread = lagrange(qf, qc), spread_table(qc, qf)
        for k in range(2):
            for i in range(qf):
                line = weighted(table[i], [hy[slot, k, pl.ds(a * NY, qc), :] for a in range(qc)])
                hyl[k, pl.ds(i * NY, NY), :] = lift_line(spread, line)

    def lift_corners(qc, qf, slot):
        spread = spread_table(qc, qf)
        for g in range(4):
            hd[slot, g] = lift_line(spread, hd[slot, g])

    def lifted_step(coarse, slot, level, here, factor):
        q, d, r, x, inv = (level[name] for name in ("q", "d", "r", "x", "inv"))
        following = (here + 1) % SLOTS
        prolong(coarse["d"].at[slot], d, here, x, q, coarse["q"])
        local_part(level, here)
        lift_cross(coarse["q"], q, slot)
        lift_slab(coarse["q"], q, slot)

        def put(at, part):
            r[at, :] = r[at, :] + part

        def advance(at):
            value = factor * inv[at, :] * r[at, :]
            d[following, at, :] = value
            x[at, :] = x[at, :] + value

        rims(level, hyl, put)
        for k in range(2):
            put(face_at(k, q, 0, q), slab_term(level, hxl, k, 0, q))
        planes(q, advance)
        send_all(q, d, following, True)

    def lifted_round(coarse, level, here, factor):
        q, d, r, x, inv = (level[name] for name in ("q", "d", "r", "x", "inv"))
        qc, other, spare = coarse["q"], (here + 1) % SLOTS, (here + 3) % SLOTS

        def partial_next(at):
            d[other, at, :] = factor * inv[at, :] * r[at, :]

        def put(at, part):
            r[at, :] = r[at, :] + part

        def put_both(at, part):
            r[at, :] = r[at, :] + part
            d[other, at, :] = d[other, at, :] + factor * inv[at, :] * part

        def add(at):
            x[at, :] = x[at, :] + d[other, at, :]

        prolong(coarse["d"].at[here], d, here, x, q, qc)
        local_part(level, here)
        planes(q, partial_next)
        send_all(q, d, other, False)
        pack_rows(q, d.at[here], pack.at[spare])
        arrived_cross(qc, here)
        lift_cross(qc, q, here)
        arrived_slab(qc, coarse["d"], here)
        lift_slab(qc, q, here)
        sent(q, d, other, False)
        rims(level, hyl, put_both)
        for k in range(2):
            put_both(face_at(k, q, 0, q), slab_term(level, hxl, k, 0, q))
        planes(q, add)
        arrived_corners(here)
        lift_corners(qc, q, here)
        correct(level, here, pack.at[spare], factor, keep_slab, keep_cross)
        rims(level, hyl, put)
        for k in range(2):
            put(face_at(k, q, 0, q), slab_term(level, hxl, k, 0, q))
        sent(qc, coarse["d"], here, True)

    def first_update(level, slot, factor, with_corners):
        q, d, x, r, inv = (level[name] for name in ("q", "d", "x", "r", "inv"))

        def body(i, carry):
            at = plane_at(i, q)
            value = inv[at, :] * r[at, :] * factor
            d[slot, at, :] = value
            x[at, :] = value
            return carry

        lax.fori_loop(0, q, body, 0)
        send_all(q, d, slot, with_corners)

    def neighbours_inverse(q, gx, gy):
        p = PENALTY[q]
        for k in range(2):
            own = hc[k, 0]
            y_pair, z_pair = (
                [jnp.broadcast_to(p * w, (q, NY, NZ)) for w in pair] for pair in ((gw[k, 0], gw[k, 1]), end_weights(own, hc[k, 1]))
            )
            base = ends_added(tiles(gx[k], q, q) * own + p * weights[k], q, y_pair, z_pair)
            gx[k] = (1.0 / base).reshape(q * q * NY, NZ)
        node = lax.broadcasted_iota(jnp.int32, (q, NZ), 0)
        for m in range(2):
            here, theirs = m * (NY - 1), (1 - m) * (NY - 1)
            low, high = (w[theirs : theirs + 1] for w in end_weights(hc[2 + m, 0], hc[2 + m, 1]))
            own = hc[2 + m, 0, pl.ds(theirs, 1), :]
            across = p * weights[2 + m, pl.ds(here, 1), :]
            along = p * (jnp.where(node == 0, low, 0.0) + jnp.where(node == q - 1, high, 0.0))
            for i in range(q):
                at = pl.ds(i * NY, q)
                base = gy[m, at, :] * own + across + along
                for k in range(2):
                    if i == k * (q - 1):
                        base = base + p * gw[2 + m, k, pl.ds(theirs, 1), :]
                gy[m, at, :] = 1.0 / base

    def zero_missing(gx, gy):
        for k in range(2):

            @pl.when(jnp.logical_not(sides[k][2]))
            def _(k=k):
                gx[k] = jnp.zeros_like(gx[k])

            @pl.when(jnp.logical_not(sides[2 + k][2]))
            def _(k=k):
                gy[k] = jnp.zeros_like(gy[k])

    def opening_step(level, factor, a, b):
        q, d, r, x, inv = (level[name] for name in ("q", "d", "r", "x", "inv"))
        p = PENALTY[q]

        def start(at):
            value = inv[at, :] * r[at, :] * factor
            d[0, at, :] = value
            x[at, :] = value

        def put(at, part):
            r[at, :] = r[at, :] + part

        def advance(at):
            value = a * d[0, at, :] + b * inv[at, :] * r[at, :]
            d[1, at, :] = value
            x[at, :] = x[at, :] + value

        planes(q, start)
        slab_do(near, "wait_send", q, raw, 0, None, False)
        for piece in range(len(lines(q))):
            slab_do(far, "wait_send", q, raw, 0, piece, False)
        local_part(level, 0)
        coefs_done(range(4, 8))
        for k in range(2):
            gw[k, 0], gw[k, 1] = cross_weights(hc[k, 0], hcc[2 * k], hcc[2 * k + 1])
            for m in range(2):
                gw[2 + m, k] = 0.5 * (hc[2 + m, 0] + hcc[2 * k + m])
        neighbours_inverse(q, gx5, gy5)
        for k in range(2):
            cross_do(k, "wait_recv", q, 0, True)
        for m in range(2):
            for i in range(q):
                at = pl.ds(i * NY, q)
                hy[0, m, at, :] = gy5[m, at, :] * hy[0, m, at, :] * factor
        rims(level, hy.at[0], put)

        def inside(i, carry):
            advance(plane_at(i, q))
            return carry

        lax.fori_loop(1, q - 1, inside, 0)

        def slab_face(k, first, count):
            inside_face = pl.ds(first * q * NY, count * q * NY)
            hx[0, k, inside_face, :] = gx5[k, inside_face, :] * hx[0, k, inside_face, :] * factor
            at = face_at(k, q, first, count)
            put(at, slab_term(level, hx.at[0], k, first, count))
            advance(at)

        slab_do(near, "wait_recv", q, raw, 0, None, True)
        slab_face(near, 0, q)
        send_near(q, d, 1)
        for number, group in enumerate(groups(q)):
            for piece in group:
                slab_do(far, "wait_recv", q, raw, 0, piece, True)
                slab_face(far, *lines(q)[piece])
            if number == 0:
                send_cross(q, d, 1)
            send_far(q, d, 1, group)
        for k in range(2):
            cross_do(k, "wait_send", q, 0, False)
        zero_missing(gx5, gy5)

    def pick(k, values):
        out = jnp.float32(values[0])
        for n in range(1, len(values)):
            out = jnp.where(k == n, jnp.float32(values[n]), out)
        return out

    def run(level, exchange, factors, last):
        loop = len(factors) if last else len(factors) - 1

        def body(k, carry):
            a, b = pick(k, [f[0] for f in factors]), pick(k, [f[1] for f in factors])
            step(level, lax.rem(exchange + k, SLOTS), a, b, True, True)
            return carry

        lax.fori_loop(0, loop, body, 0)
        slot = (exchange + loop) % SLOTS
        if last:
            step(level, slot, 0.0, 0.0, False, False)
        else:
            step(level, slot, *factors[-1], True, False)

    def restrict(fine, coarse, qf, qc):
        table = lagrange(qf, qc)

        def body(j, carry):
            rows = [tiles(fine[pl.ds(pl.multiple_of(j * (qf * NY) + i * qf * qf * NY, NY), qf * NY), :], qf) for i in range(qf)]
            for a in range(qc):
                along = weighted(table[:, a], rows)
                for e in range(qc):
                    out = weighted(table[:, e], [along[k] for k in range(qf)])
                    work[pl.ds(pl.multiple_of(j * (qc * qc * NY) + (a * qc + e) * NY, NY), NY), :] = out
            return carry

        lax.fori_loop(0, qf, body, 0)

        def gather(a, carry):
            rows = [work[pl.ds(pl.multiple_of(a * (qc * NY) + j * qc * qc * NY, NY), qc * NY), :] for j in range(qf)]
            for b in range(qc):
                at = pl.ds(pl.multiple_of(a * (qc * qc * NY) + b * qc * NY, NY), qc * NY)
                coarse[at, :] = weighted(table[:, b], rows)
            return carry

        lax.fori_loop(0, qc, gather, 0)

    def restrict_face(slot, k, coarse, qf, qc):
        table = lagrange(qf, qc)
        lines_in = tiles(hx[slot, k, pl.ds(0, qf * qf * NY), :], qf, qf)
        weight = PENALTY[qf] * weights[k]
        for b in range(qc):
            line = weighted(table[:, b], [lines_in[j] for j in range(qf)])
            for e in range(qc):
                value = weight * weighted(table[:, e], [line[n] for n in range(qf)])
                at = pl.ds(pl.multiple_of(k * ((qc**3 - qc * qc) * NY) + (b * qc + e) * NY, NY), NY)
                coarse[at, :] = coarse[at, :] + value

    def prolong(coarse, fine, slot, sum_into, qf, qc):
        table = lagrange(qf, qc)

        def spread(a, carry):
            rows = [coarse[pl.ds(pl.multiple_of(a * (qc * qc * NY) + b * qc * NY, NY), qc * NY), :] for b in range(qc)]
            for j in range(qf):
                at = pl.ds(pl.multiple_of(a * (qc * NY) + j * qc * qc * NY, NY), qc * NY)
                work[at, :] = weighted(table[j], rows)
            return carry

        lax.fori_loop(0, qc, spread, 0)

        def body(j, carry):
            along = []
            for a in range(qc):
                at = pl.ds(pl.multiple_of(j * (qc * qc * NY) + a * qc * NY, NY), qc * NY)
                part = tiles(work[at, :], qc)
                along.append([weighted(table[k], [part[e] for e in range(qc)]) for k in range(qf)])
            for i in range(qf):
                for k in range(qf):
                    value = weighted(table[i], [along[a][k] for a in range(qc)])
                    at = pl.ds(pl.multiple_of(j * (qf * NY) + (i * qf * qf + k) * NY, NY), NY)
                    fine[slot, at, :] = value
                    sum_into[at, :] = sum_into[at, :] + value
            return carry

        lax.fori_loop(0, qf, body, 0)

    five = dict(q=Q5, d=d5, t=t5, r=res, x=sol, inv=inv5, gx=gx5, gy=gy5, product=lambda slot: product_wide(Q5, d5, slot, t5, sh5, sl5))
    three = dict(q=Q3, d=d3, t=t3, r=r3, x=x3, inv=inv3, gx=gx3, gy=gy3, product=lambda slot: product_wide(Q3, d3, slot, t3, sh3, sl3))
    one = dict(q=Q1, d=d1, t=t1, r=r1, x=x1, inv=inv1, gx=gx1, gy=gy1, product=lambda slot: product_small(d1, slot, t1))

    first, pairs = chebyshev_factors(DEGREE, LAMBDA_TOP / 8.0)
    coarse_first, coarse_pairs = chebyshev_factors(COARSE_ITERS, LAMBDA_TOP / 40.0)
    opening_step(five, first, *pairs[0])

    def prepare():
        invert(Q3, inv3)
        invert(Q1, inv1)
        for q, gx, gy in ((Q3, gx3, gy3), (Q1, gx1, gy1)):
            neighbours_inverse(q, gx, gy)
            zero_missing(gx, gy)

    step(five, 1, *pairs[1], True, True, meanwhile=prepare)
    step(five, 2, 0.0, 0.0, False, False, meanwhile=lambda: restrict(res, r3, Q5, Q3))
    restrict_face(2, far, r3, Q5, Q3)
    first_update(three, 3, first, True)
    double_step(three, 3, *pairs, False, False)
    step(three, 5 % SLOTS, 0.0, 0.0, False, False, meanwhile=lambda: restrict(r3, r1, Q3, Q1))
    restrict_face(5 % SLOTS, far, r1, Q3, Q1)
    first_update(one, 6 % SLOTS, coarse_first, True)

    def coarse_rounds(n, carry):
        factors = [[pick(n, [f[part] for f in coarse_pairs[half:6:2]]) for part in range(2)] for half in range(2)]
        double_step(one, lax.rem(6 + 2 * n, SLOTS), *factors, True, False)
        return carry

    lax.fori_loop(0, 3, coarse_rounds, 0)
    finish_round(one, 12 % SLOTS, *coarse_pairs[6])
    lifted_step(one, 13 % SLOTS, three, 13 % SLOTS, first)
    double_step(three, 14 % SLOTS, *pairs, True, True)
    lifted_round(three, five, 16 % SLOTS, first)
    step(five, 17 % SLOTS, *pairs[0], True, True, settled=True)
    run(five, 18, pairs[1:], True)


def hand_out(sol, res, sol_out, res_out, done):
    rows = Q5**3 * NY // 4
    copies = [
        pltpu.make_async_copy(src.at[pl.ds(n * rows, rows), :], dst.at[pl.ds(n * rows, rows), :], done.at[k, n])
        for k, (src, dst) in enumerate(((sol, sol_out), (res, res_out))) for n in range(4)
    ]
    for copy in copies:
        copy.start()
    for copy in copies:
        copy.wait()


def per_device(right_side, coefficient, bottom_top, stiff_five, stiff_three, stiff_one):
    shape = right_side.shape
    n5, n3, n1 = Q5**3 * NY, Q3**3 * NY, Q1**3 * NY
    vmem = pl.BlockSpec(memory_space=pltpu.VMEM)
    hbm = pl.BlockSpec(memory_space=pltpu.HBM)
    field = lambda n: pltpu.VMEM((n, NZ), F32)
    slots = lambda *n: pltpu.VMEM((SLOTS, *n, NZ), F32)
    two = lambda n: pltpu.VMEM((2, n, NZ), F32)
    dma = pltpu.SemaphoreType.DMA
    sol, res = pl.pallas_call(
        kernel,
        out_shape=[jax.ShapeDtypeStruct((n5, NZ), F32)] * 2,
        in_specs=[hbm] * 6,
        out_specs=[vmem, vmem],
        scratch_shapes=[
            two(NY), pltpu.SMEM((2, NY), jnp.int32), pltpu.VMEM((Q5**3, Q5**3), F32), pltpu.VMEM((Q3**3, Q3**3), F32),
            pltpu.SMEM((Q1**3, Q1**3), F32),
            slots(n5 + 16), field(n5), field(n5 + 16),
            field(n3), field(n3), slots(n3 + 32), field(n3), field(n3 + 32),
            field(n1), field(n1), slots(n1 + 48), field(n1), field(n1 + 48),
            pltpu.VMEM((224, 224), BF16), pltpu.VMEM((224, 224), BF16),
            pltpu.VMEM((64, 64), BF16), pltpu.VMEM((64, 64), BF16),
            field(6 * 16 * NY), pltpu.VMEM((6, NY, NZ), F32),
            slots(2, Q5 * Q5 * NY), slots(2, Q5 * NY), two(Q5 * Q5 * NY + 24), slots(2, Q5 * NY), pltpu.VMEM((4, 2, NY, NZ), F32),
            slots(4, NY), slots(4, NY), two(8 * NY),
            two(Q3 * Q3 * NY), two(Q1 * Q1 * NY), two(Q3 * NY), two(Q1 * NY),
            pltpu.VMEM((4, 2, NY, NZ), F32), two(Q5 * Q5 * NY), two(Q5 * NY),
            pltpu.VMEM((4, NY, NZ), F32), two(Q5 * Q5 * NY), two(Q5 * NY),
            dma((2, 4, SLOTS)), dma((2, 4, SLOTS)), dma((2, SLOTS)), dma((2, SLOTS)), dma((4, SLOTS)), dma((4, SLOTS)),
            dma((8,)), dma((8,)), dma((6,)),
        ],
        compiler_params=pltpu.CompilerParams(
            collective_id=0, has_side_effects=True, vmem_limit_bytes=48 * 2**20
        ),
    )(
        *(
            pltpu.with_memory_space_constraint(value, pltpu.HBM)
            for value in (
                coefficient.reshape(NY, NZ), bottom_top.reshape(2, NY), right_side.reshape(n5, NZ),
                stiff_five, stiff_three, stiff_one,
            )
        )
    )
    sol, res = pl.pallas_call(
        hand_out,
        out_shape=[jax.ShapeDtypeStruct((n5, NZ), F32)] * 2,
        in_specs=[vmem] * 2,
        out_specs=[hbm, hbm],
        scratch_shapes=[dma((2, 4))],
    )(*(pltpu.with_memory_space_constraint(value, pltpu.VMEM) for value in (sol, res)))
    return sol.reshape(shape), res.reshape(shape)


def solution(mesh):
    field = P(None, None, None, "slab", "cross", None)
    return jax.shard_map(
        per_device,
        mesh=mesh,
        in_specs=(field, P("slab", "cross", None), P(None, "slab", "cross"), P(), P(), P()),
        out_specs=(field, field),
        check_vma=False,
    )
```
